32 devices in a mesh: page: 4 (over y, x), strip: 8 (over z, core).
Axes of the slice: x: 2, y: 2, z: 4, core: 2. Of those that a mesh axis runs over, the one named last changes fastest.
Arguments:
- vis_tokens: bfloat16 [4, 96, 84, 768], P('page', 'strip'), may hold values from -6 to 6
- query_tokens: bfloat16 [4, 256, 768], P('page', 'strip'), may hold values from -6 to 6
- region_ids: int32 [4, 96, 84], P('page'), may hold values from 0 to 2
- query_mask: int32 [4, 256], P('page'), may hold values 0 or 1
- answer_len: int32 [4], P('page'), may hold values from 32 to 160, as said below
- norm1_gain: float32 [2, 768], replicated, may hold values from 0.5 to 1.5
- norm1_bias: float32 [2, 768], replicated, may hold values from -1.25 to 1.25
- qkv_weight: bfloat16 [2, 768, 2304], replicated, may hold values from -0.21875 to 0.21875
- out_weight: bfloat16 [2, 768, 768], replicated, may hold values from -4 to 4
- out_bias: float32 [2, 768], replicated, may hold values from -1.25 to 1.25
- norm2_gain: float32 [2, 768], replicated, may hold values from 0.5 to 1.5
- norm2_bias: float32 [2, 768], replicated, may hold values from -1.25 to 1.25
- up_weight: bfloat16 [2, 768, 3072], replicated, may hold values from -0.21875 to 0.21875
- up_bias: float32 [2, 3072], replicated, may hold values from -1.25 to 1.25
- down_weight: bfloat16 [2, 3072, 768], replicated, may hold values from -0.109375 to 0.109375
- down_bias: float32 [2, 768], replicated, may hold values from -1.25 to 1.25
- vis_cotangent: bfloat16 [4, 96, 84, 768], P('page', 'strip'), may hold values from -6 to 6
- query_cotangent: bfloat16 [4, 256, 768], P('page', 'strip'), may hold values from -6 to 6
Outputs:
- vis_out: bfloat16 [4, 96, 84, 768], P('page', 'strip')
- query_out: bfloat16 [4, 256, 768], P('page', 'strip')
- vis_grad: bfloat16 [4, 96, 84, 768], P('page', 'strip')
- query_grad: bfloat16 [4, 256, 768], P('page', 'strip')
- grad_norm1_gain: float32 [2, 768], P(None, 'strip')
- grad_norm1_bias: float32 [2, 768], P(None, 'strip')
- grad_qkv_weight: float32 [2, 768, 2304], P(None, 'strip')
- grad_out_weight: float32 [2, 768, 768], P(None, 'strip')
- grad_out_bias: float32 [2, 768], P(None, 'strip')
- grad_norm2_gain: float32 [2, 768], P(None, 'strip')
- grad_norm2_bias: float32 [2, 768], P(None, 'strip')
- grad_up_weight: float32 [2, 768, 3072], P(None, 'strip')
- grad_up_bias: float32 [2, 3072], P(None, 'strip')
- grad_down_weight: float32 [2, 3072, 768], P(None, 'strip')
- grad_down_bias: float32 [2, 768], P(None, 'strip')
The draws below stay inside these ranges and needn't reach their ends.
Inputs may be any that keep to these rules, and one draw needn't show every extreme that they name: Some page's answer_len is exactly 160.
All inputs are finite; a program needn't handle non-finite values. No bound on the sum of `query_mask` on one device may be relied on, other than what follows from the above.
Results may differ from the reference program's by a relative error of at most 0.014.
Values may be sent and summed in bfloat16 or wider, within the bound.
No kernel may reach another device: no remote copies, remote signals or barrier semaphores. Data moves between devices by JAX's collectives and lax.ppermute only.
A program may use at most 448 MiB of HBM per device.

```python
import jax
import jax.numpy as jnp
from jax import lax

D = 768
HEADS = 12
HEAD = 64
FF = 3072
COLS = 84
WIN = 12
SHIFT = 6
Q_DEV = 32
ROWS = 96
QUERIES = 256
PAGES = 4
ANSWER_MAX = 160


def draw_answer_len(key, part):
    key = jax.random.fold_in(key, 7)
    first_key, second_key = jax.random.split(key)
    lengths = jax.random.randint(first_key, (PAGES,), QUERIES // 8, ANSWER_MAX + 1)
    longest = jax.random.randint(second_key, (), 0, PAGES)
    return jnp.where(jnp.arange(PAGES) == longest, ANSWER_MAX, lengths).astype(jnp.int32)


def place_ends(drawn, key, smallest, high):
    index_at = [jax.random.randint(jax.random.fold_in(key, axis), (), 0, length) for axis, length in enumerate(drawn.shape)]
    widest = drawn.shape.index(max(drawn.shape))
    beside = index_at[:widest] + [(index_at[widest] + 1) % drawn.shape[widest]] + index_at[widest + 1:]
    return drawn.at[tuple(index_at)].set(smallest).at[tuple(beside)].set(high)


def block_scale(stream_key, extent, cuts, low, largest):
    loudness = 1.0
    for dim, shards_of in cuts:
        heights = jax.random.uniform(jax.random.fold_in(jax.random.fold_in(stream_key, 6), dim), (shards_of,), jnp.float32, low / len(cuts), largest / len(cuts))
        loudness = loudness * jnp.repeat(jnp.exp(heights), extent[dim] // shards_of).reshape((-1,) + (1,) * (len(extent) - 1 - dim))
    return loudness


def normal_values(rng, shape, scale, bound, cuts=(), kind=jnp.bfloat16):
    drawn = jax.random.normal(rng, shape, jnp.float32) * scale
    if len(cuts) > 0:
        drawn = block_scale(rng, shape, cuts, -0.22, 0.18) * drawn
    return jnp.clip(drawn, min=-bound, max=bound).astype(kind)


def setup_inputs(seed: int = 0) -> dict:
    seeds = jax.random.split(jax.random.key(seed), 19)
    return {
        "vis_tokens": normal_values(seeds[0], (PAGES, ROWS, COLS, D), 1.0, 6.0, ((0, 4), (1, 8))),
        "query_tokens": normal_values(seeds[1], (PAGES, QUERIES, D), 1.0, 6.0, ((0, 4), (1, 8))),
        "region_ids": place_ends(jax.random.randint(seeds[2], (PAGES, ROWS, COLS), 0, 3), jax.random.fold_in(seeds[2], 1), 0, 2).astype(jnp.int32),
        "query_mask": place_ends((jax.random.randint(seeds[3], (PAGES, QUERIES), 0, 4) < 3).astype(jnp.int32), jax.random.fold_in(seeds[3], 1), 0, 1),
        "answer_len": draw_answer_len(jax.random.fold_in(seeds[18], 71), 0),
        "norm1_gain": jnp.clip(1.0 + 0.1 * jax.random.normal(seeds[5], (2, D), jnp.float32), 0.5, 1.5),
        "norm1_bias": normal_values(seeds[6], (2, D), 0.2, 1.25, (), jnp.float32),
        "qkv_weight": normal_values(seeds[7], (2, D, 3 * D), D ** -0.5, 0.21875),
        "out_weight": normal_values(seeds[8], (2, D, D), 2 ** -0.5, 4.0),
        "out_bias": normal_values(seeds[9], (2, D), 0.2, 1.25, (), jnp.float32),
        "norm2_gain": jnp.clip(1.0 + 0.1 * jax.random.normal(seeds[10], (2, D), jnp.float32), 0.5, 1.5),
        "norm2_bias": normal_values(seeds[11], (2, D), 0.2, 1.25, (), jnp.float32),
        "up_weight": normal_values(seeds[12], (2, D, FF), D ** -0.5, 0.21875),
        "up_bias": normal_values(seeds[13], (2, FF), 0.2, 1.25, (), jnp.float32),
        "down_weight": normal_values(seeds[14], (2, FF, D), FF ** -0.5, 0.109375),
        "down_bias": normal_values(seeds[15], (2, D), 0.2, 1.25, (), jnp.float32),
        "vis_cotangent": normal_values(seeds[16], (PAGES, ROWS, COLS, D), 1.0, 6.0, ((0, 4), (1, 8))),
        "query_cotangent": normal_values(seeds[17], (PAGES, QUERIES, D), 1.0, 6.0, ((0, 4), (1, 8))),
    }


@jax.custom_vjp
def low(v):
    return lax.optimization_barrier(v.astype(jnp.bfloat16)).astype(jnp.float32)

@jax.custom_vjp
def low_back(v):
    return v

def low_keep(v):
    return (low(v), None)

def low_pass(kept, grad):
    return (grad,)

def back_keep(v):
    return (v, None)

def back_low(kept, grad):
    return (low(grad),)
low.defvjp(low_keep, low_pass)
low_back.defvjp(back_keep, back_low)
masked_value = -1000000000.0

def layer_norm(values, gain, bias):
    center = values - lax.optimization_barrier(jnp.mean(values, -1, keepdims=True))
    spread = lax.optimization_barrier(jnp.mean(center * center, -1, keepdims=True))
    return center * lax.rsqrt(spread + 1e-05) * gain + bias

def matmul(operand_a, operand_b):
    return jnp.dot(operand_a, operand_b, precision=lax.Precision.HIGHEST)

def contract(form, operand_a, operand_b):
    return jnp.einsum(form, operand_a, operand_b, precision=lax.Precision.HIGHEST)

def page_forward(weights, vis, query, region, open_keys, answer_size):
    gain_one, bias_one, qkv_w, out_w, out_b, gain_two, bias_two, up_w, up_b, down_w, down_b = weights
    score_scale = HEAD ** (-0.5)
    cell_count = ROWS * COLS
    across = COLS // WIN
    vis_flat = vis.reshape(cell_count, D)
    vis_norm = low(layer_norm(vis_flat, gain_one[0], bias_one[0]))
    query_norm = low(layer_norm(query, gain_one[1], bias_one[1]))
    vis_qkv = low(low_back(matmul(vis_norm, qkv_w[0])))
    query_qkv = low(low_back(matmul(query_norm, qkv_w[1])))
    q_all = query_qkv[:, :D].reshape(QUERIES, HEADS, HEAD)
    k_all = query_qkv[:, D:2 * D].reshape(QUERIES, HEADS, HEAD)
    v_all = query_qkv[:, 2 * D:].reshape(QUERIES, HEADS, HEAD)
    key_open = open_keys > 0
    key_ids = jnp.arange(QUERIES, dtype=jnp.int32)
    prompt_open = key_open & (key_ids < QUERIES - answer_size)
    grid = jnp.roll(vis_qkv.reshape(ROWS, COLS, 3 * D), (-SHIFT, -SHIFT), (0, 1))
    grid_region = jnp.roll(region, (-SHIFT, -SHIFT), (0, 1))

    def window_row(inputs):
        row_block, block_region = inputs
        windows = row_block.reshape(WIN, across, WIN, 3, HEADS, HEAD).transpose(1, 0, 2, 3, 4, 5)
        windows = windows.reshape(across, WIN * WIN, 3, HEADS, HEAD)
        q_win = windows[:, :, 0]
        k_win = windows[:, :, 1]
        v_win = windows[:, :, 2]
        labels = block_region.reshape(WIN, across, WIN).transpose(1, 0, 2).reshape(across, WIN * WIN)
        local_scores = low_back(score_scale * contract('wqhd,wkhd->whqk', q_win, k_win))
        same_region = labels[:, None, :, None] == labels[:, None, None, :]
        local_scores = jnp.where(same_region, local_scores, masked_value)
        cross_scores = low_back(score_scale * contract('wqhd,khd->whqk', q_win, k_all))
        cross_scores = jnp.where(prompt_open[None, None, None, :], cross_scores, masked_value)
        row_top = jnp.maximum(lax.optimization_barrier(jnp.max(local_scores, -1)), lax.optimization_barrier(jnp.max(cross_scores, -1)))
        local_exp = jnp.exp(local_scores - row_top[..., None])
        cross_exp = jnp.exp(cross_scores - row_top[..., None])
        row_total = lax.optimization_barrier(jnp.sum(local_exp, -1)) + lax.optimization_barrier(jnp.sum(cross_exp, -1))
        mixture = contract('whqk,wkhd->wqhd', local_exp, v_win) + contract('whqk,khd->wqhd', cross_exp, v_all)
        mixture = mixture / jnp.swapaxes(row_total, 1, 2)[..., None]
        return mixture.reshape(across, WIN, WIN, D).transpose(1, 0, 2, 3).reshape(WIN, COLS, D)
    rows_out = lax.map(jax.checkpoint(window_row), (grid.reshape(ROWS // WIN, WIN, COLS, 3 * D), grid_region.reshape(ROWS // WIN, WIN, COLS)))
    vis_attn = jnp.roll(rows_out.reshape(ROWS, COLS, D), (SHIFT, SHIFT), (0, 1)).reshape(cell_count, D)
    vis_k = vis_qkv[:, D:2 * D].reshape(cell_count, HEADS, HEAD)
    vis_v = vis_qkv[:, 2 * D:].reshape(cell_count, HEADS, HEAD)

    def query_block(inputs):
        q_rows, positions = inputs
        seen_scores = low_back(score_scale * contract('qhd,khd->hqk', q_rows, vis_k))
        own_scores = low_back(score_scale * contract('qhd,khd->hqk', q_rows, k_all))
        allowed = key_open[None, :] & ((key_ids[None, :] < QUERIES - answer_size) | (key_ids[None, :] <= positions[:, None]))
        own_scores = jnp.where(allowed[None], own_scores, masked_value)
        row_top = jnp.maximum(lax.optimization_barrier(jnp.max(seen_scores, -1)), lax.optimization_barrier(jnp.max(own_scores, -1)))
        seen_exp = jnp.exp(seen_scores - row_top[..., None])
        own_exp = jnp.exp(own_scores - row_top[..., None])
        row_total = lax.optimization_barrier(jnp.sum(seen_exp, -1)) + lax.optimization_barrier(jnp.sum(own_exp, -1))
        mixture = contract('hqk,khd->qhd', seen_exp, vis_v) + contract('hqk,khd->qhd', own_exp, v_all)
        mixture = mixture / jnp.swapaxes(row_total, 0, 1)[..., None]
        return mixture.reshape(-1, D)
    query_attn = lax.map(jax.checkpoint(query_block), (q_all.reshape(QUERIES // Q_DEV, Q_DEV, HEADS, HEAD), key_ids.reshape(QUERIES // Q_DEV, Q_DEV))).reshape(QUERIES, D)

    def finish(values, attended, stream):
        after_attn = values + low_back(matmul(low(low_back(attended)), out_w[stream]) + out_b[stream])
        hidden_in = low(layer_norm(after_attn, gain_two[stream], bias_two[stream]))
        pre_gelu = low_back(matmul(hidden_in, up_w[stream]) + up_b[stream])
        hidden = low(jax.nn.gelu(pre_gelu, approximate=False))
        return after_attn + matmul(hidden, down_w[stream]) + down_b[stream]
    vis_result = finish(vis_flat, vis_attn, 0).reshape(ROWS, COLS, D)
    query_result = finish(query, query_attn, 1)
    return (vis_result, query_result)

def reference(vis_tokens, query_tokens, region_ids, query_mask, answer_len, norm1_gain, norm1_bias, qkv_weight, out_weight, out_bias, norm2_gain, norm2_bias, up_weight, up_bias, down_weight, down_bias, vis_cotangent, query_cotangent):
    weights = tuple((weight_item.astype(jnp.float32) for weight_item in (norm1_gain, norm1_bias, qkv_weight, out_weight, out_bias, norm2_gain, norm2_bias, up_weight, up_bias, down_weight, down_bias)))

    def forward(weight_set, vis, query):
        vis_list = []
        query_list = []
        for page_index in range(PAGES):
            vis_page, query_page = page_forward(weight_set, vis[page_index], query[page_index], region_ids[page_index], query_mask[page_index], answer_len[page_index])
            vis_list.append(vis_page)
            query_list.append(query_page)
        return (jnp.stack(vis_list), jnp.stack(query_list))
    (vis_result, query_result), pull = jax.vjp(forward, weights, vis_tokens.astype(jnp.float32), query_tokens.astype(jnp.float32))
    grads, vis_input_grad, query_input_grad = pull((vis_cotangent.astype(jnp.float32), query_cotangent.astype(jnp.float32)))
    return (vis_result.astype(jnp.bfloat16), query_result.astype(jnp.bfloat16), vis_input_grad.astype(jnp.bfloat16), query_input_grad.astype(jnp.bfloat16), grads[0], grads[1], grads[2], grads[3], grads[4], grads[5], grads[6], grads[7], grads[8], grads[9], grads[10])
```

```python
import functools

import jax
import jax.numpy as jnp
from jax import lax
from jax.experimental import pallas as pl
from jax.experimental.pallas import tpu as pltpu
from jax.sharding import PartitionSpec as P

HEADS = 12
WIN = 12
SHIFT = 6
CELLS = WIN * WIN
PAIR = 128
MASKED = -1000000000.0
VMEM_LIMIT = 56 * 1024 * 1024

bf16 = jnp.bfloat16
f32 = jnp.float32


def params():
    return pltpu.CompilerParams(vmem_limit_bytes=VMEM_LIMIT)


def row_block(rows):
    for size in range(336, 15, -16):
        if rows % size == 0:
            return size
    return rows


def dot_nn(a, b):
    return lax.dot_general(a, b, (((1,), (0,)), ((), ())), preferred_element_type=f32)


def dot_nt(a, b):
    return lax.dot_general(a, b, (((1,), (1,)), ((), ())), preferred_element_type=f32)


def dot_tn(a, b):
    return lax.dot_general(a, b, (((0,), (0,)), ((), ())), preferred_element_type=f32)


def cost(flops, moved, special=0):
    return pl.CostEstimate(flops=int(flops), bytes_accessed=int(moved), transcendentals=int(special))


def whole(shape):
    return pl.BlockSpec(shape, lambda *_: (0,) * len(shape))


def normalised(values):
    center = values - jnp.mean(values, -1, keepdims=True)
    spread = jnp.mean(center * center, -1, keepdims=True)
    rstd = lax.rsqrt(spread + 1e-05)
    return center * rstd, rstd


def norm_back(grad, hat, rstd, gain):
    scaled = grad * gain
    mean_one = jnp.mean(scaled, -1, keepdims=True)
    mean_two = jnp.mean(scaled * hat, -1, keepdims=True)
    return rstd * (scaled - mean_one - hat * mean_two)


def qkv_kernel(stream, x_ref, gain_ref, bias_ref, w_ref, a_ref, out_ref):
    rows, width = x_ref.shape
    block = row_block(rows)

    @pl.when(pl.program_id(0) == 0)
    def _():
        @pl.loop(0, rows // block)
        def _(i):
            at = pl.ds(pl.multiple_of(i * block, block), block)
            hat, _ = normalised(x_ref[at, :].astype(f32))
            a_ref[at, :] = (
                hat * gain_ref[stream : stream + 1, :] + bias_ref[stream : stream + 1, :]
            ).astype(bf16)

    @pl.loop(0, rows // block)
    def _(i):
        at = pl.ds(pl.multiple_of(i * block, block), block)
        out_ref[at, :] = dot_nn(a_ref[at, :], w_ref[...]).astype(bf16)


def norm_qkv(x, gain, bias, weight, stream):
    rows, width = x.shape
    full = weight.shape[-1]
    return pl.pallas_call(
        functools.partial(qkv_kernel, stream),
        grid=(full // width,),
        in_specs=[
            whole((rows, width)),
            whole(gain.shape),
            whole(bias.shape),
            pl.BlockSpec((None, width, width), lambda j: (stream, 0, j)),
        ],
        out_specs=[whole((rows, width)), pl.BlockSpec((rows, width), lambda j: (0, j))],
        out_shape=[
            jax.ShapeDtypeStruct((rows, width), bf16),
            jax.ShapeDtypeStruct((rows, full), bf16),
        ],
        compiler_params=params(),
        cost_estimate=cost(2 * rows * width * full, 2 * rows * (2 * width + full) + 2 * width * full),
        name="norm_qkv",
    )(x, gain, bias, weight)


def first_half(shape):
    return lax.broadcasted_iota(jnp.int32, shape, len(shape) - 1) < PAIR // 2


def stacked(block):
    left = first_half(block.shape)
    zero = jnp.zeros_like(block)
    return jnp.concatenate([jnp.where(left, block, zero), jnp.where(left, zero, block)], 0)


def unstacked(turned, rows):
    upright = turned.T
    return jnp.where(first_half((rows, PAIR)), upright[:rows], upright[rows:])


def query_forward_kernel(
    windows, qq_ref, k_ref, v_ref, ko_ref, vo_ref, bias_ref, out_ref, lse_ref, s_ref
):
    queries = qq_ref.shape[0]
    own = ko_ref.shape[0]
    scaled = stacked(qq_ref[...] * 0.125)
    cells = windows * CELLS
    bias = bias_ref[...]
    score = dot_nt(ko_ref[...], scaled) + jnp.concatenate([bias, bias], 1)
    s_ref[cells : cells + own, :] = score
    top = jnp.max(score, 0, keepdims=True)
    for w in range(windows):
        score = dot_nt(k_ref[w * CELLS : (w + 1) * CELLS, :], scaled)
        s_ref[w * CELLS : (w + 1) * CELLS, :] = score
        top = jnp.maximum(top, jnp.max(score, 0, keepdims=True))
    prob = jnp.exp(s_ref[cells : cells + own, :] - top)
    total = jnp.sum(prob, 0, keepdims=True)
    mixed = dot_nn(vo_ref[...].T, prob.astype(bf16))
    for w in range(windows):
        prob = jnp.exp(s_ref[w * CELLS : (w + 1) * CELLS, :] - top)
        total = total + jnp.sum(prob, 0, keepdims=True)
        mixed = mixed + dot_nn(v_ref[w * CELLS : (w + 1) * CELLS, :].T, prob.astype(bf16))
    out_ref[...] = unstacked(mixed * (1.0 / total), queries).astype(bf16)
    lse_ref[...] = top + jnp.log(total)


def query_forward(query_qkv, own_qkv, vis_qkv, self_bias):
    cells = vis_qkv.shape[0]
    queries = query_qkv.shape[0]
    own = own_qkv.shape[0]
    width = query_qkv.shape[1] // 3
    pairs = width // PAIR
    keys = cells + own

    def part(rows, j):
        return pl.BlockSpec((rows, PAIR), lambda p, j=j: (0, j * pairs + p))

    return pl.pallas_call(
        functools.partial(query_forward_kernel, cells // CELLS),
        grid=(pairs,),
        in_specs=[
            part(queries, 0),
            part(cells, 1),
            part(cells, 2),
            part(own, 1),
            part(own, 2),
            whole(self_bias.shape),
        ],
        out_specs=[part(queries, 0), pl.BlockSpec((None, 1, 2 * queries), lambda p: (p, 0, 0))],
        out_shape=[
            jax.ShapeDtypeStruct((queries, width), bf16),
            jax.ShapeDtypeStruct((pairs, 1, 2 * queries), f32),
        ],
        scratch_shapes=[pltpu.VMEM((keys, 2 * queries), f32)],
        compiler_params=params(),
        cost_estimate=cost(
            4 * 2 * queries * keys * width, 4 * cells * width, 2 * queries * keys * pairs
        ),
        name="query_forward",
    )(query_qkv, vis_qkv, vis_qkv, own_qkv, own_qkv, self_bias)


def window_forward_kernel(
    windows, q_ref, k_ref, v_ref, kq_ref, vq_ref, row_ref, col_ref, open_ref, out_ref, lse_ref
):
    kq = kq_ref[...]
    vq_turned = vq_ref[...].T
    closed = open_ref[...]
    for w in range(windows):
        at = slice(w * CELLS, (w + 1) * CELLS)
        scaled = stacked(q_ref[at, :] * 0.125)
        near = dot_nt(k_ref[at, :], scaled)
        near = jnp.where(col_ref[w] == row_ref[w], near, MASKED)
        far = dot_nt(kq, scaled) + closed
        top = jnp.maximum(jnp.max(near, 0, keepdims=True), jnp.max(far, 0, keepdims=True))
        near = jnp.exp(near - top)
        far = jnp.exp(far - top)
        total = jnp.sum(near, 0, keepdims=True) + jnp.sum(far, 0, keepdims=True)
        mixed = dot_nn(v_ref[at, :].T, near.astype(bf16)) + dot_nn(vq_turned, far.astype(bf16))
        out_ref[at, :] = unstacked(mixed * (1.0 / total), CELLS).astype(bf16)
        lse_ref[w : w + 1, :] = top + jnp.log(total)


def window_forward(vis_qkv, query_qkv, region_row, region_col, closed):
    cells = vis_qkv.shape[0]
    queries = query_qkv.shape[0]
    width = vis_qkv.shape[1] // 3
    pairs = width // PAIR
    windows = cells // CELLS

    def part(rows, j):
        return pl.BlockSpec((rows, PAIR), lambda p, j=j: (0, j * pairs + p))

    return pl.pallas_call(
        functools.partial(window_forward_kernel, windows),
        grid=(pairs,),
        in_specs=[
            part(cells, 0),
            part(cells, 1),
            part(cells, 2),
            part(queries, 1),
            part(queries, 2),
            whole(region_row.shape),
            whole(region_col.shape),
            whole(closed.shape),
        ],
        out_specs=[
            part(cells, 0),
            pl.BlockSpec((None, windows, 2 * CELLS), lambda p: (p, 0, 0)),
        ],
        out_shape=[
            jax.ShapeDtypeStruct((cells, width), bf16),
            jax.ShapeDtypeStruct((pairs, windows, 2 * CELLS), f32),
        ],
        compiler_params=params(),
        cost_estimate=cost(
            8 * cells * (CELLS + queries) * width,
            8 * cells * width,
            2 * pairs * cells * (CELLS + queries),
        ),
        name="window_forward",
    )(vis_qkv, vis_qkv, vis_qkv, query_qkv, query_qkv, region_row, region_col, closed)


def attention_backward_kernel(
    windows,
    q_ref,
    k_ref,
    v_ref,
    do_ref,
    qq_ref,
    kq_ref,
    vq_ref,
    doq_ref,
    ko_ref,
    vo_ref,
    row_ref,
    col_ref,
    open_ref,
    bias_ref,
    lse_ref,
    lseq_ref,
    deltaq_ref,
    dq_ref,
    dk_ref,
    dv_ref,
    dqq_ref,
    dkq_ref,
    dvq_ref,
    dko_ref,
    dvo_ref,
    sumq_ref,
):
    queries = qq_ref.shape[0]
    kq = kq_ref[...]
    vq = vq_ref[...]
    kq_turned = kq.T
    closed = open_ref[...]
    scaled_q = stacked(qq_ref[...] * 0.125)
    grad_q = stacked(doq_ref[...])
    lse_q = lseq_ref[...]
    delta_q = deltaq_ref[...]

    bias = bias_ref[...]
    prob = jnp.exp(dot_nt(ko_ref[...], scaled_q) + jnp.concatenate([bias, bias], 1) - lse_q)
    dscore = (prob * (dot_nt(vo_ref[...], grad_q) - delta_q)).astype(bf16)
    dko_ref[...] = dot_nn(dscore, scaled_q)
    dvo_ref[...] = dot_nn(prob.astype(bf16), grad_q)
    sumq_ref[...] = dot_nn(ko_ref[...].T, dscore)

    for w in range(windows):
        at = slice(w * CELLS, (w + 1) * CELLS)
        k_win = k_ref[at, :]
        v_win = v_ref[at, :]
        k_turned = k_win.T
        scaled = stacked(q_ref[at, :] * 0.125)
        grad = stacked(do_ref[at, :])
        lse = lse_ref[w : w + 1, :]
        near = dot_nt(k_win, scaled)
        near = jnp.exp(jnp.where(col_ref[w] == row_ref[w], near, MASKED) - lse)
        far = jnp.exp(dot_nt(kq, scaled) + closed - lse)
        near_t = near * dot_nt(v_win, grad)
        far_t = far * dot_nt(vq, grad)
        delta = jnp.sum(near_t, 0, keepdims=True) + jnp.sum(far_t, 0, keepdims=True)
        near_d = (near_t - near * delta).astype(bf16)
        far_d = (far_t - far * delta).astype(bf16)
        turned = dot_nn(k_turned, near_d) + dot_nn(kq_turned, far_d)
        dq_ref[at, :] = (unstacked(turned, CELLS) * 0.125).astype(bf16)
        dkq = dot_nn(far_d, scaled)
        dvq = dot_nn(far.astype(bf16), grad)
        if w == 0:
            dkq_ref[...] = dkq
            dvq_ref[...] = dvq
        else:
            dkq_ref[...] += dkq
            dvq_ref[...] += dvq

        seen = jnp.exp(dot_nt(k_win, scaled_q) - lse_q)
        seen_d = (seen * (dot_nt(v_win, grad_q) - delta_q)).astype(bf16)
        sumq_ref[...] += dot_nn(k_turned, seen_d)
        dk_ref[at, :] = (dot_nn(near_d, scaled) + dot_nn(seen_d, scaled_q)).astype(bf16)
        dv_ref[at, :] = (
            dot_nn(near.astype(bf16), grad) + dot_nn(seen.astype(bf16), grad_q)
        ).astype(bf16)
    dqq_ref[...] = unstacked(sumq_ref[...], queries) * 0.125


def attention_backward(
    vis_qkv,
    query_qkv,
    own_qkv,
    grad,
    grad_q,
    region_row,
    region_col,
    closed,
    self_bias,
    lse,
    lse_q,
    delta_q,
    first,
    count,
):
    cells = vis_qkv.shape[0]
    queries = query_qkv.shape[0]
    own = own_qkv.shape[0]
    width = vis_qkv.shape[1] // 3
    pairs = width // PAIR
    windows = cells // CELLS

    def part(rows, j):
        return pl.BlockSpec((rows, PAIR), lambda p, j=j: (0, j * pairs + first + p))

    def result(rows):
        return pl.BlockSpec((rows, PAIR), lambda p: (0, p))

    def stats(array):
        return pl.BlockSpec((None,) + array.shape[1:], lambda p: (first + p, 0, 0))

    span = count * PAIR
    return pl.pallas_call(
        functools.partial(attention_backward_kernel, windows),
        grid=(count,),
        in_specs=[
            part(cells, 0),
            part(cells, 1),
            part(cells, 2),
            part(cells, 0),
            part(queries, 0),
            part(queries, 1),
            part(queries, 2),
            part(queries, 0),
            part(own, 1),
            part(own, 2),
            whole(region_row.shape),
            whole(region_col.shape),
            whole(closed.shape),
            whole(self_bias.shape),
            stats(lse),
            stats(lse_q),
            stats(delta_q),
        ],
        out_specs=[result(cells)] * 3 + [result(queries)] * 3 + [result(own)] * 2,
        out_shape=[jax.ShapeDtypeStruct((cells, span), bf16)] * 3
        + [jax.ShapeDtypeStruct((queries, span), f32)] * 3
        + [jax.ShapeDtypeStruct((own, span), f32)] * 2,
        scratch_shapes=[pltpu.VMEM((PAIR, 2 * queries), f32)],
        compiler_params=params(),
        cost_estimate=cost(
            20 * cells * (CELLS + 2 * queries) * span,
            14 * cells * span,
            2 * count * cells * (CELLS + 2 * queries),
        ),
        name="attention_backward",
    )(
        vis_qkv,
        vis_qkv,
        vis_qkv,
        grad,
        query_qkv,
        query_qkv,
        query_qkv,
        grad_q,
        own_qkv,
        own_qkv,
        region_row,
        region_col,
        closed,
        self_bias,
        lse,
        lse_q,
        delta_q,
    )


def gelu_pair(z):
    size = jnp.abs(z)
    t = 1.0 / (1.0 + (0.3275911 * 0.7071067811865476) * size)
    bell = jnp.exp(-0.5 * z * z)
    poly = 0.5 * 1.061405429
    for term in (-1.453152027, 1.421413741, -0.284496736, 0.254829592):
        poly = poly * t + 0.5 * term
    tail = poly * t * bell
    below = jnp.where(z >= 0, 1.0 - tail, tail)
    return z * below, below + z * bell * 0.3989422804014327


def ffn_forward_kernel(
    stream,
    x_ref,
    o_ref,
    wo_ref,
    bo_ref,
    gain_ref,
    bias_ref,
    wu_ref,
    bu_ref,
    wd_ref,
    bd_ref,
    x1_ref,
    b_ref,
    hid_ref,
    slope_ref,
    out_ref,
    sum_ref,
):
    rows, width = x_ref.shape
    block = row_block(rows)
    step = pl.program_id(0)
    row = slice(stream, stream + 1)

    @pl.when(step == 0)
    def _():
        @pl.loop(0, rows // block)
        def _(i):
            at = pl.ds(pl.multiple_of(i * block, block), block)
            x1 = x_ref[at, :].astype(f32) + dot_nn(o_ref[at, :], wo_ref[...]) + bo_ref[row, :]
            x1_ref[at, :] = x1
            hat, _ = normalised(x1)
            b_ref[at, :] = (hat * gain_ref[row, :] + bias_ref[row, :]).astype(bf16)
            sum_ref[at, :] = x1 + bd_ref[row, :]

    @pl.loop(0, rows // block)
    def _(i):
        at = pl.ds(pl.multiple_of(i * block, block), block)
        z = dot_nn(b_ref[at, :], wu_ref[...]) + bu_ref[row, :]
        hidden, slope = gelu_pair(z)
        hidden = hidden.astype(bf16)
        hid_ref[at, :] = hidden
        slope_ref[at, :] = slope.astype(bf16)
        sum_ref[at, :] += dot_nn(hidden, wd_ref[...])

    @pl.when(step == pl.num_programs(0) - 1)
    def _():
        out_ref[...] = sum_ref[...].astype(bf16)


def ffn_forward(x, attended, out_w, out_b, gain, bias, up_w, up_b, down_w, down_b, stream):
    rows, width = x.shape
    hidden = up_w.shape[-1]
    chunk = 512
    return pl.pallas_call(
        functools.partial(ffn_forward_kernel, stream),
        grid=(hidden // chunk,),
        in_specs=[
            whole((rows, width)),
            whole((rows, width)),
            pl.BlockSpec((None, width, width), lambda f: (stream, 0, 0)),
            whole(out_b.shape),
            whole(gain.shape),
            whole(bias.shape),
            pl.BlockSpec((None, width, chunk), lambda f: (stream, 0, f)),
            pl.BlockSpec((2, chunk), lambda f: (0, f)),
            pl.BlockSpec((None, chunk, width), lambda f: (stream, f, 0)),
            whole(down_b.shape),
        ],
        out_specs=[
            whole((rows, width)),
            whole((rows, width)),
            pl.BlockSpec((rows, chunk), lambda f: (0, f)),
            pl.BlockSpec((rows, chunk), lambda f: (0, f)),
            whole((rows, width)),
        ],
        out_shape=[
            jax.ShapeDtypeStruct((rows, width), f32),
            jax.ShapeDtypeStruct((rows, width), bf16),
            jax.ShapeDtypeStruct((rows, hidden), bf16),
            jax.ShapeDtypeStruct((rows, hidden), bf16),
            jax.ShapeDtypeStruct((rows, width), bf16),
        ],
        scratch_shapes=[pltpu.VMEM((rows, width), f32)],
        compiler_params=params(),
        cost_estimate=cost(
            2 * rows * width * (2 * hidden + width),
            4 * width * hidden + 4 * rows * hidden + 12 * rows * width,
            2 * rows * hidden,
        ),
        name="ffn_forward",
    )(x, attended, out_w, out_b, gain, bias, up_w, up_b, down_w, down_b)


def ffn_backward_kernel(
    stream,
    g_ref,
    slope_ref,
    x1_ref,
    wd_ref,
    wu_ref,
    wo_ref,
    gain_ref,
    dz_ref,
    upb_ref,
    dx1_ref,
    du_ref,
    do_ref,
    sums_ref,
    sum_ref,
):
    rows, width = g_ref.shape
    block = row_block(rows)
    step = pl.program_id(0)
    row = slice(stream, stream + 1)

    @pl.when(step == 0)
    def _():
        sum_ref[...] = jnp.zeros_like(sum_ref)

    upb_ref[...] = jnp.zeros_like(upb_ref)

    @pl.loop(0, rows // block)
    def _(i):
        at = pl.ds(pl.multiple_of(i * block, block), block)
        dz = dot_nt(g_ref[at, :], wd_ref[...]) * slope_ref[at, :].astype(f32)
        low = dz.astype(bf16)
        dz_ref[at, :] = low
        upb_ref[...] += jnp.sum(dz, 0, keepdims=True)
        sum_ref[at, :] += dot_nt(low, wu_ref[...])

    @pl.when(step == pl.num_programs(0) - 1)
    def _():
        sums_ref[...] = jnp.zeros_like(sums_ref)

        @pl.loop(0, rows // block)
        def _(i):
            at = pl.ds(pl.multiple_of(i * block, block), block)
            hat, rstd = normalised(x1_ref[at, :])
            db = sum_ref[at, :]
            g = g_ref[at, :].astype(f32)
            dx1 = g + norm_back(db, hat, rstd, gain_ref[row, :])
            dx1_ref[at, :] = dx1
            du = dx1.astype(bf16)
            du_ref[at, :] = du
            do_ref[at, :] = dot_nt(du, wo_ref[...]).astype(bf16)
            sums_ref[0:1, :] += jnp.sum(db * hat, 0, keepdims=True)
            sums_ref[1:2, :] += jnp.sum(db, 0, keepdims=True)
            sums_ref[2:3, :] += jnp.sum(dx1, 0, keepdims=True)
            sums_ref[3:4, :] += jnp.sum(g, 0, keepdims=True)


def ffn_backward(g, slope, x1, down_w, up_w, out_w, gain, stream):
    rows, width = g.shape
    hidden = up_w.shape[-1]
    chunk = 512
    return pl.pallas_call(
        functools.partial(ffn_backward_kernel, stream),
        grid=(hidden // chunk,),
        in_specs=[
            whole((rows, width)),
            pl.BlockSpec((rows, chunk), lambda f: (0, f)),
            whole((rows, width)),
            pl.BlockSpec((None, chunk, width), lambda f: (stream, f, 0)),
            pl.BlockSpec((None, width, chunk), lambda f: (stream, 0, f)),
            pl.BlockSpec((None, width, width), lambda f: (stream, 0, 0)),
            whole(gain.shape),
        ],
        out_specs=[
            pl.BlockSpec((rows, chunk), lambda f: (0, f)),
            pl.BlockSpec((1, chunk), lambda f: (0, f)),
            whole((rows, width)),
            whole((rows, width)),
            whole((rows, width)),
            whole((8, width)),
        ],
        out_shape=[
            jax.ShapeDtypeStruct((rows, hidden), bf16),
            jax.ShapeDtypeStruct((1, hidden), f32),
            jax.ShapeDtypeStruct((rows, width), f32),
            jax.ShapeDtypeStruct((rows, width), bf16),
            jax.ShapeDtypeStruct((rows, width), bf16),
            jax.ShapeDtypeStruct((8, width), f32),
        ],
        scratch_shapes=[pltpu.VMEM((rows, width), f32)],
        compiler_params=params(),
        cost_estimate=cost(
            2 * rows * width * (2 * hidden + width),
            4 * width * hidden + 4 * rows * hidden + 14 * rows * width,
        ),
        name="ffn_backward",
    )(g, slope, x1, down_w, up_w, out_w, gain)


def input_kernel(stream, dq_ref, dk_ref, dv_ref, w_ref, x_ref, dx1_ref, gain_ref, out_ref, sums_ref):
    rows, width = x_ref.shape
    block = row_block(rows)
    row = slice(stream, stream + 1)
    sums_ref[...] = jnp.zeros_like(sums_ref)

    @pl.loop(0, rows // block)
    def _(i):
        at = pl.ds(pl.multiple_of(i * block, block), block)
        grad = dot_nt(dq_ref[at, :], w_ref[:, :width])
        grad = grad + dot_nt(dk_ref[at, :], w_ref[:, width : 2 * width])
        grad = grad + dot_nt(dv_ref[at, :], w_ref[:, 2 * width :])
        hat, rstd = normalised(x_ref[at, :].astype(f32))
        out_ref[at, :] = (
            dx1_ref[at, :] + norm_back(grad, hat, rstd, gain_ref[row, :])
        ).astype(bf16)
        sums_ref[0:1, :] += jnp.sum(grad * hat, 0, keepdims=True)
        sums_ref[1:2, :] += jnp.sum(grad, 0, keepdims=True)


def input_grad(dq, dk, dv, weight, x, dx1, gain, stream):
    rows, width = x.shape
    return pl.pallas_call(
        functools.partial(input_kernel, stream),
        grid=(1,),
        in_specs=[whole((rows, width))] * 3
        + [
            pl.BlockSpec((None, width, 3 * width), lambda j: (stream, 0, 0)),
            whole((rows, width)),
            whole((rows, width)),
            whole(gain.shape),
        ],
        out_specs=[whole((rows, width)), whole((8, width))],
        out_shape=[
            jax.ShapeDtypeStruct((rows, width), bf16),
            jax.ShapeDtypeStruct((8, width), f32),
        ],
        compiler_params=params(),
        cost_estimate=cost(6 * rows * width * width, 14 * rows * width + 6 * width * width),
        name="input_grad",
    )(dq, dk, dv, weight, x, dx1, gain)


def moved(block, axis, step):
    size = lax.axis_size(axis)
    return lax.ppermute(block, axis, [(i, (i + step) % size) for i in range(size)])


def other_core(block):
    size = lax.axis_size("strip")
    return lax.ppermute(block, "strip", [(i, i ^ 1) for i in range(size)])


def pick(block, index, axis=0):
    return lax.dynamic_index_in_dim(block, index, axis, keepdims=False)


def added(*blocks):
    total = blocks[0].astype(f32)
    for block in blocks[1:]:
        total = total + block.astype(f32)
    return total.astype(bf16)


def sum_cores(grad):
    core = lax.axis_index("strip") % 2
    return added(pick(grad, core, 1), other_core(pick(grad, 1 - core, 1)))


def sum_line(grad):
    size = lax.axis_size("strip") // 2
    z = lax.axis_index("strip") // 2
    blocks = [pick(grad, z)]
    for step in range(1, size):
        blocks.append(moved(pick(grad, (z + step) % size), "strip", 2 * step))
    return added(*blocks)


def sum_pages(grad):
    size = lax.axis_size("page")
    page = lax.axis_index("page")
    axis = grad.ndim - 3
    blocks = [pick(grad, page, axis)]
    for step in range(1, size):
        blocks.append(moved(pick(grad, (page + step) % size, axis), "page", step))
    return added(*blocks)


def gather_pages(block):
    size = lax.axis_size("page")
    page = lax.axis_index("page")
    blocks = [block] + [moved(block, "page", size - step) for step in range(1, size)]
    double = jnp.stack(blocks + blocks)
    return lax.dynamic_slice_in_dim(double, (size - page) % size, size, 0)


def by_strip(grad):
    strips = lax.axis_size("strip")
    return grad.reshape(strips // 2, 2, grad.shape[0] // strips, grad.shape[1])


def by_page(grad):
    pages = lax.axis_size("page")
    return grad.reshape(grad.shape[:-2] + (pages, grad.shape[-2] // pages, grad.shape[-1]))


def finished(parts):
    every = gather_pages(parts)
    every = jnp.swapaxes(every, 0, 1).astype(f32)
    return every.reshape(2, -1, every.shape[-1])


def reduce_line_first(vis_grad, query_grad):
    rows = sum_line(sum_cores(by_strip(vis_grad)))
    return finished(sum_pages(by_page(jnp.stack([rows, query_grad]))))


def reduce_pages_first(vis_grad, query_grad):
    strips = sum_cores(by_strip(vis_grad))
    both = jnp.concatenate([strips, query_grad[None]], 0)
    part = sum_pages(by_page(both))
    rows = sum_line(part[:-1])
    return finished(jnp.stack([rows, part[-1]]))


def to_windows(rows):
    across = rows.shape[1] // WIN
    rolled = jnp.roll(rows, -SHIFT, axis=1)
    return (
        rolled.reshape(WIN, across, WIN, rows.shape[-1])
        .transpose(1, 0, 2, 3)
        .reshape(-1, rows.shape[-1])
    )


def from_windows(cells, columns):
    across = columns // WIN
    rows = (
        cells.reshape(across, WIN, WIN, cells.shape[-1])
        .transpose(1, 0, 2, 3)
        .reshape(WIN, columns, cells.shape[-1])
    )
    return jnp.roll(rows, SHIFT, axis=1)


def weight_grad(left, right):
    return dot_tn(left, right).astype(bf16)


def body(
    vis_tokens,
    query_tokens,
    region_ids,
    query_mask,
    answer_len,
    norm1_gain,
    norm1_bias,
    qkv_weight,
    out_weight,
    out_bias,
    norm2_gain,
    norm2_bias,
    up_weight,
    up_bias,
    down_weight,
    down_bias,
    vis_cotangent,
    query_cotangent,
):
    strips = lax.axis_size("strip")
    strip = lax.axis_index("strip")
    local_rows, columns, features = vis_tokens.shape[1:]
    own_count = query_tokens.shape[1]
    query_count = query_mask.shape[1]
    total_rows = region_ids.shape[1]
    windows = columns // WIN
    own_start = strip * own_count

    head_rows = moved(vis_tokens[0, :SHIFT], "strip", -1)
    head_cot = moved(vis_cotangent[0, :SHIFT], "strip", -1)
    query = lax.all_gather(query_tokens[0], "strip", axis=0, tiled=True)
    query_cot = lax.all_gather(query_cotangent[0], "strip", axis=0, tiled=True)
    vis = to_windows(jnp.concatenate([vis_tokens[0, SHIFT:], head_rows], 0))
    vis_cot = to_windows(jnp.concatenate([vis_cotangent[0, SHIFT:], head_cot], 0))

    key_open = query_mask[0] > 0
    key_ids = jnp.arange(query_count, dtype=jnp.int32)
    prompt = key_ids < query_count - answer_len[0]
    closed = jnp.where(key_open & prompt, 0.0, MASKED).astype(f32)[:, None]
    own_ids = own_start + jnp.arange(own_count, dtype=jnp.int32)
    own_open = lax.dynamic_slice_in_dim(key_open, own_start, own_count)
    own_prompt = lax.dynamic_slice_in_dim(prompt, own_start, own_count)
    allowed = own_open[:, None] & (own_prompt[:, None] | (own_ids[:, None] <= key_ids[None, :]))
    self_bias = jnp.where(allowed, 0.0, MASKED).astype(f32)
    row_ids = (strip * local_rows + SHIFT + jnp.arange(local_rows, dtype=jnp.int32)) % total_rows
    region = to_windows(jnp.take(region_ids[0], row_ids, axis=0)[..., None]).reshape(windows, CELLS)
    region_row = jnp.concatenate([region, region], 1)[:, None, :]
    region_col = region[:, :, None]

    query_norm, query_qkv = norm_qkv(query, norm1_gain, norm1_bias, qkv_weight, 1)
    own_qkv = lax.dynamic_slice_in_dim(query_qkv, own_start, own_count, 0)
    vis_norm, vis_qkv = norm_qkv(vis, norm1_gain, norm1_bias, qkv_weight, 0)
    part_mix, part_lse = query_forward(query_qkv, own_qkv, vis_qkv, self_bias)
    mixes, tops = [part_mix], [part_lse]
    for step in range(1, strips):
        mixes.append(moved(part_mix, "strip", step))
        tops.append(moved(part_lse, "strip", step))
    vis_attn, vis_lse = window_forward(vis_qkv, query_qkv, region_row, region_col, closed)

    weights = (out_weight, out_bias, norm2_gain, norm2_bias, up_weight, up_bias, down_weight, down_bias)
    vis_x1, vis_b, vis_hid, vis_slope, vis_result = ffn_forward(vis, vis_attn, *weights, 0)
    vis_down = weight_grad(vis_hid, vis_cot)
    vis_dz, vis_upb, vis_dx1, vis_du, vis_do, vis_sums = ffn_backward(
        vis_cot, vis_slope, vis_x1, down_weight, up_weight, out_weight, norm2_gain, 0
    )
    vis_up = weight_grad(vis_b, vis_dz)
    vis_outg = weight_grad(vis_attn, vis_du)

    pairs = part_lse.shape[0]
    tops = jnp.stack(tops)
    top = tops.max(0)
    shares = jnp.exp(tops - top)
    total = shares.sum(0)
    query_lse = top + jnp.log(total)
    shares = (shares / total).reshape(strips, pairs, 2, query_count)
    shares = shares.transpose(0, 3, 1, 2).reshape(strips, query_count, HEADS, 1)
    mixes = jnp.stack(mixes).reshape(strips, query_count, HEADS, -1)
    query_mix = (mixes.astype(f32) * shares).sum(0).reshape(query_count, features)
    query_attn = query_mix.astype(bf16)
    query_x1, query_b, query_hid, query_slope, query_result = ffn_forward(
        query, query_attn, *weights, 1
    )
    query_dz, query_upb, query_dx1, query_du, query_do, query_sums = ffn_backward(
        query_cot, query_slope, query_x1, down_weight, up_weight, out_weight, norm2_gain, 1
    )
    query_delta = (query_do.astype(f32) * query_mix).reshape(query_count, pairs, 2, -1).sum(-1)
    query_delta = query_delta.transpose(1, 2, 0).reshape(pairs, 1, 2 * query_count)

    def own_slice(values):
        span = values.shape[1] // strips
        return lax.dynamic_slice_in_dim(values, strip * span, span, 1)

    def query_weight_grad(left, right):
        return weight_grad(own_slice(left), right)

    down_grad = reduce_line_first(vis_down, query_weight_grad(query_hid, query_cot))
    up_grad = reduce_pages_first(vis_up, query_weight_grad(query_b, query_dz))
    out_grad = reduce_line_first(vis_outg, query_weight_grad(query_attn, query_du))

    vis_dq, vis_dk, vis_dv, part_q, part_k, part_v, self_k, self_v = attention_backward(
        vis_qkv,
        query_qkv,
        own_qkv,
        vis_do,
        query_do,
        region_row,
        region_col,
        closed,
        self_bias,
        vis_lse,
        query_lse,
        query_delta,
        0,
        pairs,
    )
    part = jnp.concatenate([part_q, part_k, part_v], 1).astype(bf16)
    own_dqkv = sum_line(sum_cores(by_strip(part))).astype(f32)
    own_dqkv = own_dqkv + jnp.concatenate([jnp.zeros_like(self_k), self_k, self_v], 1)
    own_dqkv = own_dqkv.astype(bf16)
    query_dqkv = lax.all_gather(own_dqkv, "strip", axis=0, tiled=True)

    vis_qkvg = jnp.concatenate([weight_grad(vis_norm, each) for each in (vis_dq, vis_dk, vis_dv)], 1)
    qkv_grad = reduce_pages_first(vis_qkvg, query_weight_grad(query_norm, query_dqkv))

    vis_input, vis_head = input_grad(
        vis_dq, vis_dk, vis_dv, qkv_weight, vis, vis_dx1, norm1_gain, 0
    )
    own_input, own_head = input_grad(
        own_dqkv[:, :features],
        own_dqkv[:, features : 2 * features],
        own_dqkv[:, 2 * features :],
        qkv_weight,
        query_tokens[0],
        lax.dynamic_slice_in_dim(query_dx1, own_start, own_count, 0),
        norm1_gain,
        1,
    )
    own_result = lax.dynamic_slice_in_dim(query_result, own_start, own_count, 0)

    def to_rows(cells):
        grid = from_windows(cells, columns)
        tail = moved(grid[local_rows - SHIFT :], "strip", 1)
        return jnp.concatenate([tail, grid[: local_rows - SHIFT]], 0)[None]

    once = jnp.where(strip == 0, 1.0, 0.0)
    small = jnp.stack(
        [
            jnp.concatenate([vis_head[:2], vis_sums[:4], vis_upb.reshape(-1, features)], 0),
            jnp.concatenate(
                [own_head[:2], once * query_sums[:4], once * query_upb.reshape(-1, features)], 0
            ),
        ]
    )
    small = lax.psum(small, ("page", "strip"))
    gain_one, bias_one, gain_two, bias_two, obias, dbias = [own_slice(small[:, i]) for i in range(6)]
    ubias = own_slice(small[:, 6:].reshape(2, -1))

    return (
        to_rows(vis_result),
        own_result[None],
        to_rows(vis_input),
        own_input[None],
        gain_one,
        bias_one,
        qkv_grad,
        out_grad,
        obias,
        gain_two,
        bias_two,
        up_grad,
        ubias,
        down_grad,
        dbias,
    )


def solution(mesh):
    return jax.shard_map(
        body,
        mesh=mesh,
        in_specs=(
            P("page", "strip", None, None),
            P("page", "strip", None),
            P("page", None, None),
            P("page", None),
            P("page"),
            P(),
            P(),
            P(),
            P(),
            P(),
            P(),
            P(),
            P(),
            P(),
            P(),
            P(),
            P("page", "strip", None, None),
            P("page", "strip", None),
        ),
        out_specs=(
            P("page", "strip", None, None),
            P("page", "strip", None),
            P("page", "strip", None, None),
            P("page", "strip", None),
            P(None, "strip"),
            P(None, "strip"),
            P(None, "strip", None),
            P(None, "strip", None),
            P(None, "strip"),
            P(None, "strip"),
            P(None, "strip"),
            P(None, "strip", None),
            P(None, "strip"),
            P(None, "strip", None),
            P(None, "strip"),
        ),
        check_vma=False,
    )
```

```python
import functools

import jax
import jax.numpy as jnp
from jax import lax
from jax.experimental import pallas as pl
from jax.experimental.pallas import tpu as pltpu
from jax.sharding import PartitionSpec as P

HEADS = 12
WIN = 12
SHIFT = 6
CELLS = WIN * WIN
PAIR = 128
MASKED = -1000000000.0
VMEM_LIMIT = 56 * 1024 * 1024

bf16 = jnp.bfloat16
f32 = jnp.float32


def params():
    return pltpu.CompilerParams(vmem_limit_bytes=VMEM_LIMIT)


def row_block(rows):
    for size in range(336, 15, -16):
        if rows % size == 0:
            return size
    return rows


def dot_nn(a, b):
    return lax.dot_general(a, b, (((1,), (0,)), ((), ())), preferred_element_type=f32)


def dot_nt(a, b):
    return lax.dot_general(a, b, (((1,), (1,)), ((), ())), preferred_element_type=f32)


def dot_tn(a, b):
    return lax.dot_general(a, b, (((0,), (0,)), ((), ())), preferred_element_type=f32)


def cost(flops, moved, special=0):
    share = 30
    return pl.CostEstimate(
        flops=int(flops) // share,
        bytes_accessed=int(moved) // share,
        transcendentals=int(special) // share,
    )


def whole(shape):
    return pl.BlockSpec(shape, lambda *_: (0,) * len(shape))


def normalised(values):
    center = values - jnp.mean(values, -1, keepdims=True)
    spread = jnp.mean(center * center, -1, keepdims=True)
    rstd = lax.rsqrt(spread + 1e-05)
    return center * rstd, rstd


def norm_back(grad, hat, rstd, gain):
    scaled = grad * gain
    mean_one = jnp.mean(scaled, -1, keepdims=True)
    mean_two = jnp.mean(scaled * hat, -1, keepdims=True)
    return rstd * (scaled - mean_one - hat * mean_two)


def enter_kernel(own_ref, head_ref, out_ref, row_ref, cells_ref):
    columns = own_ref.shape[1]
    for r in range(WIN):
        row = own_ref[SHIFT + r] if r < WIN - SHIFT else head_ref[r - (WIN - SHIFT)]
        row_ref[0:columns, :] = row.astype(f32)
        row_ref[columns : columns + SHIFT, :] = row_ref[0:SHIFT, :]
        for w in range(columns // WIN):
            at = w * CELLS + r * WIN
            cells_ref[at : at + WIN, :] = row_ref[w * WIN + SHIFT : (w + 1) * WIN + SHIFT, :]
    for w in range(columns // WIN):
        at = slice(w * CELLS, (w + 1) * CELLS)
        out_ref[at, :] = cells_ref[at, :].astype(bf16)


def enter(own, head):
    rows, columns, width = own.shape
    cells = rows * columns
    return pl.pallas_call(
        enter_kernel,
        out_shape=jax.ShapeDtypeStruct((cells, width), bf16),
        scratch_shapes=[
            pltpu.VMEM((columns + 2 * WIN, width), f32),
            pltpu.VMEM((cells, width), f32),
        ],
        compiler_params=params(),
        cost_estimate=cost(0, 4 * cells * width),
        name="enter",
    )(own, head)


def leave_kernel(cells_ref, keep_ref, send_ref, row_ref, wide_ref):
    columns = keep_ref.shape[1]
    for w in range(columns // WIN):
        at = slice(w * CELLS, (w + 1) * CELLS)
        wide_ref[at, :] = cells_ref[at, :].astype(f32)
    for r in range(WIN):
        for w in range(columns // WIN):
            at = w * CELLS + r * WIN
            row_ref[w * WIN + SHIFT : (w + 1) * WIN + SHIFT, :] = wide_ref[at : at + WIN, :]
        row_ref[0:SHIFT, :] = row_ref[columns : columns + SHIFT, :]
        row = row_ref[0:columns, :].astype(bf16)
        if r < WIN - SHIFT:
            keep_ref[r] = row
        else:
            send_ref[r - (WIN - SHIFT)] = row


def leave(cells, columns):
    width = cells.shape[1]
    return pl.pallas_call(
        leave_kernel,
        out_shape=[
            jax.ShapeDtypeStruct((WIN - SHIFT, columns, width), bf16),
            jax.ShapeDtypeStruct((SHIFT, columns, width), bf16),
        ],
        scratch_shapes=[
            pltpu.VMEM((columns + 2 * WIN, width), f32),
            pltpu.VMEM(cells.shape, f32),
        ],
        compiler_params=params(),
        cost_estimate=cost(0, 4 * cells.size),
        name="leave",
    )(cells)


def qkv_kernel(stream, x_ref, gain_ref, bias_ref, w_ref, a_ref, out_ref):
    rows, width = x_ref.shape
    block = row_block(rows)
    row = slice(stream, stream + 1)
    ats = [slice(i * block, (i + 1) * block) for i in range(rows // block)]

    @pl.when(pl.program_id(0) == 0)
    def _():
        for at in ats:
            hat, _ = normalised(x_ref[at, :].astype(f32))
            low = (hat * gain_ref[row, :] + bias_ref[row, :]).astype(bf16)
            a_ref[at, :] = low
            out_ref[at, :] = dot_nn(low, w_ref[...]).astype(bf16)

    @pl.when(pl.program_id(0) != 0)
    def _():
        for at in ats:
            out_ref[at, :] = dot_nn(a_ref[at, :], w_ref[...]).astype(bf16)


def norm_qkv(x, gain, bias, weight, stream):
    rows, width = x.shape
    full = weight.shape[-1]
    return pl.pallas_call(
        functools.partial(qkv_kernel, stream),
        grid=(full // width,),
        in_specs=[
            whole((rows, width)),
            whole(gain.shape),
            whole(bias.shape),
            pl.BlockSpec((None, width, width), lambda j: (stream, 0, j)),
        ],
        out_specs=[whole((rows, width)), pl.BlockSpec((rows, width), lambda j: (0, j))],
        out_shape=[
            jax.ShapeDtypeStruct((rows, width), bf16),
            jax.ShapeDtypeStruct((rows, full), bf16),
        ],
        compiler_params=params(),
        cost_estimate=cost(2 * rows * width * full, 2 * rows * (2 * width + full) + 2 * width * full),
        name="norm_qkv",
    )(x, gain, bias, weight)


def first_half(shape):
    return lax.broadcasted_iota(jnp.int32, shape, len(shape) - 1) < PAIR // 2


def stacked(block):
    left = first_half(block.shape)
    zero = jnp.zeros_like(block)
    return jnp.concatenate([jnp.where(left, block, zero), jnp.where(left, zero, block)], 0)


def joined(upright):
    rows = upright.shape[0] // 2
    return jnp.where(first_half((rows, PAIR)), upright[:rows], upright[rows:])


def unstacked(turned):
    return joined(turned.T)


def query_forward_kernel(qq_ref, k_ref, v_ref, ko_ref, vo_ref, bias_ref, out_ref, lse_ref, s_ref):
    queries = qq_ref.shape[0]
    cells = k_ref.shape[0]
    own = ko_ref.shape[0]
    scaled = stacked(qq_ref[...] * 0.125)
    bias = bias_ref[...]
    self_score = dot_nt(ko_ref[...], scaled) + jnp.concatenate([bias, bias], 1)
    top = jnp.max(self_score, 0, keepdims=True)
    block = row_block(cells)
    blocks = [slice(i * block, (i + 1) * block) for i in range(cells // block)]
    for at in blocks:
        score = dot_nt(k_ref[at, :], scaled)
        s_ref[at, :] = score
        top = jnp.maximum(top, jnp.max(score, 0, keepdims=True))
    prob = jnp.exp(self_score - top)
    total = jnp.sum(prob, 0, keepdims=True)
    mixed = dot_nn(vo_ref[...].T, prob.astype(bf16))
    for at in blocks:
        prob = jnp.exp(s_ref[at, :] - top)
        total = total + jnp.sum(prob, 0, keepdims=True)
        mixed = mixed + dot_nn(v_ref[at, :].T, prob.astype(bf16))
    out_ref[...] = unstacked(mixed * (1.0 / total)).astype(bf16)
    lse_ref[...] = top + jnp.log(total)


def query_forward(query_qkv, own_qkv, vis_qkv, self_bias):
    cells = vis_qkv.shape[0]
    queries = query_qkv.shape[0]
    own = own_qkv.shape[0]
    width = query_qkv.shape[1] // 3
    pairs = width // PAIR
    keys = cells + own

    def part(rows, j):
        return pl.BlockSpec((rows, PAIR), lambda p, j=j: (0, j * pairs + p))

    return pl.pallas_call(
        query_forward_kernel,
        grid=(pairs,),
        in_specs=[
            part(queries, 0),
            part(cells, 1),
            part(cells, 2),
            part(own, 1),
            part(own, 2),
            whole(self_bias.shape),
        ],
        out_specs=[part(queries, 0), pl.BlockSpec((None, 1, 2 * queries), lambda p: (p, 0, 0))],
        out_shape=[
            jax.ShapeDtypeStruct((queries, width), bf16),
            jax.ShapeDtypeStruct((pairs, 1, 2 * queries), f32),
        ],
        scratch_shapes=[pltpu.VMEM((cells, 2 * queries), f32)],
        compiler_params=params(),
        cost_estimate=cost(
            4 * 2 * queries * keys * width, 4 * cells * width, 2 * queries * keys * pairs
        ),
        name="query_forward",
    )(query_qkv, vis_qkv, vis_qkv, own_qkv, own_qkv, self_bias)


def window_forward_kernel(
    windows,
    q_ref,
    k_ref,
    v_ref,
    kq_ref,
    vq_ref,
    row_ref,
    col_ref,
    open_ref,
    out_ref,
    lse_ref,
    scaled_ref,
    near_ref,
    mixed_ref,
    far_ref,
):
    cells = [slice(w * CELLS, (w + 1) * CELLS) for w in range(windows)]
    lanes = [slice(2 * w * CELLS, 2 * (w + 1) * CELLS) for w in range(windows)]
    tops = []
    for w in range(windows):
        scaled = stacked(q_ref[cells[w], :] * 0.125)
        scaled_ref[lanes[w], :] = scaled
        near = dot_nt(k_ref[cells[w], :], scaled)
        near = jnp.where(col_ref[w] == row_ref[w], near, MASKED)
        near_ref[w] = near
        tops.append(jnp.max(near, 0, keepdims=True))
    far = dot_nt(kq_ref[...], scaled_ref[...]) + open_ref[...]
    top = jnp.maximum(jnp.concatenate(tops, 1), jnp.max(far, 0, keepdims=True))
    far = jnp.exp(far - top)
    total = jnp.sum(far, 0, keepdims=True)
    far_mixed = dot_nn(vq_ref[...].T, far.astype(bf16))
    totals = []
    for w in range(windows):
        near = jnp.exp(near_ref[w] - top[:, lanes[w]])
        totals.append(jnp.sum(near, 0, keepdims=True))
        mixed_ref[w] = dot_nn(v_ref[cells[w], :].T, near.astype(bf16))
    total = total + jnp.concatenate(totals, 1)
    share = 1.0 / total
    lse_ref[...] = top + jnp.log(total)
    far_ref[...] = far_mixed
    for w in range(windows):
        turned = (mixed_ref[w] + far_ref[:, lanes[w]]) * share[:, lanes[w]]
        out_ref[cells[w], :] = joined(turned.astype(bf16).T)


def window_forward(vis_qkv, query_qkv, region_row, region_col, closed):
    cells = vis_qkv.shape[0]
    queries = query_qkv.shape[0]
    width = vis_qkv.shape[1] // 3
    pairs = width // PAIR
    windows = cells // CELLS

    def part(rows, j):
        return pl.BlockSpec((rows, PAIR), lambda p, j=j: (0, j * pairs + p))

    return pl.pallas_call(
        functools.partial(window_forward_kernel, windows),
        grid=(pairs,),
        in_specs=[
            part(cells, 0),
            part(cells, 1),
            part(cells, 2),
            part(queries, 1),
            part(queries, 2),
            whole(region_row.shape),
            whole(region_col.shape),
            whole(closed.shape),
        ],
        out_specs=[
            part(cells, 0),
            pl.BlockSpec((None, 1, 2 * cells), lambda p: (p, 0, 0)),
        ],
        out_shape=[
            jax.ShapeDtypeStruct((cells, width), bf16),
            jax.ShapeDtypeStruct((pairs, 1, 2 * cells), f32),
        ],
        scratch_shapes=[
            pltpu.VMEM((2 * cells, PAIR), bf16),
            pltpu.VMEM((windows, CELLS, 2 * CELLS), f32),
            pltpu.VMEM((windows, PAIR, 2 * CELLS), f32),
            pltpu.VMEM((PAIR, 2 * cells), f32),
        ],
        compiler_params=params(),
        cost_estimate=cost(
            8 * cells * (CELLS + queries) * width,
            8 * cells * width,
            2 * pairs * cells * (CELLS + queries),
        ),
        name="window_forward",
    )(vis_qkv, vis_qkv, vis_qkv, query_qkv, query_qkv, region_row, region_col, closed)


def attention_backward_kernel(
    windows,
    q_ref,
    k_ref,
    v_ref,
    do_ref,
    qq_ref,
    kq_ref,
    vq_ref,
    doq_ref,
    ko_ref,
    vo_ref,
    row_ref,
    col_ref,
    open_ref,
    bias_ref,
    lse_ref,
    lseq_ref,
    deltaq_ref,
    dq_ref,
    dk_ref,
    dv_ref,
    dqq_ref,
    dkq_ref,
    dvq_ref,
    dko_ref,
    dvo_ref,
    scaled_ref,
    grad_ref,
    near_ref,
    neart_ref,
    seenk_ref,
    seenv_ref,
    far_ref,
):
    cells = [slice(w * CELLS, (w + 1) * CELLS) for w in range(windows)]
    lanes = [slice(2 * w * CELLS, 2 * (w + 1) * CELLS) for w in range(windows)]
    lse = lse_ref[...]

    deltas = []
    for w in range(windows):
        scaled = stacked(q_ref[cells[w], :] * 0.125)
        grad = stacked(do_ref[cells[w], :])
        scaled_ref[lanes[w], :] = scaled
        grad_ref[lanes[w], :] = grad
        near = dot_nt(k_ref[cells[w], :], scaled)
        near = jnp.exp(jnp.where(col_ref[w] == row_ref[w], near, MASKED) - lse[:, lanes[w]])
        near_t = near * dot_nt(v_ref[cells[w], :], grad)
        near_ref[w] = near
        neart_ref[w] = near_t
        deltas.append(jnp.sum(near_t, 0, keepdims=True))
    kq = kq_ref[...]
    far = jnp.exp(dot_nt(kq, scaled_ref[...]) + open_ref[...] - lse)
    far_t = far * dot_nt(vq_ref[...], grad_ref[...])
    delta = jnp.concatenate(deltas, 1) + jnp.sum(far_t, 0, keepdims=True)
    far_d = (far_t - far * delta).astype(bf16)
    dkq_ref[...] = dot_nn(far_d, scaled_ref[...])
    dvq_ref[...] = dot_nn(far.astype(bf16), grad_ref[...])
    far_ref[...] = dot_nn(kq.T, far_d).T

    scaled_q = stacked(qq_ref[...] * 0.125)
    grad_q = stacked(doq_ref[...])
    lse_q = lseq_ref[...]
    delta_q = deltaq_ref[...]
    bias = bias_ref[...]
    prob = jnp.exp(dot_nt(ko_ref[...], scaled_q) + jnp.concatenate([bias, bias], 1) - lse_q)
    dscore = (prob * (dot_nt(vo_ref[...], grad_q) - delta_q)).astype(bf16)
    dko_ref[...] = dot_nn(dscore, scaled_q)
    dvo_ref[...] = dot_nn(prob.astype(bf16), grad_q)
    turned = dot_nn(ko_ref[...].T, dscore)
    rows = k_ref.shape[0]
    block = row_block(rows)
    for i in range(rows // block):
        at = slice(i * block, (i + 1) * block)
        k_rows = k_ref[at, :]
        prob = jnp.exp(dot_nt(k_rows, scaled_q) - lse_q)
        dscore = (prob * (dot_nt(v_ref[at, :], grad_q) - delta_q)).astype(bf16)
        seenk_ref[at, :] = dot_nn(dscore, scaled_q)
        seenv_ref[at, :] = dot_nn(prob.astype(bf16), grad_q)
        turned = turned + dot_nn(k_rows.T, dscore)
    dqq_ref[...] = unstacked(turned) * 0.125

    for w in range(windows):
        near = near_ref[w]
        near_d = (neart_ref[w] - near * delta[:, lanes[w]]).astype(bf16)
        upright = dot_nn(k_ref[cells[w], :].T, near_d).T + far_ref[lanes[w], :]
        dq_ref[cells[w], :] = (joined(upright) * 0.125).astype(bf16)
        dk_ref[cells[w], :] = (
            dot_nn(near_d, scaled_ref[lanes[w], :]) + seenk_ref[cells[w], :]
        ).astype(bf16)
        dv_ref[cells[w], :] = (
            dot_nn(near.astype(bf16), grad_ref[lanes[w], :]) + seenv_ref[cells[w], :]
        ).astype(bf16)


def attention_backward(
    vis_qkv,
    query_qkv,
    own_qkv,
    grad,
    grad_q,
    region_row,
    region_col,
    closed,
    self_bias,
    lse,
    lse_q,
    delta_q,
    first,
    count,
):
    cells = vis_qkv.shape[0]
    queries = query_qkv.shape[0]
    own = own_qkv.shape[0]
    width = vis_qkv.shape[1] // 3
    pairs = width // PAIR
    windows = cells // CELLS

    def part(rows, j):
        return pl.BlockSpec((rows, PAIR), lambda p, j=j: (0, j * pairs + first + p))

    def result(rows):
        return pl.BlockSpec((rows, PAIR), lambda p: (0, p))

    def stats(array):
        return pl.BlockSpec((None,) + array.shape[1:], lambda p: (first + p, 0, 0))

    span = count * PAIR
    return pl.pallas_call(
        functools.partial(attention_backward_kernel, windows),
        grid=(count,),
        in_specs=[
            part(cells, 0),
            part(cells, 1),
            part(cells, 2),
            part(cells, 0),
            part(queries, 0),
            part(queries, 1),
            part(queries, 2),
            part(queries, 0),
            part(own, 1),
            part(own, 2),
            whole(region_row.shape),
            whole(region_col.shape),
            whole(closed.shape),
            whole(self_bias.shape),
            stats(lse),
            stats(lse_q),
            stats(delta_q),
        ],
        out_specs=[result(cells)] * 3 + [result(queries)] * 3 + [result(own)] * 2,
        out_shape=[jax.ShapeDtypeStruct((cells, span), bf16)] * 3
        + [jax.ShapeDtypeStruct((queries, span), f32)] * 3
        + [jax.ShapeDtypeStruct((own, span), f32)] * 2,
        scratch_shapes=[
            pltpu.VMEM((2 * cells, PAIR), bf16),
            pltpu.VMEM((2 * cells, PAIR), bf16),
            pltpu.VMEM((windows, CELLS, 2 * CELLS), f32),
            pltpu.VMEM((windows, CELLS, 2 * CELLS), f32),
            pltpu.VMEM((cells, PAIR), f32),
            pltpu.VMEM((cells, PAIR), f32),
            pltpu.VMEM((2 * cells, PAIR), f32),
        ],
        compiler_params=params(),
        cost_estimate=cost(
            20 * cells * (CELLS + 2 * queries) * span,
            14 * cells * span,
            2 * count * cells * (CELLS + 2 * queries),
        ),
        name="attention_backward",
    )(
        vis_qkv,
        vis_qkv,
        vis_qkv,
        grad,
        query_qkv,
        query_qkv,
        query_qkv,
        grad_q,
        own_qkv,
        own_qkv,
        region_row,
        region_col,
        closed,
        self_bias,
        lse,
        lse_q,
        delta_q,
    )


def gelu_pair(z):
    below = 0.5 + 0.5 * lax.erf(z * 0.7071067811865476)
    bell = jnp.exp(-0.5 * z * z)
    return z * below, below + z * bell * 0.3989422804014327


def ffn_forward_kernel(
    stream,
    x_ref,
    o_ref,
    wo_ref,
    bo_ref,
    gain_ref,
    bias_ref,
    wu_ref,
    bu_ref,
    wd_ref,
    bd_ref,
    x1_ref,
    b_ref,
    hid_ref,
    slope_ref,
    out_ref,
    sum_ref,
):
    rows, width = x_ref.shape
    block = row_block(rows)
    count = rows // block
    ats = [slice(i * block, (i + 1) * block) for i in range(count)]
    step = pl.program_id(0)
    row = slice(stream, stream + 1)

    @pl.when(step == 0)
    def _():
        for at in ats:
            x1 = x_ref[at, :].astype(f32) + dot_nn(o_ref[at, :], wo_ref[...]) + bo_ref[row, :]
            x1_ref[at, :] = x1
            hat, _ = normalised(x1)
            b_ref[at, :] = (hat * gain_ref[row, :] + bias_ref[row, :]).astype(bf16)
            sum_ref[at, :] = x1 + bd_ref[row, :]

    def project(i):
        return dot_nn(b_ref[ats[i], :], wu_ref[...]) + bu_ref[row, :]

    z = project(0)
    for i in range(count):
        ahead = project(i + 1) if i + 1 < count else None
        hidden, slope = gelu_pair(z)
        hidden = hidden.astype(bf16)
        hid_ref[ats[i], :] = hidden
        slope_ref[ats[i], :] = slope.astype(bf16)
        sum_ref[ats[i], :] += dot_nn(hidden, wd_ref[...])
        z = ahead

    @pl.when(step == pl.num_programs(0) - 1)
    def _():
        out_ref[...] = sum_ref[...].astype(bf16)


def ffn_forward(x, attended, out_w, out_b, gain, bias, up_w, up_b, down_w, down_b, stream):
    rows, width = x.shape
    hidden = up_w.shape[-1]
    chunk = 768
    return pl.pallas_call(
        functools.partial(ffn_forward_kernel, stream),
        grid=(hidden // chunk,),
        in_specs=[
            whole((rows, width)),
            whole((rows, width)),
            pl.BlockSpec((None, width, width), lambda f: (stream, 0, 0)),
            whole(out_b.shape),
            whole(gain.shape),
            whole(bias.shape),
            pl.BlockSpec((None, width, chunk), lambda f: (stream, 0, f)),
            pl.BlockSpec((2, chunk), lambda f: (0, f)),
            pl.BlockSpec((None, chunk, width), lambda f: (stream, f, 0)),
            whole(down_b.shape),
        ],
        out_specs=[
            whole((rows, width)),
            whole((rows, width)),
            pl.BlockSpec((rows, chunk), lambda f: (0, f)),
            pl.BlockSpec((rows, chunk), lambda f: (0, f)),
            whole((rows, width)),
        ],
        out_shape=[
            jax.ShapeDtypeStruct((rows, width), f32),
            jax.ShapeDtypeStruct((rows, width), bf16),
            jax.ShapeDtypeStruct((rows, hidden), bf16),
            jax.ShapeDtypeStruct((rows, hidden), bf16),
            jax.ShapeDtypeStruct((rows, width), bf16),
        ],
        scratch_shapes=[pltpu.VMEM((rows, width), f32)],
        compiler_params=params(),
        cost_estimate=cost(
            2 * rows * width * (2 * hidden + width),
            4 * width * hidden + 4 * rows * hidden + 12 * rows * width,
            2 * rows * hidden,
        ),
        name="ffn_forward",
    )(x, attended, out_w, out_b, gain, bias, up_w, up_b, down_w, down_b)


def ffn_backward_kernel(
    stream,
    g_ref,
    slope_ref,
    x1_ref,
    wd_ref,
    wu_ref,
    wo_ref,
    gain_ref,
    dz_ref,
    upb_ref,
    dx1_ref,
    du_ref,
    do_ref,
    sums_ref,
    sum_ref,
):
    rows, width = g_ref.shape
    block = row_block(rows)
    count = rows // block
    ats = [slice(i * block, (i + 1) * block) for i in range(count)]
    step = pl.program_id(0)
    row = slice(stream, stream + 1)

    @pl.when(step == 0)
    def _():
        sum_ref[...] = jnp.zeros_like(sum_ref)

    upb_ref[...] = jnp.zeros_like(upb_ref)

    def pulled(i):
        return dot_nt(g_ref[ats[i], :], wd_ref[...])

    grad = pulled(0)
    for i in range(count):
        ahead = pulled(i + 1) if i + 1 < count else None
        dz = grad * slope_ref[ats[i], :].astype(f32)
        low = dz.astype(bf16)
        dz_ref[ats[i], :] = low
        upb_ref[...] += jnp.sum(dz, 0, keepdims=True)
        sum_ref[ats[i], :] += dot_nt(low, wu_ref[...])
        grad = ahead

    @pl.when(step == pl.num_programs(0) - 1)
    def _():
        sums_ref[...] = jnp.zeros_like(sums_ref)

        for at in ats:
            hat, rstd = normalised(x1_ref[at, :])
            db = sum_ref[at, :]
            g = g_ref[at, :].astype(f32)
            dx1 = g + norm_back(db, hat, rstd, gain_ref[row, :])
            dx1_ref[at, :] = dx1
            du = dx1.astype(bf16)
            du_ref[at, :] = du
            do_ref[at, :] = dot_nt(du, wo_ref[...]).astype(bf16)
            sums_ref[0:1, :] += jnp.sum(db * hat, 0, keepdims=True)
            sums_ref[1:2, :] += jnp.sum(db, 0, keepdims=True)
            sums_ref[2:3, :] += jnp.sum(dx1, 0, keepdims=True)
            sums_ref[3:4, :] += jnp.sum(g, 0, keepdims=True)


def ffn_backward(g, slope, x1, down_w, up_w, out_w, gain, stream):
    rows, width = g.shape
    hidden = up_w.shape[-1]
    chunk = 768
    return pl.pallas_call(
        functools.partial(ffn_backward_kernel, stream),
        grid=(hidden // chunk,),
        in_specs=[
            whole((rows, width)),
            pl.BlockSpec((rows, chunk), lambda f: (0, f)),
            whole((rows, width)),
            pl.BlockSpec((None, chunk, width), lambda f: (stream, f, 0)),
            pl.BlockSpec((None, width, chunk), lambda f: (stream, 0, f)),
            pl.BlockSpec((None, width, width), lambda f: (stream, 0, 0)),
            whole(gain.shape),
        ],
        out_specs=[
            pl.BlockSpec((rows, chunk), lambda f: (0, f)),
            pl.BlockSpec((1, chunk), lambda f: (0, f)),
            whole((rows, width)),
            whole((rows, width)),
            whole((rows, width)),
            whole((8, width)),
        ],
        out_shape=[
            jax.ShapeDtypeStruct((rows, hidden), bf16),
            jax.ShapeDtypeStruct((1, hidden), f32),
            jax.ShapeDtypeStruct((rows, width), f32),
            jax.ShapeDtypeStruct((rows, width), bf16),
            jax.ShapeDtypeStruct((rows, width), bf16),
            jax.ShapeDtypeStruct((8, width), f32),
        ],
        scratch_shapes=[pltpu.VMEM((rows, width), f32)],
        compiler_params=params(),
        cost_estimate=cost(
            2 * rows * width * (2 * hidden + width),
            4 * width * hidden + 4 * rows * hidden + 14 * rows * width,
        ),
        name="ffn_backward",
    )(g, slope, x1, down_w, up_w, out_w, gain)


def input_kernel(stream, dq_ref, dk_ref, dv_ref, w_ref, x_ref, dx1_ref, gain_ref, out_ref, sums_ref):
    width = x_ref.shape[1]

    @pl.when(pl.program_id(0) == 0)
    def _():
        sums_ref[...] = jnp.zeros_like(sums_ref)

    grad = dot_nt(dq_ref[...], w_ref[:, :width])
    grad = grad + dot_nt(dk_ref[...], w_ref[:, width : 2 * width])
    grad = grad + dot_nt(dv_ref[...], w_ref[:, 2 * width :])
    hat, rstd = normalised(x_ref[...].astype(f32))
    out_ref[...] = (
        dx1_ref[...] + norm_back(grad, hat, rstd, gain_ref[stream : stream + 1, :])
    ).astype(bf16)
    sums_ref[0:1, :] += jnp.sum(grad * hat, 0, keepdims=True)
    sums_ref[1:2, :] += jnp.sum(grad, 0, keepdims=True)


def input_grad(dq, dk, dv, weight, x, dx1, gain, stream):
    rows, width = x.shape
    block = row_block(rows)
    rows_spec = pl.BlockSpec((block, width), lambda i: (i, 0))
    return pl.pallas_call(
        functools.partial(input_kernel, stream),
        grid=(rows // block,),
        in_specs=[rows_spec] * 3
        + [
            pl.BlockSpec((None, width, 3 * width), lambda i: (stream, 0, 0)),
            rows_spec,
            rows_spec,
            whole(gain.shape),
        ],
        out_specs=[rows_spec, whole((8, width))],
        out_shape=[
            jax.ShapeDtypeStruct((rows, width), bf16),
            jax.ShapeDtypeStruct((8, width), f32),
        ],
        compiler_params=params(),
        cost_estimate=cost(6 * rows * width * width, 14 * rows * width + 6 * width * width),
        name="input_grad",
    )(dq, dk, dv, weight, x, dx1, gain)


def after(value, *before):
    return lax.optimization_barrier((value,) + before)[0]


def moved(block, axis, step):
    size = lax.axis_size(axis)
    return lax.ppermute(block, axis, [(i, (i + step) % size) for i in range(size)])


def swapped(block, axis, mask):
    size = lax.axis_size(axis)
    return lax.ppermute(block, axis, [(i, i ^ mask) for i in range(size)])


def other_core(block):
    return swapped(block, "strip", 1)


def place():
    strip = lax.axis_index("strip")
    return lax.axis_size("strip") // 2, strip // 2, strip % 2


def pick(block, index, axis=0):
    return lax.dynamic_index_in_dim(block, index, axis, keepdims=False)


def added(blocks, kind=bf16):
    total = blocks[0].astype(f32)
    for block in blocks[1:]:
        total = total + block.astype(f32)
    return total.astype(kind)


def bit_of(axis, mask):
    return (lax.axis_index(axis) // mask) % 2


class Phase:
    def __init__(self, blocks, dims, axis, mask):
        bit = bit_of(axis, mask)
        self.mine = [pick(block, bit, dim) for block, dim in zip(blocks, dims)]
        theirs = [pick(block, 1 - bit, dim) for block, dim in zip(blocks, dims)]
        self.sent, self.got = exchange(theirs, axis, mask)

    def sums(self, *before):
        mine, got = after((self.mine, self.got), *before)
        return [added(pair) for pair in zip(mine, got)]


class Gather:
    def __init__(self, blocks, dims, axis, mask):
        self.bit = bit_of(axis, mask)
        self.blocks, self.dims = blocks, dims
        self.sent, self.got = exchange(blocks, axis, mask)

    def pairs(self, *before):
        mine, got = after((self.blocks, self.got), *before)
        first = self.bit == 0
        return [
            jnp.stack([jnp.where(first, one, two), jnp.where(first, two, one)], dim)
            for one, two, dim in zip(mine, got, self.dims)
        ]


def exchange(blocks, axis, mask):
    if len(blocks) == 1:
        return blocks[0], [swapped(blocks[0], axis, mask)]
    rows = [block.reshape(-1, block.shape[-1]) for block in blocks]
    sent = jnp.concatenate(rows, 0)
    got = swapped(sent, axis, mask)
    out, at = [], 0
    for block, row in zip(blocks, rows):
        out.append(got[at : at + row.shape[0]].reshape(block.shape))
        at += row.shape[0]
    return sent, out


def by_core(grad):
    strips = lax.axis_size("strip")
    return grad.reshape(strips // 2, 2, grad.shape[0] // strips, grad.shape[1])


def tiled(grad, width):
    count = grad.shape[-1] // width
    return jnp.stack([grad[..., i * width : (i + 1) * width] for i in range(count)], -3)


def untiled(blocks):
    return jnp.concatenate([blocks[i] for i in range(blocks.shape[0])], -1)


def by_page(blocks):
    rows = blocks.shape[-2]
    return blocks.reshape(blocks.shape[:-2] + (2, 2, rows // 4, blocks.shape[-1]))


def from_page(blocks):
    return blocks.reshape(blocks.shape[:-4] + (-1, blocks.shape[-1]))


def by_chip(blocks):
    return blocks.reshape((blocks.shape[0] // 2, 2) + blocks.shape[1:])


def line_exchange(block):
    size, z, _ = place()
    return [pick(block, z)] + [
        moved(pick(block, (z + step) % size), "strip", 2 * step) for step in range(1, size)
    ]


def line_gather(block):
    size, _, _ = place()
    return [block] + [moved(block, "strip", 2 * step) for step in range(1, size)]


def line_order(blocks):
    size, z, _ = place()
    double = jnp.stack(blocks[:1] + blocks[:0:-1] + blocks[:1] + blocks[:0:-1])
    return lax.dynamic_slice_in_dim(double, (size - z) % size, size, 0)


def page_exchange(block):
    size = lax.axis_size("page")
    page = lax.axis_index("page")
    shares = block.reshape(size, block.shape[0] // size, block.shape[1])
    return [pick(shares, page)] + [
        swapped(pick(shares, page ^ mask), "page", mask) for mask in range(1, size)
    ]


def page_gather(block):
    size = lax.axis_size("page")
    return [block] + [swapped(block, "page", mask) for mask in range(1, size)]


def page_order(blocks):
    size = len(blocks)
    page = lax.axis_index("page")
    rows, columns = blocks[0].shape
    joined = jnp.zeros((size * rows, columns), f32)
    for mask, block in enumerate(blocks):
        joined = lax.dynamic_update_slice_in_dim(
            joined, block.astype(f32), (page ^ mask) * rows, 0
        )
    return joined


def core_order(mine, other):
    _, _, core = place()
    pair = jnp.stack(
        [jnp.where(core == 0, mine, other), jnp.where(core == 0, other, mine)], 1
    )
    return pair.reshape(-1, pair.shape[-1])


def packed(mix, lse):
    rows = mix.shape[0]
    pairs = lse.shape[0]
    stats = lse.reshape(pairs, 2, rows).transpose(2, 0, 1).reshape(rows, 2 * pairs)
    stats = jnp.pad(stats, ((0, 0), (0, PAIR - 2 * pairs)))
    return jnp.concatenate([mix.astype(f32), stats], 1)


def merged(blocks):
    width = blocks[0].shape[-1] - PAIR
    lead = blocks[0].shape[:-1]
    tops = [block[..., width : width + HEADS] for block in blocks]
    top = functools.reduce(jnp.maximum, tops)
    shares = [jnp.exp(each - top) for each in tops]
    total = functools.reduce(jnp.add, shares)
    mix = 0.0
    for block, share in zip(blocks, shares):
        heads = block[..., :width].reshape(lead + (HEADS, width // HEADS))
        mix = mix + heads * (share / total)[..., None]
    stats = jnp.pad(top + jnp.log(total), [(0, 0)] * len(lead) + [(0, PAIR - HEADS)])
    return jnp.concatenate([mix.reshape(lead + (width,)), stats], -1)


def region_windows(rows):
    across = rows.shape[1] // WIN
    rolled = jnp.roll(rows, -SHIFT, axis=1)
    return rolled.reshape(WIN, across, WIN).transpose(1, 0, 2).reshape(across, CELLS)


def weight_grad(left, right):
    return dot_tn(left, right).astype(bf16)


def body(
    vis_tokens,
    query_tokens,
    region_ids,
    query_mask,
    answer_len,
    norm1_gain,
    norm1_bias,
    qkv_weight,
    out_weight,
    out_bias,
    norm2_gain,
    norm2_bias,
    up_weight,
    up_bias,
    down_weight,
    down_bias,
    vis_cotangent,
    query_cotangent,
):
    strips = lax.axis_size("strip")
    strip = lax.axis_index("strip")
    chips, z, core = place()
    local_rows, columns, features = vis_tokens.shape[1:]
    own_count = query_tokens.shape[1]
    query_count = query_mask.shape[1]
    total_rows = region_ids.shape[1]
    own_start = strip * own_count

    def own_rows(values):
        return lax.dynamic_slice_in_dim(values, own_start, own_count, 0)

    def own_columns(values):
        span = values.shape[1] // strips
        return lax.dynamic_slice_in_dim(values, strip * span, span, 1)

    tokens = line_gather(query_tokens[0])
    head_rows = moved(vis_tokens[0, :SHIFT], "strip", -1)
    tokens = line_order(tokens)
    query = core_order(tokens, other_core(tokens))

    key_open = query_mask[0] > 0
    key_ids = jnp.arange(query_count, dtype=jnp.int32)
    prompt = key_ids < query_count - answer_len[0]
    closed = jnp.where(key_open & prompt, 0.0, MASKED).astype(f32)[:, None]
    own_ids = own_start + jnp.arange(own_count, dtype=jnp.int32)
    allowed = own_rows(key_open)[:, None] & (
        own_rows(prompt)[:, None] | (own_ids[:, None] <= key_ids[None, :])
    )
    self_bias = jnp.where(allowed, 0.0, MASKED).astype(f32)
    row_ids = (strip * local_rows + SHIFT + jnp.arange(local_rows, dtype=jnp.int32)) % total_rows
    region = region_windows(jnp.take(region_ids[0], row_ids, axis=0))
    region_row = jnp.concatenate([region, region], 1)[:, None, :]
    region_col = region[:, :, None]

    query_norm, query_qkv = norm_qkv(query, norm1_gain, norm1_bias, qkv_weight, 1)
    own_qkv = own_rows(query_qkv)
    vis = enter(vis_tokens[0], after(head_rows, query_qkv))
    head_cot = moved(after(vis_cotangent[0, :SHIFT], vis), "strip", -1)
    vis_norm, vis_qkv = norm_qkv(vis, norm1_gain, norm1_bias, qkv_weight, 0)

    part = packed(*query_forward(query_qkv, own_qkv, vis_qkv, self_bias))
    part = by_core(part)
    mine, theirs = pick(part, core, 1), pick(part, 1 - core, 1)
    others = other_core(theirs)
    vis_cot = enter(vis_cotangent[0], after(head_cot, theirs))
    part = merged(after([mine, others], vis_cot))
    others = swapped(part, "strip", 2)

    vis_attn, vis_lse = window_forward(
        after(vis_qkv, part), query_qkv, region_row, region_col, closed
    )
    part = merged(after([part, others], vis_attn))
    mask = 4
    while 2 * mask < strips:
        part = merged([part, swapped(part, "strip", mask)])
        mask = 2 * mask
    others = swapped(part, "strip", mask)
    cotangents = line_gather(after(query_cotangent[0], vis_attn))

    weights = (out_weight, out_bias, norm2_gain, norm2_bias, up_weight, up_bias, down_weight, down_bias)
    vis_x1, vis_b, vis_hid, vis_slope, vis_result = ffn_forward(
        vis, after(vis_attn, part), *weights, 0
    )
    part = merged(after([part, others], vis_result))
    others = other_core(part)
    cotangents = line_order(after(cotangents, vis_result))
    cot_others = other_core(cotangents)
    vis_down = weight_grad(after(vis_hid, part), vis_cot)
    down = by_core(vis_down)
    down = down.reshape(chips, 2, -1, features // strips, features)
    down_core = Phase([down], [1], "strip", 1)

    every = core_order(*after((part, others), down_core.sent))
    query_cot = core_order(cotangents, cot_others)
    query_mix = every[:, :features]
    stats = every[:, features : features + HEADS]
    query_lse = stats.T.reshape(HEADS // 2, 1, 2 * query_count)
    query_attn = query_mix.astype(bf16)
    query_x1, query_b, query_hid, query_slope, query_result = ffn_forward(
        query, query_attn, *weights, 1
    )
    (down,) = down_core.sums(query_result)
    down_x = Phase([by_page(down)], [3], "page", 1)
    query_dz, query_upb, query_dx1, query_du, query_do, query_sums = ffn_backward(
        query_cot, after(query_slope, down_x.sent), query_x1, down_weight, up_weight, out_weight, norm2_gain, 1
    )
    query_delta = (query_do.astype(f32) * query_mix).reshape(query_count, HEADS, -1).sum(-1)
    query_delta = query_delta.T.reshape(HEADS // 2, 1, 2 * query_count)

    def query_grads(left, right):
        return weight_grad(own_columns(left), right)

    up_rows = features // strips
    one = jnp.concatenate(
        [
            tiled(query_grads(query_b, query_dz), features),
            query_grads(query_attn, query_du)[None],
            query_grads(query_hid, query_cot).reshape(-1, up_rows, features),
        ],
        0,
    )
    one_x = Phase([by_page(one)], [2], "page", 1)

    vis_dz, vis_upb, vis_dx1, vis_du, vis_do, vis_sums = ffn_backward(
        after(vis_cot, one_x.sent), vis_slope, vis_x1, down_weight, up_weight, out_weight, norm2_gain, 0
    )
    (down,) = down_x.sums(vis_do)
    (one,) = one_x.sums(vis_do)
    early_y = Phase([down, one], [2, 1], "page", 2)
    vis_up = weight_grad(after(vis_b, early_y.sent), vis_dz)
    vis_outg = weight_grad(vis_attn, vis_du)
    up = jnp.concatenate(
        [tiled(by_core(vis_up), features), tiled(by_core(vis_outg), features)], 2
    )
    up_core = Phase([up], [1], "strip", 1)
    vis_keep, vis_send = leave(after(vis_result, up_core.sent), columns)
    vis_first = moved(vis_send, "strip", 1)
    (up,) = up_core.sums(vis_keep)
    up_one = Phase([by_chip(up)], [1], "strip", 2)

    pairs = HEADS // 2
    half = pairs // 2

    def backward(values, first):
        return attention_backward(
            values,
            query_qkv,
            own_qkv,
            vis_do,
            query_do,
            region_row,
            region_col,
            closed,
            self_bias,
            vis_lse,
            query_lse,
            query_delta,
            first,
            half,
        )

    back_one = backward(after(vis_qkv, up_one.sent), 0)
    grads = [by_core(weight_grad(vis_norm, each)) for each in back_one[:3]]
    first_core = Phase([jnp.stack(grads, 2)], [1], "strip", 1)
    down, one = early_y.sums(first_core.sent)
    down_one = Phase([by_chip(down)], [1], "strip", 2)
    one_gx = Gather([one], [1], "page", 1)
    (up,) = up_one.sums(first_core.sent)
    up_x = Phase([by_page(up)], [3], "page", 1)

    back_two = backward(
        after(vis_qkv, first_core.sent, down_one.sent, up_x.sent, one_gx.sent), half
    )
    spread = [jnp.concatenate(two, 1) for two in zip(back_one, back_two)]
    part_grad = by_core(jnp.concatenate(spread[3:6], 1).astype(bf16))
    part_core = Phase([part_grad], [1], "strip", 1)
    grads = [
        by_core(weight_grad(after(vis_norm, part_core.sent), each)) for each in back_two[:3]
    ]
    second_core = Phase([jnp.stack(grads, 2)], [1], "strip", 1)
    (part_grad,) = part_core.sums(second_core.sent)
    part_line = line_exchange(part_grad)
    (first,) = first_core.sums(back_two[0])
    (second,) = second_core.sums(spread[0], spread[1], spread[2])
    qkv_x = Phase([by_page(jnp.concatenate([first, second], 1))], [3], "page", 1)

    vis_input, vis_head = input_grad(
        after(spread[0], qkv_x.sent, part_grad),
        spread[1],
        spread[2],
        qkv_weight,
        vis,
        vis_dx1,
        norm1_gain,
        0,
    )
    own_dqkv = added(after(part_line, vis_input), f32)
    own_dqkv = own_dqkv + jnp.concatenate([jnp.zeros_like(spread[6]), spread[6], spread[7]], 1)
    own_dqkv = own_dqkv.astype(bf16)
    own_every = line_gather(own_dqkv)
    grad_keep, grad_send = leave(after(vis_input, own_dqkv), columns)
    grad_first = moved(grad_send, "strip", 1)
    (qkv,) = qkv_x.sums(grad_keep)
    qkv_y = Phase([qkv], [2], "page", 2)
    own_input, own_head = input_grad(
        own_dqkv[:, :features],
        own_dqkv[:, features : 2 * features],
        own_dqkv[:, 2 * features :],
        qkv_weight,
        query_tokens[0],
        own_rows(query_dx1),
        norm1_gain,
        1,
    )
    own_lined = line_order(after(own_every, own_input))
    query_dqkv = core_order(own_lined, other_core(own_lined))
    query_qkvg = query_grads(query_norm, query_dqkv)
    three_pages = page_exchange(query_qkvg)
    (qkv,) = qkv_y.sums(query_qkvg)
    qkv_line = line_exchange(qkv)
    three = added(three_pages)
    three_every = page_gather(three)
    qkv = added(qkv_line)
    six, rows, span = qkv.shape
    qkv_every = page_gather(qkv.reshape(six * rows, span))

    (up,) = up_x.sums(back_two[0])
    up_y = Phase([up], [2], "page", 2)
    (down,) = down_one.sums(back_two[0])
    (one,) = one_gx.pairs(back_two[0])
    one_gy = Gather([one], [1], "page", 2)
    (up,) = up_y.sums(vis_input)
    mask = 4
    while 2 * mask < strips:
        up, down = Phase([by_chip(up), by_chip(down)], [1, 1], "strip", mask).sums()
        mask = 2 * mask
    line_two = Phase([by_chip(up), by_chip(down)], [1, 1], "strip", mask)
    up, down = [each[0] for each in line_two.sums(own_input)]
    late_gx = Gather([up, down], [1, 1], "page", 1)
    up, down = late_gx.pairs(query_qkvg)
    late_gy = Gather([up, down], [1, 1], "page", 2)

    once = jnp.where(strip == 0, 1.0, 0.0)
    small = jnp.concatenate(
        [
            vis_head[:2],
            vis_sums[:4],
            vis_upb.reshape(-1, features),
            own_head[:2],
            once * query_sums[:4],
            once * query_upb.reshape(-1, features),
        ],
        0,
    )
    mask = 1
    while mask < strips:
        small = small + swapped(small, "strip", mask)
        mask = 2 * mask
    small = small + swapped(small, "page", 1)
    small = (small + swapped(small, "page", 2)).reshape(2, -1, features)

    up, down = [from_page(each) for each in late_gy.pairs(three)]
    (one,) = one_gy.pairs(three)
    one = from_page(one)
    hidden = up_weight.shape[-1] // features
    up_grad = jnp.stack([untiled(up[:hidden]), untiled(one[:hidden])]).astype(f32)
    out_grad = jnp.stack([up[hidden], one[hidden]]).astype(f32)
    down_grad = jnp.stack([down, one[hidden + 1 :]]).astype(f32).reshape(2, -1, features)
    whole_qkv = page_order(qkv_every).reshape(-1, six, rows, span)
    whole_qkv = whole_qkv.transpose(1, 0, 2, 3).reshape(six, -1, span)
    vis_qkv_grad = jnp.concatenate([whole_qkv[i] for i in (0, 3, 1, 4, 2, 5)], 1)
    qkv_grad = jnp.stack([vis_qkv_grad, page_order(three_every)])

    gain_one, bias_one, gain_two, bias_two, obias, dbias = [
        own_columns(small[:, i]) for i in range(6)
    ]
    ubias = own_columns(small[:, 6:].reshape(2, -1))

    return (
        jnp.concatenate([vis_first, vis_keep], 0)[None],
        own_rows(query_result)[None],
        jnp.concatenate([grad_first, grad_keep], 0)[None],
        own_input[None],
        gain_one,
        bias_one,
        qkv_grad,
        out_grad,
        obias,
        gain_two,
        bias_two,
        up_grad,
        ubias,
        down_grad,
        dbias,
    )


def solution(mesh):
    return jax.shard_map(
        body,
        mesh=mesh,
        in_specs=(
            P("page", "strip", None, None),
            P("page", "strip", None),
            P("page", None, None),
            P("page", None),
            P("page"),
            P(),
            P(),
            P(),
            P(),
            P(),
            P(),
            P(),
            P(),
            P(),
            P(),
            P(),
            P("page", "strip", None, None),
            P("page", "strip", None),
        ),
        out_specs=(
            P("page", "strip", None, None),
            P("page", "strip", None),
            P("page", "strip", None, None),
            P("page", "strip", None),
            P(None, "strip"),
            P(None, "strip"),
            P(None, "strip", None),
            P(None, "strip", None),
            P(None, "strip"),
            P(None, "strip"),
            P(None, "strip"),
            P(None, "strip", None),
            P(None, "strip"),
            P(None, "strip", None),
            P(None, "strip"),
        ),
        check_vma=False,
    )
```

```python
import functools

import jax
import jax.numpy as jnp
from jax import lax
from jax.experimental import pallas as pl
from jax.experimental.pallas import tpu as pltpu
from jax.sharding import PartitionSpec as P

HEADS = 12
WIN = 12
SHIFT = 6
CELLS = WIN * WIN
PAIR = 128
MASKED = -1000000000.0
VMEM_LIMIT = 56 * 1024 * 1024

bf16 = jnp.bfloat16
f32 = jnp.float32


def params():
    return pltpu.CompilerParams(vmem_limit_bytes=VMEM_LIMIT)


def row_block(rows):
    for size in range(336, 15, -16):
        if rows % size == 0:
            return size
    return rows


def dot_nn(a, b):
    return lax.dot_general(a, b, (((1,), (0,)), ((), ())), preferred_element_type=f32)


def dot_nt(a, b):
    return lax.dot_general(a, b, (((1,), (1,)), ((), ())), preferred_element_type=f32)


def dot_tn(a, b):
    return lax.dot_general(a, b, (((0,), (0,)), ((), ())), preferred_element_type=f32)


def cost(flops, moved, special=0):
    share = 20000
    return pl.CostEstimate(
        flops=int(flops) // share,
        bytes_accessed=int(moved) // share,
        transcendentals=int(special) // share,
    )


def whole(shape):
    return pl.BlockSpec(shape, lambda *_: (0,) * len(shape))


def normalised(values):
    center = values - jnp.mean(values, -1, keepdims=True)
    spread = jnp.mean(center * center, -1, keepdims=True)
    rstd = lax.rsqrt(spread + 1e-05)
    return center * rstd, rstd


def norm_back(grad, hat, rstd, gain):
    scaled = grad * gain
    mean_one = jnp.mean(scaled, -1, keepdims=True)
    mean_two = jnp.mean(scaled * hat, -1, keepdims=True)
    return rstd * (scaled - mean_one - hat * mean_two)


def enter_kernel(own_ref, head_ref, out_ref, row_ref, cells_ref):
    columns = own_ref.shape[1]
    for r in range(WIN):
        row = own_ref[SHIFT + r] if r < WIN - SHIFT else head_ref[r - (WIN - SHIFT)]
        row_ref[0:columns, :] = row.astype(f32)
        row_ref[columns : columns + SHIFT, :] = row_ref[0:SHIFT, :]
        for w in range(columns // WIN):
            at = w * CELLS + r * WIN
            cells_ref[at : at + WIN, :] = row_ref[w * WIN + SHIFT : (w + 1) * WIN + SHIFT, :]
    for w in range(columns // WIN):
        at = slice(w * CELLS, (w + 1) * CELLS)
        out_ref[at, :] = cells_ref[at, :].astype(bf16)


def enter(own, head):
    rows, columns, width = own.shape
    cells = rows * columns
    return pl.pallas_call(
        enter_kernel,
        out_shape=jax.ShapeDtypeStruct((cells, width), bf16),
        scratch_shapes=[
            pltpu.VMEM((columns + 2 * WIN, width), f32),
            pltpu.VMEM((cells, width), f32),
        ],
        compiler_params=params(),
        cost_estimate=cost(0, 4 * cells * width),
        name="enter",
    )(own, head)


def leave_kernel(cells_ref, keep_ref, send_ref, row_ref, wide_ref):
    columns = keep_ref.shape[1]
    for w in range(columns // WIN):
        at = slice(w * CELLS, (w + 1) * CELLS)
        wide_ref[at, :] = cells_ref[at, :].astype(f32)
    for r in range(WIN):
        for w in range(columns // WIN):
            at = w * CELLS + r * WIN
            row_ref[w * WIN + SHIFT : (w + 1) * WIN + SHIFT, :] = wide_ref[at : at + WIN, :]
        row_ref[0:SHIFT, :] = row_ref[columns : columns + SHIFT, :]
        row = row_ref[0:columns, :].astype(bf16)
        if r < WIN - SHIFT:
            keep_ref[r] = row
        else:
            send_ref[r - (WIN - SHIFT)] = row


def leave(cells, columns):
    width = cells.shape[1]
    return pl.pallas_call(
        leave_kernel,
        out_shape=[
            jax.ShapeDtypeStruct((WIN - SHIFT, columns, width), bf16),
            jax.ShapeDtypeStruct((SHIFT, columns, width), bf16),
        ],
        scratch_shapes=[
            pltpu.VMEM((columns + 2 * WIN, width), f32),
            pltpu.VMEM(cells.shape, f32),
        ],
        compiler_params=params(),
        cost_estimate=cost(0, 4 * cells.size),
        name="leave",
    )(cells)


def qkv_kernel(stream, x_ref, gain_ref, bias_ref, w_ref, a_ref, out_ref):
    rows, width = x_ref.shape
    block = row_block(rows)
    row = slice(stream, stream + 1)
    ats = [slice(i * block, (i + 1) * block) for i in range(rows // block)]

    @pl.when(pl.program_id(0) == 0)
    def _():
        for at in ats:
            hat, _ = normalised(x_ref[at, :].astype(f32))
            low = (hat * gain_ref[row, :] + bias_ref[row, :]).astype(bf16)
            a_ref[at, :] = low
            out_ref[at, :] = dot_nn(low, w_ref[...]).astype(bf16)

    @pl.when(pl.program_id(0) != 0)
    def _():
        for at in ats:
            out_ref[at, :] = dot_nn(a_ref[at, :], w_ref[...]).astype(bf16)


def norm_qkv(x, gain, bias, weight, stream):
    rows, width = x.shape
    full = weight.shape[-1]
    return pl.pallas_call(
        functools.partial(qkv_kernel, stream),
        grid=(full // width,),
        in_specs=[
            whole((rows, width)),
            whole(gain.shape),
            whole(bias.shape),
            pl.BlockSpec((None, width, width), lambda j: (stream, 0, j)),
        ],
        out_specs=[whole((rows, width)), pl.BlockSpec((rows, width), lambda j: (0, j))],
        out_shape=[
            jax.ShapeDtypeStruct((rows, width), bf16),
            jax.ShapeDtypeStruct((rows, full), bf16),
        ],
        compiler_params=params(),
        cost_estimate=cost(2 * rows * width * full, 2 * rows * (2 * width + full) + 2 * width * full),
        name="norm_qkv",
    )(x, gain, bias, weight)


def first_half(shape):
    return lax.broadcasted_iota(jnp.int32, shape, len(shape) - 1) < PAIR // 2


def stacked(block):
    left = first_half(block.shape)
    zero = jnp.zeros_like(block)
    return jnp.concatenate([jnp.where(left, block, zero), jnp.where(left, zero, block)], 0)


def row_sums(values):
    ones = jnp.ones((8, PAIR), f32)
    return lax.dot_general(
        ones,
        values,
        (((1,), (1,)), ((), ())),
        precision=lax.Precision.HIGHEST,
        preferred_element_type=f32,
    )[:1]


def joined(upright):
    rows = upright.shape[0] // 2
    return jnp.where(first_half((rows, PAIR)), upright[:rows], upright[rows:])


def unstacked(turned):
    return joined(turned.T)


def query_forward_kernel(qq_ref, k_ref, v_ref, ko_ref, vo_ref, bias_ref, out_ref, lse_ref, s_ref):
    queries = qq_ref.shape[0]
    cells = k_ref.shape[0]
    own = ko_ref.shape[0]
    scaled = stacked(qq_ref[...] * 0.125)
    bias = bias_ref[...]
    self_score = dot_nt(ko_ref[...], scaled) + jnp.concatenate([bias, bias], 1)
    top = jnp.max(self_score, 0, keepdims=True)
    block = row_block(cells)
    blocks = [slice(i * block, (i + 1) * block) for i in range(cells // block)]
    for at in blocks:
        score = dot_nt(k_ref[at, :], scaled)
        s_ref[at, :] = score
        top = jnp.maximum(top, jnp.max(score, 0, keepdims=True))
    prob = jnp.exp(self_score - top)
    total = jnp.sum(prob, 0, keepdims=True)
    mixed = dot_nn(vo_ref[...].T, prob.astype(bf16))
    for at in blocks:
        prob = jnp.exp(s_ref[at, :] - top)
        total = total + jnp.sum(prob, 0, keepdims=True)
        mixed = mixed + dot_nn(v_ref[at, :].T, prob.astype(bf16))
    out_ref[...] = unstacked(mixed * (1.0 / total)).astype(bf16)
    lse_ref[...] = top + jnp.log(total)


def query_forward(query_qkv, own_qkv, vis_qkv, self_bias):
    cells = vis_qkv.shape[0]
    queries = query_qkv.shape[0]
    own = own_qkv.shape[0]
    width = query_qkv.shape[1] // 3
    pairs = width // PAIR
    keys = cells + own

    def part(rows, j):
        return pl.BlockSpec((rows, PAIR), lambda p, j=j: (0, j * pairs + p))

    return pl.pallas_call(
        query_forward_kernel,
        grid=(pairs,),
        in_specs=[
            part(queries, 0),
            part(cells, 1),
            part(cells, 2),
            part(own, 1),
            part(own, 2),
            whole(self_bias.shape),
        ],
        out_specs=[part(queries, 0), pl.BlockSpec((None, 1, 2 * queries), lambda p: (p, 0, 0))],
        out_shape=[
            jax.ShapeDtypeStruct((queries, width), bf16),
            jax.ShapeDtypeStruct((pairs, 1, 2 * queries), f32),
        ],
        scratch_shapes=[pltpu.VMEM((cells, 2 * queries), f32)],
        compiler_params=params(),
        cost_estimate=cost(
            4 * 2 * queries * keys * width, 4 * cells * width, 2 * queries * keys * pairs
        ),
        name="query_forward",
    )(query_qkv, vis_qkv, vis_qkv, own_qkv, own_qkv, self_bias)


def window_forward_kernel(
    windows,
    q_ref,
    k_ref,
    v_ref,
    kq_ref,
    vq_ref,
    row_ref,
    col_ref,
    open_ref,
    out_ref,
    lse_ref,
    scaled_ref,
    near_ref,
    mixed_ref,
    far_ref,
):
    cells = [slice(w * CELLS, (w + 1) * CELLS) for w in range(windows)]
    lanes = [slice(2 * w * CELLS, 2 * (w + 1) * CELLS) for w in range(windows)]
    tops = []
    for w in range(windows):
        scaled = stacked(q_ref[cells[w], :] * 0.125)
        scaled_ref[lanes[w], :] = scaled
        near = dot_nt(k_ref[cells[w], :], scaled)
        near = jnp.where(col_ref[w] == row_ref[w], near, MASKED)
        near_ref[w] = near
        tops.append(jnp.max(near, 0, keepdims=True))
    far = dot_nt(kq_ref[...], scaled_ref[...]) + open_ref[...]
    top = jnp.maximum(jnp.concatenate(tops, 1), jnp.max(far, 0, keepdims=True))
    far = jnp.exp(far - top)
    total = jnp.sum(far, 0, keepdims=True)
    far_mixed = dot_nn(vq_ref[...].T, far.astype(bf16))
    totals = []
    for w in range(windows):
        near = jnp.exp(near_ref[w] - top[:, lanes[w]])
        totals.append(jnp.sum(near, 0, keepdims=True))
        mixed_ref[w] = dot_nn(v_ref[cells[w], :].T, near.astype(bf16))
    total = total + jnp.concatenate(totals, 1)
    share = 1.0 / total
    lse_ref[...] = top + jnp.log(total)
    far_ref[...] = far_mixed
    for w in range(windows):
        turned = (mixed_ref[w] + far_ref[:, lanes[w]]) * share[:, lanes[w]]
        out_ref[cells[w], :] = joined(turned.astype(bf16).T)


def window_forward(vis_qkv, query_qkv, region_row, region_col, closed):
    cells = vis_qkv.shape[0]
    queries = query_qkv.shape[0]
    width = vis_qkv.shape[1] // 3
    pairs = width // PAIR
    windows = cells // CELLS

    def part(rows, j):
        return pl.BlockSpec((rows, PAIR), lambda p, j=j: (0, j * pairs + p))

    return pl.pallas_call(
        functools.partial(window_forward_kernel, windows),
        grid=(pairs,),
        in_specs=[
            part(cells, 0),
            part(cells, 1),
            part(cells, 2),
            part(queries, 1),
            part(queries, 2),
            whole(region_row.shape),
            whole(region_col.shape),
            whole(closed.shape),
        ],
        out_specs=[
            part(cells, 0),
            pl.BlockSpec((None, 1, 2 * cells), lambda p: (p, 0, 0)),
        ],
        out_shape=[
            jax.ShapeDtypeStruct((cells, width), bf16),
            jax.ShapeDtypeStruct((pairs, 1, 2 * cells), f32),
        ],
        scratch_shapes=[
            pltpu.VMEM((2 * cells, PAIR), bf16),
            pltpu.VMEM((windows, CELLS, 2 * CELLS), f32),
            pltpu.VMEM((windows, PAIR, 2 * CELLS), f32),
            pltpu.VMEM((PAIR, 2 * cells), f32),
        ],
        compiler_params=params(),
        cost_estimate=cost(
            8 * cells * (CELLS + queries) * width,
            8 * cells * width,
            2 * pairs * cells * (CELLS + queries),
        ),
        name="window_forward",
    )(vis_qkv, vis_qkv, vis_qkv, query_qkv, query_qkv, region_row, region_col, closed)


def attention_backward_kernel(
    windows,
    q_ref,
    k_ref,
    v_ref,
    do_ref,
    qq_ref,
    kq_ref,
    vq_ref,
    doq_ref,
    ko_ref,
    vo_ref,
    row_ref,
    col_ref,
    open_ref,
    bias_ref,
    lse_ref,
    lseq_ref,
    mixq_ref,
    *rest,
):
    if len(rest) > 15:
        rest = rest[3:]
    attention_backward_body(
        windows,
        q_ref,
        k_ref,
        v_ref,
        do_ref,
        qq_ref,
        kq_ref,
        vq_ref,
        doq_ref,
        ko_ref,
        vo_ref,
        row_ref,
        col_ref,
        open_ref,
        bias_ref,
        lse_ref,
        lseq_ref,
        mixq_ref,
        *rest,
    )


def attention_backward_body(
    windows,
    q_ref,
    k_ref,
    v_ref,
    do_ref,
    qq_ref,
    kq_ref,
    vq_ref,
    doq_ref,
    ko_ref,
    vo_ref,
    row_ref,
    col_ref,
    open_ref,
    bias_ref,
    lse_ref,
    lseq_ref,
    mixq_ref,
    dq_ref,
    dk_ref,
    dv_ref,
    dqq_ref,
    dkq_ref,
    dvq_ref,
    dko_ref,
    dvo_ref,
    scaled_ref,
    grad_ref,
    near_ref,
    neart_ref,
    seenk_ref,
    seenv_ref,
    far_ref,
):
    cells = [slice(w * CELLS, (w + 1) * CELLS) for w in range(windows)]
    lanes = [slice(2 * w * CELLS, 2 * (w + 1) * CELLS) for w in range(windows)]
    lse = lse_ref[...]

    deltas = []
    for w in range(windows):
        scaled = stacked(q_ref[cells[w], :] * 0.125)
        grad = stacked(do_ref[cells[w], :])
        scaled_ref[lanes[w], :] = scaled
        grad_ref[lanes[w], :] = grad
        near = dot_nt(k_ref[cells[w], :], scaled)
        near = jnp.exp(jnp.where(col_ref[w] == row_ref[w], near, MASKED) - lse[:, lanes[w]])
        near_t = near * dot_nt(v_ref[cells[w], :], grad)
        near_ref[w] = near
        neart_ref[w] = near_t
        deltas.append(jnp.sum(near_t, 0, keepdims=True))
    kq = kq_ref[...]
    far = jnp.exp(dot_nt(kq, scaled_ref[...]) + open_ref[...] - lse)
    far_t = far * dot_nt(vq_ref[...], grad_ref[...])
    delta = jnp.concatenate(deltas, 1) + jnp.sum(far_t, 0, keepdims=True)
    far_d = (far_t - far * delta).astype(bf16)
    dkq_ref[...] = dot_nn(far_d, scaled_ref[...]).astype(bf16)
    dvq_ref[...] = dot_nn(far.astype(bf16), grad_ref[...]).astype(bf16)
    far_ref[...] = dot_nn(kq.T, far_d).T

    scaled_q = stacked(qq_ref[...] * 0.125)
    grad_q = stacked(doq_ref[...])
    lse_q = lseq_ref[...]
    mix_q = mixq_ref[...]
    delta_q = row_sums(grad_q.astype(f32) * jnp.concatenate([mix_q, mix_q], 0))
    bias = bias_ref[...]
    prob = jnp.exp(dot_nt(ko_ref[...], scaled_q) + jnp.concatenate([bias, bias], 1) - lse_q)
    dscore = (prob * (dot_nt(vo_ref[...], grad_q) - delta_q)).astype(bf16)
    dko_ref[...] = dot_nn(dscore, scaled_q)
    dvo_ref[...] = dot_nn(prob.astype(bf16), grad_q)
    turned = dot_nn(ko_ref[...].T, dscore)
    rows = k_ref.shape[0]
    block = row_block(rows)
    for i in range(rows // block):
        at = slice(i * block, (i + 1) * block)
        k_rows = k_ref[at, :]
        prob = jnp.exp(dot_nt(k_rows, scaled_q) - lse_q)
        dscore = (prob * (dot_nt(v_ref[at, :], grad_q) - delta_q)).astype(bf16)
        seenk_ref[at, :] = dot_nn(dscore, scaled_q)
        seenv_ref[at, :] = dot_nn(prob.astype(bf16), grad_q)
        turned = turned + dot_nn(k_rows.T, dscore)
    dqq_ref[...] = (unstacked(turned) * 0.125).astype(bf16)

    for w in range(windows):
        near = near_ref[w]
        near_d = (neart_ref[w] - near * delta[:, lanes[w]]).astype(bf16)
        upright = dot_nn(k_ref[cells[w], :].T, near_d).T + far_ref[lanes[w], :]
        dq_ref[cells[w], :] = (joined(upright) * 0.125).astype(bf16)
        dk_ref[cells[w], :] = (
            dot_nn(near_d, scaled_ref[lanes[w], :]) + seenk_ref[cells[w], :]
        ).astype(bf16)
        dv_ref[cells[w], :] = (
            dot_nn(near.astype(bf16), grad_ref[lanes[w], :]) + seenv_ref[cells[w], :]
        ).astype(bf16)


def attention_backward(
    vis_qkv,
    query_qkv,
    own_qkv,
    grad,
    grad_q,
    region_row,
    region_col,
    closed,
    self_bias,
    lse,
    lse_q,
    mix_q,
    first,
    count,
    begun=(),
):
    cells = vis_qkv.shape[0]
    queries = query_qkv.shape[0]
    own = own_qkv.shape[0]
    width = vis_qkv.shape[1] // 3
    pairs = width // PAIR
    windows = cells // CELLS

    def part(rows, j):
        return pl.BlockSpec((rows, PAIR), lambda p, j=j: (0, j * pairs + first + p))

    def result(rows):
        return pl.BlockSpec((rows, PAIR), lambda p: (0, p))

    def filled(rows):
        return pl.BlockSpec((rows, PAIR), lambda p: (0, first + p))

    def stats(array):
        return pl.BlockSpec((None,) + array.shape[1:], lambda p: (first + p, 0, 0))

    span = count * PAIR
    return pl.pallas_call(
        functools.partial(attention_backward_kernel, windows),
        grid=(count,),
        in_specs=[
            part(cells, 0),
            part(cells, 1),
            part(cells, 2),
            part(cells, 0),
            part(queries, 0),
            part(queries, 1),
            part(queries, 2),
            part(queries, 0),
            part(own, 1),
            part(own, 2),
            whole(region_row.shape),
            whole(region_col.shape),
            whole(closed.shape),
            whole(self_bias.shape),
            stats(lse),
            stats(lse_q),
            part(queries, 0),
        ]
        + [pl.BlockSpec(memory_space=pl.ANY)] * len(begun),
        out_specs=[filled(cells)] * 3 + [result(queries)] * 3 + [result(own)] * 2,
        out_shape=[jax.ShapeDtypeStruct((cells, width), bf16)] * 3
        + [jax.ShapeDtypeStruct((queries, span), bf16)] * 3
        + [jax.ShapeDtypeStruct((own, span), f32)] * 2,
        scratch_shapes=[
            pltpu.VMEM((2 * cells, PAIR), bf16),
            pltpu.VMEM((2 * cells, PAIR), bf16),
            pltpu.VMEM((windows, CELLS, 2 * CELLS), f32),
            pltpu.VMEM((windows, CELLS, 2 * CELLS), f32),
            pltpu.VMEM((cells, PAIR), f32),
            pltpu.VMEM((cells, PAIR), f32),
            pltpu.VMEM((2 * cells, PAIR), f32),
        ],
        compiler_params=params(),
        cost_estimate=cost(
            20 * cells * (CELLS + 2 * queries) * span,
            14 * cells * span,
            2 * count * cells * (CELLS + 2 * queries),
        ),
        input_output_aliases={17 + i: i for i in range(len(begun))},
        name="attention_backward",
    )(
        vis_qkv,
        vis_qkv,
        vis_qkv,
        grad,
        query_qkv,
        query_qkv,
        query_qkv,
        grad_q,
        own_qkv,
        own_qkv,
        region_row,
        region_col,
        closed,
        self_bias,
        lse,
        lse_q,
        mix_q,
        *begun,
    )


def gelu_pair(z):
    below = 0.5 + 0.5 * lax.erf(z * 0.7071067811865476)
    bell = jnp.exp(-0.5 * z * z)
    return z * below, below + z * bell * 0.3989422804014327


def ffn_forward_kernel(
    stream,
    x_ref,
    o_ref,
    wo_ref,
    bo_ref,
    gain_ref,
    bias_ref,
    wu_ref,
    bu_ref,
    wd_ref,
    bd_ref,
    x1_ref,
    b_ref,
    hid_ref,
    slope_ref,
    out_ref,
    sum_ref,
):
    rows, width = x_ref.shape
    block = row_block(rows)
    count = rows // block
    ats = [slice(i * block, (i + 1) * block) for i in range(count)]
    step = pl.program_id(0)
    row = slice(stream, stream + 1)

    @pl.when(step == 0)
    def _():
        for at in ats:
            x1 = x_ref[at, :].astype(f32) + dot_nn(o_ref[at, :], wo_ref[...]) + bo_ref[row, :]
            x1_ref[at, :] = x1
            hat, _ = normalised(x1)
            b_ref[at, :] = (hat * gain_ref[row, :] + bias_ref[row, :]).astype(bf16)
            sum_ref[at, :] = x1 + bd_ref[row, :]

    def project(i):
        return dot_nn(b_ref[ats[i], :], wu_ref[...]) + bu_ref[row, :]

    z = project(0)
    for i in range(count):
        ahead = project(i + 1) if i + 1 < count else None
        hidden, slope = gelu_pair(z)
        hidden = hidden.astype(bf16)
        hid_ref[ats[i], :] = hidden
        slope_ref[ats[i], :] = slope.astype(bf16)
        sum_ref[ats[i], :] += dot_nn(hidden, wd_ref[...])
        z = ahead

    @pl.when(step == pl.num_programs(0) - 1)
    def _():
        out_ref[...] = sum_ref[...].astype(bf16)


def ffn_forward(x, attended, out_w, out_b, gain, bias, up_w, up_b, down_w, down_b, stream):
    rows, width = x.shape
    hidden = up_w.shape[-1]
    chunk = 768
    return pl.pallas_call(
        functools.partial(ffn_forward_kernel, stream),
        grid=(hidden // chunk,),
        in_specs=[
            whole((rows, width)),
            whole((rows, width)),
            pl.BlockSpec((None, width, width), lambda f: (stream, 0, 0)),
            whole(out_b.shape),
            whole(gain.shape),
            whole(bias.shape),
            pl.BlockSpec((None, width, chunk), lambda f: (stream, 0, f)),
            pl.BlockSpec((2, chunk), lambda f: (0, f)),
            pl.BlockSpec((None, chunk, width), lambda f: (stream, f, 0)),
            whole(down_b.shape),
        ],
        out_specs=[
            whole((rows, width)),
            whole((rows, width)),
            pl.BlockSpec((rows, chunk), lambda f: (0, f)),
            pl.BlockSpec((rows, chunk), lambda f: (0, f)),
            whole((rows, width)),
        ],
        out_shape=[
            jax.ShapeDtypeStruct((rows, width), f32),
            jax.ShapeDtypeStruct((rows, width), bf16),
            jax.ShapeDtypeStruct((rows, hidden), bf16),
            jax.ShapeDtypeStruct((rows, hidden), bf16),
            jax.ShapeDtypeStruct((rows, width), bf16),
        ],
        scratch_shapes=[pltpu.VMEM((rows, width), f32)],
        compiler_params=params(),
        cost_estimate=cost(
            2 * rows * width * (2 * hidden + width),
            4 * width * hidden + 4 * rows * hidden + 12 * rows * width,
            2 * rows * hidden,
        ),
        name="ffn_forward",
    )(x, attended, out_w, out_b, gain, bias, up_w, up_b, down_w, down_b)


def ffn_backward_kernel(
    stream,
    g_ref,
    slope_ref,
    x1_ref,
    wd_ref,
    wu_ref,
    wo_ref,
    gain_ref,
    dz_ref,
    dx1_ref,
    du_ref,
    do_ref,
    sums_ref,
    sum_ref,
):
    rows, width = g_ref.shape
    block = row_block(rows)
    count = rows // block
    ats = [slice(i * block, (i + 1) * block) for i in range(count)]
    step = pl.program_id(0)
    row = slice(stream, stream + 1)

    @pl.when(step == 0)
    def _():
        sum_ref[...] = jnp.zeros_like(sum_ref)

    up_bias = jnp.zeros((1, dz_ref.shape[1]), f32)

    def pulled(i):
        return dot_nt(g_ref[ats[i], :], wd_ref[...])

    grad = pulled(0)
    for i in range(count):
        ahead = pulled(i + 1) if i + 1 < count else None
        dz = grad * slope_ref[ats[i], :].astype(f32)
        low = dz.astype(bf16)
        dz_ref[ats[i], :] = low
        up_bias = up_bias + jnp.sum(dz, 0, keepdims=True)
        sum_ref[ats[i], :] += dot_nt(low, wu_ref[...])
        grad = ahead
    sums_ref[pl.ds(4 + step, 1), :] = up_bias

    @pl.when(step == pl.num_programs(0) - 1)
    def _():
        sums_ref[0:4, :] = jnp.zeros((4, width), f32)
        for at in ats:
            hat, rstd = normalised(x1_ref[at, :])
            db = sum_ref[at, :]
            g = g_ref[at, :].astype(f32)
            dx1 = g + norm_back(db, hat, rstd, gain_ref[row, :])
            dx1_ref[at, :] = dx1
            du = dx1.astype(bf16)
            du_ref[at, :] = du
            do_ref[at, :] = dot_nt(du, wo_ref[...]).astype(bf16)
            sums_ref[0:1, :] += jnp.sum(db * hat, 0, keepdims=True)
            sums_ref[1:2, :] += jnp.sum(db, 0, keepdims=True)
            sums_ref[2:3, :] += jnp.sum(dx1, 0, keepdims=True)
            sums_ref[3:4, :] += jnp.sum(g, 0, keepdims=True)


def ffn_backward(g, slope, x1, down_w, up_w, out_w, gain, stream):
    rows, width = g.shape
    hidden = up_w.shape[-1]
    chunk = width
    return pl.pallas_call(
        functools.partial(ffn_backward_kernel, stream),
        grid=(hidden // chunk,),
        in_specs=[
            whole((rows, width)),
            pl.BlockSpec((rows, chunk), lambda f: (0, f)),
            whole((rows, width)),
            pl.BlockSpec((None, chunk, width), lambda f: (stream, f, 0)),
            pl.BlockSpec((None, width, chunk), lambda f: (stream, 0, f)),
            pl.BlockSpec((None, width, width), lambda f: (stream, 0, 0)),
            whole(gain.shape),
        ],
        out_specs=[
            pl.BlockSpec((rows, chunk), lambda f: (0, f)),
            whole((rows, width)),
            whole((rows, width)),
            whole((rows, width)),
            whole((4 + hidden // chunk, width)),
        ],
        out_shape=[
            jax.ShapeDtypeStruct((rows, hidden), bf16),
            jax.ShapeDtypeStruct((rows, width), f32),
            jax.ShapeDtypeStruct((rows, width), bf16),
            jax.ShapeDtypeStruct((rows, width), bf16),
            jax.ShapeDtypeStruct((4 + hidden // chunk, width), f32),
        ],
        scratch_shapes=[pltpu.VMEM((rows, width), f32)],
        compiler_params=params(),
        cost_estimate=cost(
            2 * rows * width * (2 * hidden + width),
            4 * width * hidden + 4 * rows * hidden + 14 * rows * width,
        ),
        name="ffn_backward",
    )(g, slope, x1, down_w, up_w, out_w, gain)


def input_kernel(stream, dq_ref, dk_ref, dv_ref, w_ref, x_ref, dx1_ref, gain_ref, out_ref, sums_ref):
    width = x_ref.shape[1]

    @pl.when(pl.program_id(0) == 0)
    def _():
        sums_ref[...] = jnp.zeros_like(sums_ref)

    grad = dot_nt(dq_ref[...], w_ref[:, :width])
    grad = grad + dot_nt(dk_ref[...], w_ref[:, width : 2 * width])
    grad = grad + dot_nt(dv_ref[...], w_ref[:, 2 * width :])
    hat, rstd = normalised(x_ref[...].astype(f32))
    out_ref[...] = (
        dx1_ref[...] + norm_back(grad, hat, rstd, gain_ref[stream : stream + 1, :])
    ).astype(bf16)
    sums_ref[0:1, :] += jnp.sum(grad * hat, 0, keepdims=True)
    sums_ref[1:2, :] += jnp.sum(grad, 0, keepdims=True)


def input_grad(dq, dk, dv, weight, x, dx1, gain, stream):
    rows, width = x.shape
    block = row_block(rows)
    rows_spec = pl.BlockSpec((block, width), lambda i: (i, 0))
    return pl.pallas_call(
        functools.partial(input_kernel, stream),
        grid=(rows // block,),
        in_specs=[rows_spec] * 3
        + [
            pl.BlockSpec((None, width, 3 * width), lambda i: (stream, 0, 0)),
            rows_spec,
            rows_spec,
            whole(gain.shape),
        ],
        out_specs=[rows_spec, whole((8, width))],
        out_shape=[
            jax.ShapeDtypeStruct((rows, width), bf16),
            jax.ShapeDtypeStruct((8, width), f32),
        ],
        compiler_params=params(),
        cost_estimate=cost(6 * rows * width * width, 14 * rows * width + 6 * width * width),
        name="input_grad",
    )(dq, dk, dv, weight, x, dx1, gain)


def after(value, *before):
    return lax.optimization_barrier((value,) + before)[0]


def beside(made, *flights):
    return lax.optimization_barrier((made,) + flights)


def moved(block, axis, step):
    size = lax.axis_size(axis)
    return lax.ppermute(block, axis, [(i, (i + step) % size) for i in range(size)])


def swapped(block, axis, mask):
    size = lax.axis_size(axis)
    return lax.ppermute(block, axis, [(i, i ^ mask) for i in range(size)])


def other_core(block):
    return swapped(block, "strip", 1)


def place():
    strip = lax.axis_index("strip")
    return lax.axis_size("strip") // 2, strip // 2, strip % 2


def pick(block, index, axis=0):
    return lax.dynamic_index_in_dim(block, index, axis, keepdims=False)


def added(blocks, kind=bf16):
    total = blocks[0].astype(f32)
    for block in blocks[1:]:
        total = total + block.astype(f32)
    return total.astype(kind)


def bit_of(axis, mask):
    return (lax.axis_index(axis) // mask) % 2


class Phase:
    def __init__(self, blocks, dims, axis, mask):
        bit = bit_of(axis, mask)
        self.mine = [[pick(term, bit, dim) for term in terms] for terms, dim in zip(blocks, dims)]
        theirs = [
            added([pick(term, 1 - bit, dim) for term in terms]) for terms, dim in zip(blocks, dims)
        ]
        self.shapes = [block.shape for block in theirs]
        self.sent, self.got = exchange(theirs, axis, mask)

    def terms(self):
        got = parted(self.got, self.shapes)
        return [[added(mine + [more])] for mine, more in zip(self.mine, got)]


def mapped(change, terms):
    return [change(term) for term in terms]


class Gather:
    def __init__(self, blocks, dims, axis, mask):
        self.bit = bit_of(axis, mask)
        self.blocks, self.dims = blocks, dims
        self.shapes = [block.shape for block in blocks]
        self.sent, self.got = exchange(blocks, axis, mask)

    def pairs(self):
        first = self.bit == 0
        return [
            jnp.stack([jnp.where(first, one, two), jnp.where(first, two, one)], dim)
            for one, two, dim in zip(self.blocks, parted(self.got, self.shapes), self.dims)
        ]


def parted(rows, shapes):
    if len(shapes) == 1:
        return [rows]
    blocks, at = [], 0
    for shape in shapes:
        count = 1
        for size in shape[:-1]:
            count *= size
        blocks.append(rows[at : at + count].reshape(shape))
        at += count
    return blocks


def exchange(blocks, axis, mask):
    if len(blocks) == 1:
        sent = blocks[0]
    else:
        sent = jnp.concatenate([block.reshape(-1, block.shape[-1]) for block in blocks], 0)
    return sent, swapped(sent, axis, mask)


def by_core(grad):
    strips = lax.axis_size("strip")
    return grad.reshape(strips // 2, 2, grad.shape[0] // strips, grad.shape[1])


def tiled(grad, width):
    count = grad.shape[-1] // width
    return jnp.stack([grad[..., i * width : (i + 1) * width] for i in range(count)], -3)


def untiled(blocks):
    return jnp.concatenate([blocks[i] for i in range(blocks.shape[0])], -1)


def by_page(blocks):
    rows = blocks.shape[-2]
    return blocks.reshape(blocks.shape[:-2] + (2, 2, rows // 4, blocks.shape[-1]))


def from_page(blocks):
    return blocks.reshape(blocks.shape[:-4] + (-1, blocks.shape[-1]))


def by_chip(blocks):
    return blocks.reshape((blocks.shape[0] // 2, 2) + blocks.shape[1:])


def line_masks():
    size, _, _ = place()
    return [2 << i for i in range(size.bit_length() - 1)]


def line_phase(blocks, mask):
    return Phase([mapped(by_chip, terms) for terms in blocks], [1] * len(blocks), "strip", mask)


def line_first(blocks):
    masks = line_masks()
    for mask in masks[:-2]:
        blocks = line_phase(blocks, mask).terms()
    return line_phase(blocks, masks[-2])


def line_last(blocks):
    return line_phase(blocks, line_masks()[-1])


def line_exchange(block):
    size, z, _ = place()
    return [pick(block, z)] + [
        moved(pick(block, (z + step) % size), "strip", 2 * step) for step in range(1, size)
    ]


def line_gather(block):
    size, _, _ = place()
    return [block] + [moved(block, "strip", 2 * step) for step in range(1, size)]


def line_order(blocks):
    size, z, _ = place()
    double = jnp.stack(blocks[:1] + blocks[:0:-1] + blocks[:1] + blocks[:0:-1])
    return lax.dynamic_slice_in_dim(double, (size - z) % size, size, 0)


def page_exchange(block):
    size = lax.axis_size("page")
    page = lax.axis_index("page")
    shares = block.reshape(size, block.shape[0] // size, block.shape[1])
    return [pick(shares, page)] + [
        swapped(pick(shares, page ^ mask), "page", mask) for mask in range(1, size)
    ]


def page_gather(block):
    size = lax.axis_size("page")
    return [block] + [swapped(block, "page", mask) for mask in range(1, size)]


def page_order(blocks):
    size = len(blocks)
    page = lax.axis_index("page")
    rows, columns = blocks[0].shape
    joined = jnp.zeros((size * rows, columns), f32)
    for mask, block in enumerate(blocks):
        joined = lax.dynamic_update_slice_in_dim(
            joined, block.astype(f32), (page ^ mask) * rows, 0
        )
    return joined


def core_order(mine, other):
    _, _, core = place()
    pair = jnp.stack(
        [jnp.where(core == 0, mine, other), jnp.where(core == 0, other, mine)], 1
    )
    return pair.reshape(-1, pair.shape[-1])


def packed(mix, lse):
    rows = mix.shape[0]
    pairs = lse.shape[0]
    stats = lse.reshape(pairs, 2, rows).transpose(2, 0, 1).reshape(rows, 2 * pairs)
    stats = jnp.pad(stats, ((0, 0), (0, PAIR - 2 * pairs)))
    return jnp.concatenate([mix.astype(f32), stats], 1)


def merged(blocks):
    width = blocks[0].shape[-1] - PAIR
    lead = blocks[0].shape[:-1]
    tops = [block[..., width : width + HEADS] for block in blocks]
    top = functools.reduce(jnp.maximum, tops)
    shares = [jnp.exp(each - top) for each in tops]
    total = functools.reduce(jnp.add, shares)
    mix = 0.0
    for block, share in zip(blocks, shares):
        heads = block[..., :width].reshape(lead + (HEADS, width // HEADS))
        mix = mix + heads * (share / total)[..., None]
    stats = jnp.pad(top + jnp.log(total), [(0, 0)] * len(lead) + [(0, PAIR - HEADS)])
    return jnp.concatenate([mix.reshape(lead + (width,)), stats], -1)


def region_windows(rows):
    across = rows.shape[1] // WIN
    rolled = jnp.roll(rows, -SHIFT, axis=1)
    return rolled.reshape(WIN, across, WIN).transpose(1, 0, 2).reshape(across, CELLS)


def weight_grad(left, right):
    return dot_tn(left, right).astype(bf16)


def body(
    vis_tokens,
    query_tokens,
    region_ids,
    query_mask,
    answer_len,
    norm1_gain,
    norm1_bias,
    qkv_weight,
    out_weight,
    out_bias,
    norm2_gain,
    norm2_bias,
    up_weight,
    up_bias,
    down_weight,
    down_bias,
    vis_cotangent,
    query_cotangent,
):
    strips = lax.axis_size("strip")
    strip = lax.axis_index("strip")
    chips, z, core = place()
    local_rows, columns, features = vis_tokens.shape[1:]
    own_count = query_tokens.shape[1]
    query_count = query_mask.shape[1]
    total_rows = region_ids.shape[1]
    own_start = strip * own_count

    def own_rows(values):
        return lax.dynamic_slice_in_dim(values, own_start, own_count, 0)

    def own_columns(values):
        span = values.shape[1] // strips
        return lax.dynamic_slice_in_dim(values, strip * span, span, 1)

    tokens = line_gather(query_tokens[0])
    head_rows = moved(vis_tokens[0, :SHIFT], "strip", -1)
    tokens = line_order(tokens)
    query = core_order(tokens, other_core(tokens))

    key_open = query_mask[0] > 0
    key_ids = jnp.arange(query_count, dtype=jnp.int32)
    prompt = key_ids < query_count - answer_len[0]
    closed = jnp.where(key_open & prompt, 0.0, MASKED).astype(f32)[:, None]
    own_ids = own_start + jnp.arange(own_count, dtype=jnp.int32)
    allowed = own_rows(key_open)[:, None] & (
        own_rows(prompt)[:, None] | (own_ids[:, None] <= key_ids[None, :])
    )
    self_bias = jnp.where(allowed, 0.0, MASKED).astype(f32)
    row_ids = (strip * local_rows + SHIFT + jnp.arange(local_rows, dtype=jnp.int32)) % total_rows
    region = region_windows(jnp.take(region_ids[0], row_ids, axis=0))
    region_row = jnp.concatenate([region, region], 1)[:, None, :]
    region_col = region[:, :, None]

    query_norm, query_qkv = norm_qkv(query, norm1_gain, norm1_bias, qkv_weight, 1)
    (query_norm, query_qkv), head_rows = beside((query_norm, query_qkv), head_rows)
    own_qkv = own_rows(query_qkv)
    vis = enter(vis_tokens[0], head_rows)
    head_cot = moved(after(vis_cotangent[0, :SHIFT], vis), "strip", -1)
    vis_norm, vis_qkv = norm_qkv(vis, norm1_gain, norm1_bias, qkv_weight, 0)
    (vis_norm, vis_qkv), head_cot = beside((vis_norm, vis_qkv), head_cot)

    part = by_core(packed(*query_forward(query_qkv, own_qkv, vis_qkv, self_bias)))
    mine, theirs = pick(part, core, 1), pick(part, 1 - core, 1)
    others = other_core(theirs)
    vis_cot = enter(after(vis_cotangent[0], theirs), head_cot)
    vis_cot, mine, others = beside(vis_cot, mine, others)
    part = merged([mine, others])
    others = swapped(part, "strip", 2)

    vis_windows = window_forward(after(vis_qkv, part), query_qkv, region_row, region_col, closed)
    (vis_attn, vis_lse), part, others = beside(vis_windows, part, others)
    part = merged([part, others])
    mask = 4
    while 2 * mask < strips:
        part = merged([part, swapped(part, "strip", mask)])
        mask = 2 * mask
    others = swapped(part, "strip", mask)
    cotangents = line_gather(after(query_cotangent[0], vis_attn))

    weights = (out_weight, out_bias, norm2_gain, norm2_bias, up_weight, up_bias, down_weight, down_bias)
    made = ffn_forward(vis, after(vis_attn, part), *weights, 0)
    made, part, others, cotangents = beside(made, part, others, cotangents)
    vis_x1, vis_b, vis_hid, vis_slope, vis_result = made
    part = merged([part, others])
    others = other_core(part)
    cotangents = line_order(cotangents)
    cot_others = other_core(cotangents)
    vis_down = weight_grad(after(vis_hid, part, cotangents), vis_cot)
    vis_down, part, others, cotangents, cot_others = beside(
        vis_down, part, others, cotangents, cot_others
    )
    down = by_core(vis_down)
    down = Phase([[down.reshape(chips, 2, -1, features // strips, features)]], [1], "strip", 1)

    made = ffn_backward(
        after(vis_cot, down.sent), vis_slope, vis_x1, down_weight, up_weight, out_weight, norm2_gain, 0
    )
    made, down.got = beside(made, down.got)
    vis_dz, vis_dx1, vis_du, vis_do, vis_sums = made
    (down,) = down.terms()
    down = Phase([mapped(by_page, down)], [3], "page", 1)
    vis_up = weight_grad(after(vis_b, down.sent), vis_dz)
    vis_outg = weight_grad(vis_attn, vis_du)
    up = jnp.concatenate(
        [tiled(by_core(vis_up), features), tiled(by_core(vis_outg), features)], 2
    )
    up = Phase([[up]], [1], "strip", 1)
    made = leave(after(vis_result, up.sent), columns)
    (vis_keep, vis_send), up.got = beside(made, up.got)
    vis_first = moved(vis_send, "strip", 1)
    (up,) = up.terms()
    up_a = line_first([mapped(lambda term: term[:, :3], up)])

    every = core_order(part, others)
    query_cot = core_order(cotangents, cot_others)
    query_mix = every[:, :features]
    stats = every[:, features : features + HEADS]
    query_lse = stats.T.reshape(HEADS // 2, 1, 2 * query_count)
    query_attn = query_mix.astype(bf16)
    made = ffn_forward(query, after(query_attn, up_a.sent), *weights, 1)
    made, down.got = beside(made, down.got)
    query_x1, query_b, query_hid, query_slope, query_result = made
    (down,) = down.terms()
    up_b = Phase([mapped(lambda term: by_page(term[:, 3:]), up)], [3], "page", 1)
    made = ffn_backward(
        query_cot,
        after(query_slope, up_b.sent),
        query_x1,
        down_weight,
        up_weight,
        out_weight,
        norm2_gain,
        1,
    )
    made, up_a.got, up_b.got, vis_first = beside(made, up_a.got, up_b.got, vis_first)
    query_dz, query_dx1, query_du, query_do, query_sums = made
    (up_a,) = up_a.terms()
    (up_b,) = up_b.terms()
    up_a = Phase([mapped(by_page, up_a)], [3], "page", 1)
    low = Phase([down, up_b], [2, 2], "page", 2)

    def query_grads(left, right):
        return weight_grad(own_columns(left), right)

    up_rows = features // strips
    one = jnp.concatenate(
        [
            tiled(query_grads(query_b, after(query_dz, up_a.sent, low.sent)), features),
            query_grads(query_attn, query_du)[None],
            query_grads(query_hid, query_cot).reshape(-1, up_rows, features),
        ],
        0,
    )
    one = Phase([[by_page(one)]], [2], "page", 1)

    pairs = HEADS // 2
    half = pairs // 2

    def backward(values, first, begun=()):
        return attention_backward(
            values,
            query_qkv,
            own_qkv,
            vis_do,
            query_do,
            region_row,
            region_col,
            closed,
            self_bias,
            vis_lse,
            query_lse,
            query_mix,
            first,
            half,
            begun,
        )

    def head_grads(normed, grads, first):
        span = half * PAIR
        return jnp.stack(
            [
                by_core(weight_grad(normed, each[:, first * PAIR : first * PAIR + span]))
                for each in grads
            ],
            2,
        )

    back_one = backward(after(vis_qkv, one.sent), 0)
    back_one, up_a.got, low.got = beside(back_one, up_a.got, low.got)
    (up_a,) = up_a.terms()
    low = low.terms()
    up_a = Phase([up_a], [2], "page", 2)
    low = line_first(low)
    first = Phase(
        [[head_grads(after(vis_norm, up_a.sent, low.sent), back_one[:3], 0)]], [1], "strip", 1
    )
    first.sent, one.got = beside(first.sent, one.got)
    (one,) = one.terms()
    one = Phase([one], [1], "page", 2)

    back_two = backward(after(vis_qkv, first.sent, one.sent), half, back_one[:3])
    back_two, first.got, up_a.got, low.got, one.got = beside(
        back_two, first.got, up_a.got, low.got, one.got
    )
    (up_a,) = up_a.terms()
    low = low.terms()
    line = line_last([up_a] + low)
    (one,) = one.terms()
    one_gather = Gather([one[0]], [1], "page", 1)
    part = jnp.stack(
        [by_core(each) for pair in zip(back_one[3:6], back_two[3:6]) for each in pair], 2
    )
    part = Phase([[part]], [1], "strip", 1)
    second = Phase(
        [
            [
                head_grads(
                    after(vis_norm, part.sent, line.sent, one_gather.sent), back_two[:3], half
                )
            ]
        ],
        [1],
        "strip",
        1,
    )
    second.sent, part.got = beside(second.sent, part.got)
    (part,) = part.terms()
    part = line_first([part])
    (first,) = first.terms()
    first = Phase([mapped(by_page, after(first, part.sent))], [3], "page", 1)
    first.sent, second.got = beside(first.sent, second.got)
    (second,) = second.terms()

    made = input_grad(
        after(back_two[0], second, part.sent, first.sent),
        back_two[1],
        back_two[2],
        qkv_weight,
        vis,
        vis_dx1,
        norm1_gain,
        0,
    )
    made, first.got, part.got, line.got, one_gather.got = beside(
        made, first.got, part.got, line.got, one_gather.got
    )
    vis_input, vis_head = made
    (part,) = part.terms()
    part = line_last([part])
    second = Phase([mapped(by_page, after(second, part.sent))], [3], "page", 1)
    one_gather = Gather(one_gather.pairs(), [1], "page", 2)
    all_gather = Gather([terms[0][0] for terms in line.terms()], [1, 1, 1], "page", 1)
    made = leave(after(vis_input, part.sent, second.sent, all_gather.sent), columns)
    made, part.got = beside(made, part.got)
    grad_keep, grad_send = made
    (part,) = part.terms()
    own_self = [jnp.zeros_like(back_one[6])] * 2 + [back_one[6], back_two[6], back_one[7], back_two[7]]
    own_dqkv = added(mapped(lambda term: term[0], part) + [jnp.stack(own_self)])
    masks = line_masks()
    lined = own_dqkv[None]
    for mask in reversed(masks[1:-1]):
        lined = Gather([lined], [1], "strip", mask).pairs()[0]
        lined = lined.reshape((-1,) + own_dqkv.shape)
    lined = Gather([lined], [0], "strip", masks[-1])
    made = input_grad(
        untiled(after(own_dqkv, lined.sent)[0:2]),
        untiled(own_dqkv[2:4]),
        untiled(own_dqkv[4:6]),
        qkv_weight,
        query_tokens[0],
        own_rows(query_dx1),
        norm1_gain,
        1,
    )
    made, lined.got, second.got, all_gather.got = beside(
        made, lined.got, second.got, all_gather.got
    )
    own_input, own_head = made
    lined = lined.pairs()[0].reshape((-1,) + own_dqkv.shape)
    lined = Gather([lined], [1], "strip", masks[0])
    (first,) = first.terms()
    (second,) = second.terms()
    qkv = Phase([first, second], [2, 2], "page", 2)
    up_a, down, up_b = all_gather.pairs()
    up_gather = Gather([up_a, up_b], [1, 1], "page", 2)

    once = jnp.where(strip == 0, 1.0, 0.0)
    small = jnp.concatenate([vis_sums, vis_head, once * query_sums, own_head], 0)
    lined.got, small, one_gather.got = beside(lined.got, small, one_gather.got)
    lined = lined.pairs()[0].reshape((-1,) + own_dqkv.shape)
    lined_others = other_core(lined)
    small_others = other_core(small)
    lined_others, small_others, qkv.got = beside(lined_others, small_others, qkv.got)
    small = small + small_others
    query_dqkv = jnp.stack(
        [jnp.where(core == 0, lined, lined_others), jnp.where(core == 0, lined_others, lined)], 1
    )
    query_dqkv = [query_dqkv[:, :, i].reshape(query_count, -1) for i in range(6)]
    qkv = line_first(qkv.terms())
    three = query_grads(query_norm, jnp.concatenate(query_dqkv, 1))
    three = page_exchange(three)
    for mask in masks[:-2]:
        small = small + swapped(small, "strip", mask)
    small_others = swapped(small, "strip", masks[-2])
    three, qkv.got, small_others, up_gather.got = beside(
        three, qkv.got, small_others, up_gather.got
    )
    three = page_gather(added(three))
    qkv = line_last(qkv.terms())
    small = small + small_others
    small_others = swapped(small, "strip", masks[-1])
    down_gather = Gather([down], [1], "page", 2)
    three, qkv.got, small_others, down_gather.got = beside(
        three, qkv.got, small_others, down_gather.got
    )
    qkv = [terms[0][0] for terms in qkv.terms()]
    late = Gather(qkv, [1, 1], "page", 1)
    small = small + small_others
    small_others = swapped(small, "page", 1)
    grad_first = moved(after(grad_send, late.sent), "strip", 1)
    three = page_order(three)
    late.got, small_others = beside(late.got, small_others)
    late = Gather(late.pairs(), [1, 1], "page", 2)
    small = small + small_others
    small_others = swapped(small, "page", 2)
    small = small + small_others

    up_a, up_b = [from_page(each) for each in up_gather.pairs()]
    (one,) = [from_page(each) for each in one_gather.pairs()]
    (down,) = [from_page(each) for each in down_gather.pairs()]
    hidden = up_weight.shape[-1] // features
    up = jnp.concatenate([up_a, up_b], 0)
    up_grad = jnp.stack([untiled(up[:hidden]), untiled(one[:hidden])]).astype(f32)
    out_grad = jnp.stack([up[hidden], one[hidden]]).astype(f32)
    down_grad = jnp.stack([down, one[hidden + 1 :]]).astype(f32).reshape(2, -1, features)
    first, second = [from_page(each) for each in late.pairs()]
    vis_qkv_grad = jnp.concatenate(
        [each[i] for i in range(3) for each in (first, second)], 1
    )
    qkv_grad = jnp.stack([vis_qkv_grad.astype(f32), three])

    count = vis_sums.shape[0]
    small = small.reshape(2, count + 8, features)
    gain_two, bias_two, obias, dbias = [own_columns(small[:, i]) for i in range(4)]
    gain_one, bias_one = [own_columns(small[:, count + i]) for i in range(2)]
    ubias = own_columns(small[:, 4:count].reshape(2, -1))

    return (
        jnp.concatenate([vis_first, vis_keep], 0)[None],
        own_rows(query_result)[None],
        jnp.concatenate([grad_first, grad_keep], 0)[None],
        own_input[None],
        gain_one,
        bias_one,
        qkv_grad,
        out_grad,
        obias,
        gain_two,
        bias_two,
        up_grad,
        ubias,
        down_grad,
        dbias,
    )


def solution(mesh):
    return jax.shard_map(
        body,
        mesh=mesh,
        in_specs=(
            P("page", "strip", None, None),
            P("page", "strip", None),
            P("page", None, None),
            P("page", None),
            P("page"),
            P(),
            P(),
            P(),
            P(),
            P(),
            P(),
            P(),
            P(),
            P(),
            P(),
            P(),
            P("page", "strip", None, None),
            P("page", "strip", None),
        ),
        out_specs=(
            P("page", "strip", None, None),
            P("page", "strip", None),
            P("page", "strip", None, None),
            P("page", "strip", None),
            P(None, "strip"),
            P(None, "strip"),
            P(None, "strip", None),
            P(None, "strip", None),
            P(None, "strip"),
            P(None, "strip"),
            P(None, "strip"),
            P(None, "strip", None),
            P(None, "strip"),
            P(None, "strip", None),
            P(None, "strip"),
        ),
        check_vma=False,
    )
```

```python
import functools

import jax
import jax.numpy as jnp
from jax import lax
from jax.experimental import pallas as pl
from jax.experimental.pallas import tpu as pltpu
from jax.sharding import PartitionSpec as P

HEADS = 12
WIN = 12
SHIFT = 6
CELLS = WIN * WIN
PAIR = 128
MASKED = -1000000000.0
MIB = 1024 * 1024

bf16 = jnp.bfloat16
f32 = jnp.float32


def params(mib):
    return pltpu.CompilerParams(vmem_limit_bytes=min(int(mib), 56) * MIB)


def row_block(rows):
    for size in range(336, 15, -16):
        if rows % size == 0:
            return size
    return rows


def dot_nn(a, b):
    return lax.dot_general(a, b, (((1,), (0,)), ((), ())), preferred_element_type=f32)


def dot_nt(a, b):
    return lax.dot_general(a, b, (((1,), (1,)), ((), ())), preferred_element_type=f32)


def dot_tn(a, b):
    return lax.dot_general(a, b, (((0,), (0,)), ((), ())), preferred_element_type=f32)


def cost(flops, moved, special=0):
    share = 20000
    return pl.CostEstimate(
        flops=int(flops) // share,
        bytes_accessed=int(moved) // share,
        transcendentals=int(special) // share,
    )


def whole(shape):
    return pl.BlockSpec(shape, lambda *_: (0,) * len(shape))


def normalised(values):
    center = values - jnp.mean(values, -1, keepdims=True)
    spread = jnp.mean(center * center, -1, keepdims=True)
    rstd = lax.rsqrt(spread + 1e-05)
    return center * rstd, rstd


def norm_back(grad, hat, rstd, gain):
    scaled = grad * gain
    mean_one = jnp.mean(scaled, -1, keepdims=True)
    mean_two = jnp.mean(scaled * hat, -1, keepdims=True)
    return rstd * (scaled - mean_one - hat * mean_two)


def enter_kernel(own_ref, head_ref, out_ref, row_ref, cells_ref):
    columns = own_ref.shape[1]
    for r in range(WIN):
        row = own_ref[SHIFT + r] if r < WIN - SHIFT else head_ref[r - (WIN - SHIFT)]
        row_ref[0:columns, :] = row.astype(f32)
        row_ref[columns : columns + SHIFT, :] = row_ref[0:SHIFT, :]
        for w in range(columns // WIN):
            at = w * CELLS + r * WIN
            cells_ref[at : at + WIN, :] = row_ref[w * WIN + SHIFT : (w + 1) * WIN + SHIFT, :]
    for w in range(columns // WIN):
        at = slice(w * CELLS, (w + 1) * CELLS)
        out_ref[at, :] = cells_ref[at, :].astype(bf16)


def enter(own, head):
    rows, columns, width = own.shape
    cells = rows * columns
    return pl.pallas_call(
        enter_kernel,
        out_shape=jax.ShapeDtypeStruct((cells, width), bf16),
        scratch_shapes=[
            pltpu.VMEM((columns + 2 * WIN, width), f32),
            pltpu.VMEM((cells, width), f32),
        ],
        compiler_params=params(14),
        cost_estimate=cost(0, 4 * cells * width),
        name="enter",
    )(own, head)


def leave_kernel(cells_ref, keep_ref, send_ref, row_ref, wide_ref):
    columns = keep_ref.shape[1]
    for w in range(columns // WIN):
        at = slice(w * CELLS, (w + 1) * CELLS)
        wide_ref[at, :] = cells_ref[at, :].astype(f32)
    for r in range(WIN):
        for w in range(columns // WIN):
            at = w * CELLS + r * WIN
            row_ref[w * WIN + SHIFT : (w + 1) * WIN + SHIFT, :] = wide_ref[at : at + WIN, :]
        row_ref[0:SHIFT, :] = row_ref[columns : columns + SHIFT, :]
        row = row_ref[0:columns, :].astype(bf16)
        if r < WIN - SHIFT:
            keep_ref[r] = row
        else:
            send_ref[r - (WIN - SHIFT)] = row


def leave(cells, columns):
    width = cells.shape[1]
    return pl.pallas_call(
        leave_kernel,
        out_shape=[
            jax.ShapeDtypeStruct((WIN - SHIFT, columns, width), bf16),
            jax.ShapeDtypeStruct((SHIFT, columns, width), bf16),
        ],
        scratch_shapes=[
            pltpu.VMEM((columns + 2 * WIN, width), f32),
            pltpu.VMEM(cells.shape, f32),
        ],
        compiler_params=params(14),
        cost_estimate=cost(0, 4 * cells.size),
        name="leave",
    )(cells)


def qkv_kernel(stream, x_ref, gain_ref, bias_ref, w_ref, a_ref, out_ref):
    rows, width = x_ref.shape
    block = row_block(rows)
    row = slice(stream, stream + 1)
    ats = [slice(i * block, (i + 1) * block) for i in range(rows // block)]

    @pl.when(pl.program_id(0) == 0)
    def _():
        for at in ats:
            hat, _ = normalised(x_ref[at, :].astype(f32))
            low = (hat * gain_ref[row, :] + bias_ref[row, :]).astype(bf16)
            a_ref[at, :] = low
            out_ref[at, :] = dot_nn(low, w_ref[...]).astype(bf16)

    @pl.when(pl.program_id(0) != 0)
    def _():
        for at in ats:
            out_ref[at, :] = dot_nn(a_ref[at, :], w_ref[...]).astype(bf16)


def norm_qkv(x, gain, bias, weight, stream):
    rows, width = x.shape
    full = weight.shape[-1]
    return pl.pallas_call(
        functools.partial(qkv_kernel, stream),
        grid=(full // width,),
        in_specs=[
            whole((rows, width)),
            whole(gain.shape),
            whole(bias.shape),
            pl.BlockSpec((None, width, width), lambda j: (stream, 0, j)),
        ],
        out_specs=[whole((rows, width)), pl.BlockSpec((rows, width), lambda j: (0, j))],
        out_shape=[
            jax.ShapeDtypeStruct((rows, width), bf16),
            jax.ShapeDtypeStruct((rows, full), bf16),
        ],
        compiler_params=params(8 + rows // 80),
        cost_estimate=cost(2 * rows * width * full, 2 * rows * (2 * width + full) + 2 * width * full),
        name="norm_qkv",
    )(x, gain, bias, weight)


def first_half(shape):
    return lax.broadcasted_iota(jnp.int32, shape, len(shape) - 1) < PAIR // 2


def stacked(block):
    left = first_half(block.shape)
    zero = jnp.zeros_like(block)
    return jnp.concatenate([jnp.where(left, block, zero), jnp.where(left, zero, block)], 0)


def row_sums(values):
    ones = jnp.ones((8, PAIR), f32)
    return lax.dot_general(
        ones,
        values,
        (((1,), (1,)), ((), ())),
        precision=lax.Precision.HIGHEST,
        preferred_element_type=f32,
    )[:1]


def joined(upright):
    rows = upright.shape[0] // 2
    return jnp.where(first_half((rows, PAIR)), upright[:rows], upright[rows:])


def unstacked(turned):
    return joined(turned.T)


def query_forward_kernel(
    qq_ref, k_ref, v_ref, ko_ref, vo_ref, bias_ref, out_ref, stats_ref, s_ref, lse_ref
):
    queries = qq_ref.shape[0]
    cells = k_ref.shape[0]
    own = ko_ref.shape[0]
    scaled = stacked(qq_ref[...] * 0.125)
    bias = bias_ref[...]
    self_score = dot_nt(ko_ref[...], scaled) + jnp.concatenate([bias, bias], 1)
    top = jnp.max(self_score, 0, keepdims=True)
    block = row_block(cells)
    blocks = [slice(i * block, (i + 1) * block) for i in range(cells // block)]
    for at in blocks:
        score = dot_nt(k_ref[at, :], scaled)
        s_ref[at, :] = score
        top = jnp.maximum(top, jnp.max(score, 0, keepdims=True))
    prob = jnp.exp(self_score - top)
    total = jnp.sum(prob, 0, keepdims=True)
    mixed = dot_nn(vo_ref[...].T, prob.astype(bf16))
    for at in blocks:
        prob = jnp.exp(s_ref[at, :] - top)
        total = total + jnp.sum(prob, 0, keepdims=True)
        mixed = mixed + dot_nn(v_ref[at, :].T, prob.astype(bf16))
    out_ref[...] = unstacked(mixed * (1.0 / total))
    lse = top + jnp.log(total)
    pair = pl.program_id(0)

    @pl.when(pair == 0)
    def _():
        lse_ref[...] = jnp.zeros_like(lse_ref)

    lse_ref[pl.ds(2 * pair, 1), :] = lse[:, :queries]
    lse_ref[pl.ds(2 * pair + 1, 1), :] = lse[:, queries:]

    @pl.when(pair == pl.num_programs(0) - 1)
    def _():
        stats_ref[...] = lse_ref[...].T


def query_forward(query_qkv, own_qkv, vis_qkv, self_bias):
    cells = vis_qkv.shape[0]
    queries = query_qkv.shape[0]
    own = own_qkv.shape[0]
    width = query_qkv.shape[1] // 3
    pairs = width // PAIR
    keys = cells + own

    def part(rows, j):
        return pl.BlockSpec((rows, PAIR), lambda p, j=j: (0, j * pairs + p))

    return pl.pallas_call(
        query_forward_kernel,
        grid=(pairs,),
        in_specs=[
            part(queries, 0),
            part(cells, 1),
            part(cells, 2),
            part(own, 1),
            part(own, 2),
            whole(self_bias.shape),
        ],
        out_specs=[part(queries, 0), whole((queries, PAIR))],
        out_shape=[
            jax.ShapeDtypeStruct((queries, width), f32),
            jax.ShapeDtypeStruct((queries, PAIR), f32),
        ],
        scratch_shapes=[
            pltpu.VMEM((cells, 2 * queries), f32),
            pltpu.VMEM((PAIR, queries), f32),
        ],
        compiler_params=params(10 + queries // 32),
        cost_estimate=cost(
            4 * 2 * queries * keys * width, 4 * cells * width, 2 * queries * keys * pairs
        ),
        name="query_forward",
    )(query_qkv, vis_qkv, vis_qkv, own_qkv, own_qkv, self_bias)


def window_forward_kernel(
    windows,
    q_ref,
    k_ref,
    v_ref,
    kq_ref,
    vq_ref,
    row_ref,
    col_ref,
    open_ref,
    out_ref,
    lse_ref,
    scaled_ref,
    near_ref,
    mixed_ref,
    far_ref,
):
    cells = [slice(w * CELLS, (w + 1) * CELLS) for w in range(windows)]
    lanes = [slice(2 * w * CELLS, 2 * (w + 1) * CELLS) for w in range(windows)]
    tops = []
    for w in range(windows):
        scaled = stacked(q_ref[cells[w], :] * 0.125)
        scaled_ref[lanes[w], :] = scaled
        near = dot_nt(k_ref[cells[w], :], scaled)
        near = jnp.where(col_ref[w] == row_ref[w], near, MASKED)
        near_ref[w] = near
        tops.append(jnp.max(near, 0, keepdims=True))
    far = dot_nt(kq_ref[...], scaled_ref[...]) + open_ref[...]
    top = jnp.maximum(jnp.concatenate(tops, 1), jnp.max(far, 0, keepdims=True))
    far = jnp.exp(far - top)
    total = jnp.sum(far, 0, keepdims=True)
    far_mixed = dot_nn(vq_ref[...].T, far.astype(bf16))
    totals = []
    for w in range(windows):
        near = jnp.exp(near_ref[w] - top[:, lanes[w]])
        totals.append(jnp.sum(near, 0, keepdims=True))
        mixed_ref[w] = dot_nn(v_ref[cells[w], :].T, near.astype(bf16))
    total = total + jnp.concatenate(totals, 1)
    share = 1.0 / total
    lse_ref[...] = top + jnp.log(total)
    far_ref[...] = far_mixed
    for w in range(windows):
        turned = (mixed_ref[w] + far_ref[:, lanes[w]]) * share[:, lanes[w]]
        out_ref[cells[w], :] = joined(turned.astype(bf16).T)


def window_forward(vis_qkv, query_qkv, region_row, region_col, closed):
    cells = vis_qkv.shape[0]
    queries = query_qkv.shape[0]
    width = vis_qkv.shape[1] // 3
    pairs = width // PAIR
    windows = cells // CELLS

    def part(rows, j):
        return pl.BlockSpec((rows, PAIR), lambda p, j=j: (0, j * pairs + p))

    return pl.pallas_call(
        functools.partial(window_forward_kernel, windows),
        grid=(pairs,),
        in_specs=[
            part(cells, 0),
            part(cells, 1),
            part(cells, 2),
            part(queries, 1),
            part(queries, 2),
            whole(region_row.shape),
            whole(region_col.shape),
            whole(closed.shape),
        ],
        out_specs=[
            part(cells, 0),
            pl.BlockSpec((None, 1, 2 * cells), lambda p: (p, 0, 0)),
        ],
        out_shape=[
            jax.ShapeDtypeStruct((cells, width), bf16),
            jax.ShapeDtypeStruct((pairs, 1, 2 * cells), f32),
        ],
        scratch_shapes=[
            pltpu.VMEM((2 * cells, PAIR), bf16),
            pltpu.VMEM((windows, CELLS, 2 * CELLS), f32),
            pltpu.VMEM((windows, PAIR, 2 * CELLS), f32),
            pltpu.VMEM((PAIR, 2 * cells), f32),
        ],
        compiler_params=params(12 + queries // 28),
        cost_estimate=cost(
            8 * cells * (CELLS + queries) * width,
            8 * cells * width,
            2 * pairs * cells * (CELLS + queries),
        ),
        name="window_forward",
    )(vis_qkv, vis_qkv, vis_qkv, query_qkv, query_qkv, region_row, region_col, closed)


def attention_backward_kernel(
    windows,
    first,
    q_ref,
    k_ref,
    v_ref,
    do_ref,
    qq_ref,
    kq_ref,
    vq_ref,
    doq_ref,
    ko_ref,
    vo_ref,
    row_ref,
    col_ref,
    open_ref,
    bias_ref,
    lse_ref,
    lseq_ref,
    mixq_ref,
    *rest,
):
    if len(rest) > 16:
        rest = rest[3:]
    attention_backward_body(
        windows,
        first,
        q_ref,
        k_ref,
        v_ref,
        do_ref,
        qq_ref,
        kq_ref,
        vq_ref,
        doq_ref,
        ko_ref,
        vo_ref,
        row_ref,
        col_ref,
        open_ref,
        bias_ref,
        lse_ref,
        lseq_ref,
        mixq_ref,
        *rest,
    )


def attention_backward_body(
    windows,
    first,
    q_ref,
    k_ref,
    v_ref,
    do_ref,
    qq_ref,
    kq_ref,
    vq_ref,
    doq_ref,
    ko_ref,
    vo_ref,
    row_ref,
    col_ref,
    open_ref,
    bias_ref,
    lse_ref,
    lseq_ref,
    mixq_ref,
    dq_ref,
    dk_ref,
    dv_ref,
    dqq_ref,
    dkq_ref,
    dvq_ref,
    dko_ref,
    dvo_ref,
    scaled_ref,
    grad_ref,
    near_ref,
    neart_ref,
    seenk_ref,
    seenv_ref,
    far_ref,
    stats_ref,
):
    cells = [slice(w * CELLS, (w + 1) * CELLS) for w in range(windows)]
    lanes = [slice(2 * w * CELLS, 2 * (w + 1) * CELLS) for w in range(windows)]
    lse = lse_ref[...]

    deltas = []
    for w in range(windows):
        scaled = stacked(q_ref[cells[w], :] * 0.125)
        grad = stacked(do_ref[cells[w], :])
        scaled_ref[lanes[w], :] = scaled
        grad_ref[lanes[w], :] = grad
        near = dot_nt(k_ref[cells[w], :], scaled)
        near = jnp.exp(jnp.where(col_ref[w] == row_ref[w], near, MASKED) - lse[:, lanes[w]])
        near_t = near * dot_nt(v_ref[cells[w], :], grad)
        near_ref[w] = near
        neart_ref[w] = near_t
        deltas.append(jnp.sum(near_t, 0, keepdims=True))
    kq = kq_ref[...]
    far = jnp.exp(dot_nt(kq, scaled_ref[...]) + open_ref[...] - lse)
    far_t = far * dot_nt(vq_ref[...], grad_ref[...])
    delta = jnp.concatenate(deltas, 1) + jnp.sum(far_t, 0, keepdims=True)
    far_d = (far_t - far * delta).astype(bf16)
    dkq_ref[...] = dot_nn(far_d, scaled_ref[...]).astype(bf16)
    dvq_ref[...] = dot_nn(far.astype(bf16), grad_ref[...]).astype(bf16)
    far_ref[...] = dot_nn(kq.T, far_d).T

    scaled_q = stacked(qq_ref[...] * 0.125)
    grad_q = stacked(doq_ref[...])
    stats_ref[...] = lseq_ref[...].T
    head = 2 * (first + pl.program_id(0))
    lse_q = jnp.concatenate(
        [stats_ref[pl.ds(head, 1), :], stats_ref[pl.ds(head + 1, 1), :]], 1
    )
    mix_q = mixq_ref[...]
    delta_q = row_sums(grad_q.astype(f32) * jnp.concatenate([mix_q, mix_q], 0))
    bias = bias_ref[...]
    prob = jnp.exp(dot_nt(ko_ref[...], scaled_q) + jnp.concatenate([bias, bias], 1) - lse_q)
    dscore = (prob * (dot_nt(vo_ref[...], grad_q) - delta_q)).astype(bf16)
    dko_ref[...] = dot_nn(dscore, scaled_q)
    dvo_ref[...] = dot_nn(prob.astype(bf16), grad_q)
    turned = dot_nn(ko_ref[...].T, dscore)
    rows = k_ref.shape[0]
    block = row_block(rows)
    for i in range(rows // block):
        at = slice(i * block, (i + 1) * block)
        k_rows = k_ref[at, :]
        prob = jnp.exp(dot_nt(k_rows, scaled_q) - lse_q)
        dscore = (prob * (dot_nt(v_ref[at, :], grad_q) - delta_q)).astype(bf16)
        seenk_ref[at, :] = dot_nn(dscore, scaled_q)
        seenv_ref[at, :] = dot_nn(prob.astype(bf16), grad_q)
        turned = turned + dot_nn(k_rows.T, dscore)
    dqq_ref[...] = (unstacked(turned) * 0.125).astype(bf16)

    for w in range(windows):
        near = near_ref[w]
        near_d = (neart_ref[w] - near * delta[:, lanes[w]]).astype(bf16)
        upright = dot_nn(k_ref[cells[w], :].T, near_d).T + far_ref[lanes[w], :]
        dq_ref[cells[w], :] = (joined(upright) * 0.125).astype(bf16)
        dk_ref[cells[w], :] = (
            dot_nn(near_d, scaled_ref[lanes[w], :]) + seenk_ref[cells[w], :]
        ).astype(bf16)
        dv_ref[cells[w], :] = (
            dot_nn(near.astype(bf16), grad_ref[lanes[w], :]) + seenv_ref[cells[w], :]
        ).astype(bf16)


def attention_backward(
    vis_qkv,
    query_qkv,
    own_qkv,
    grad,
    grad_q,
    region_row,
    region_col,
    closed,
    self_bias,
    lse,
    joint_q,
    first,
    count,
    begun=(),
):
    cells = vis_qkv.shape[0]
    queries = query_qkv.shape[0]
    own = own_qkv.shape[0]
    width = vis_qkv.shape[1] // 3
    pairs = width // PAIR
    windows = cells // CELLS

    def part(rows, j):
        return pl.BlockSpec((rows, PAIR), lambda p, j=j: (0, j * pairs + first + p))

    def result(rows):
        return pl.BlockSpec((rows, PAIR), lambda p: (0, p))

    def filled(rows):
        return pl.BlockSpec((rows, PAIR), lambda p: (0, first + p))

    def stats(array):
        return pl.BlockSpec((None,) + array.shape[1:], lambda p: (first + p, 0, 0))

    span = count * PAIR
    return pl.pallas_call(
        functools.partial(attention_backward_kernel, windows, first),
        grid=(count,),
        in_specs=[
            part(cells, 0),
            part(cells, 1),
            part(cells, 2),
            part(cells, 0),
            part(queries, 0),
            part(queries, 1),
            part(queries, 2),
            part(queries, 0),
            part(own, 1),
            part(own, 2),
            whole(region_row.shape),
            whole(region_col.shape),
            whole(closed.shape),
            whole(self_bias.shape),
            stats(lse),
            pl.BlockSpec((queries, PAIR), lambda p: (0, pairs)),
            part(queries, 0),
        ]
        + [pl.BlockSpec(memory_space=pl.ANY)] * len(begun),
        out_specs=[filled(cells)] * 3 + [result(queries)] * 3 + [result(own)] * 2,
        out_shape=[jax.ShapeDtypeStruct((cells, width), bf16)] * 3
        + [jax.ShapeDtypeStruct((queries, span), bf16)] * 3
        + [jax.ShapeDtypeStruct((own, span), f32)] * 2,
        scratch_shapes=[
            pltpu.VMEM((2 * cells, PAIR), bf16),
            pltpu.VMEM((2 * cells, PAIR), bf16),
            pltpu.VMEM((windows, CELLS, 2 * CELLS), f32),
            pltpu.VMEM((windows, CELLS, 2 * CELLS), f32),
            pltpu.VMEM((cells, PAIR), f32),
            pltpu.VMEM((cells, PAIR), f32),
            pltpu.VMEM((2 * cells, PAIR), f32),
            pltpu.VMEM((PAIR, queries), f32),
        ],
        compiler_params=params(16 + queries // 25),
        cost_estimate=cost(
            20 * cells * (CELLS + 2 * queries) * span,
            14 * cells * span,
            2 * count * cells * (CELLS + 2 * queries),
        ),
        input_output_aliases={17 + i: i for i in range(len(begun))},
        name="attention_backward",
    )(
        vis_qkv,
        vis_qkv,
        vis_qkv,
        grad,
        query_qkv,
        query_qkv,
        query_qkv,
        grad_q,
        own_qkv,
        own_qkv,
        region_row,
        region_col,
        closed,
        self_bias,
        lse,
        joint_q,
        joint_q,
        *begun,
    )


def gelu_pair(z):
    below = 0.5 + 0.5 * lax.erf(z * 0.7071067811865476)
    bell = jnp.exp(-0.5 * z * z)
    return z * below, below + z * bell * 0.3989422804014327


def ffn_forward_kernel(
    stream,
    x_ref,
    o_ref,
    wo_ref,
    bo_ref,
    gain_ref,
    bias_ref,
    wu_ref,
    bu_ref,
    wd_ref,
    bd_ref,
    x1_ref,
    b_ref,
    hid_ref,
    slope_ref,
    out_ref,
    sum_ref,
):
    rows, width = x_ref.shape
    block = row_block(rows)
    count = rows // block
    ats = [slice(i * block, (i + 1) * block) for i in range(count)]
    step = pl.program_id(0)
    row = slice(stream, stream + 1)

    @pl.when(step == 0)
    def _():
        for at in ats:
            x1 = x_ref[at, :].astype(f32) + dot_nn(o_ref[at, :].astype(bf16), wo_ref[...]) + bo_ref[row, :]
            x1_ref[at, :] = x1
            hat, _ = normalised(x1)
            b_ref[at, :] = (hat * gain_ref[row, :] + bias_ref[row, :]).astype(bf16)
            sum_ref[at, :] = x1 + bd_ref[row, :]

    def project(i):
        return dot_nn(b_ref[ats[i], :], wu_ref[...]) + bu_ref[row, :]

    z = project(0)
    for i in range(count):
        ahead = project(i + 1) if i + 1 < count else None
        hidden, slope = gelu_pair(z)
        hidden = hidden.astype(bf16)
        hid_ref[ats[i], :] = hidden
        slope_ref[ats[i], :] = slope.astype(bf16)
        sum_ref[ats[i], :] += dot_nn(hidden, wd_ref[...])
        z = ahead

    @pl.when(step == pl.num_programs(0) - 1)
    def _():
        out_ref[...] = sum_ref[...].astype(bf16)


def ffn_forward(x, attended, out_w, out_b, gain, bias, up_w, up_b, down_w, down_b, stream):
    rows, width = x.shape
    hidden = up_w.shape[-1]
    chunk = 768
    return pl.pallas_call(
        functools.partial(ffn_forward_kernel, stream),
        grid=(hidden // chunk,),
        in_specs=[
            whole((rows, width)),
            whole((rows, width)),
            pl.BlockSpec((None, width, width), lambda f: (stream, 0, 0)),
            whole(out_b.shape),
            whole(gain.shape),
            whole(bias.shape),
            pl.BlockSpec((None, width, chunk), lambda f: (stream, 0, f)),
            pl.BlockSpec((2, chunk), lambda f: (0, f)),
            pl.BlockSpec((None, chunk, width), lambda f: (stream, f, 0)),
            whole(down_b.shape),
        ],
        out_specs=[
            whole((rows, width)),
            whole((rows, width)),
            pl.BlockSpec((rows, chunk), lambda f: (0, f)),
            pl.BlockSpec((rows, chunk), lambda f: (0, f)),
            whole((rows, width)),
        ],
        out_shape=[
            jax.ShapeDtypeStruct((rows, width), f32),
            jax.ShapeDtypeStruct((rows, width), bf16),
            jax.ShapeDtypeStruct((rows, hidden), bf16),
            jax.ShapeDtypeStruct((rows, hidden), bf16),
            jax.ShapeDtypeStruct((rows, width), bf16),
        ],
        scratch_shapes=[pltpu.VMEM((rows, width), f32)],
        compiler_params=params(44),
        cost_estimate=cost(
            2 * rows * width * (2 * hidden + width),
            4 * width * hidden + 4 * rows * hidden + 12 * rows * width,
            2 * rows * hidden,
        ),
        name="ffn_forward",
    )(x, attended, out_w, out_b, gain, bias, up_w, up_b, down_w, down_b)


def ffn_backward_kernel(
    stream,
    g_ref,
    slope_ref,
    x1_ref,
    wd_ref,
    wu_ref,
    wo_ref,
    gain_ref,
    dz_ref,
    dx1_ref,
    du_ref,
    do_ref,
    sums_ref,
    sum_ref,
):
    rows, width = g_ref.shape
    block = row_block(rows)
    count = rows // block
    ats = [slice(i * block, (i + 1) * block) for i in range(count)]
    step = pl.program_id(0)
    row = slice(stream, stream + 1)

    @pl.when(step == 0)
    def _():
        sum_ref[...] = jnp.zeros_like(sum_ref)

    up_bias = jnp.zeros((1, dz_ref.shape[1]), f32)

    def pulled(i):
        return dot_nt(g_ref[ats[i], :], wd_ref[...])

    grad = pulled(0)
    for i in range(count):
        ahead = pulled(i + 1) if i + 1 < count else None
        dz = grad * slope_ref[ats[i], :].astype(f32)
        low = dz.astype(bf16)
        dz_ref[ats[i], :] = low
        up_bias = up_bias + jnp.sum(dz, 0, keepdims=True)
        sum_ref[ats[i], :] += dot_nt(low, wu_ref[...])
        grad = ahead
    sums_ref[pl.ds(4 + step, 1), :] = up_bias

    @pl.when(step == pl.num_programs(0) - 1)
    def _():
        sums_ref[0:4, :] = jnp.zeros((4, width), f32)
        for at in ats:
            hat, rstd = normalised(x1_ref[at, :])
            db = sum_ref[at, :]
            g = g_ref[at, :].astype(f32)
            dx1 = g + norm_back(db, hat, rstd, gain_ref[row, :])
            dx1_ref[at, :] = dx1
            du = dx1.astype(bf16)
            du_ref[at, :] = du
            do_ref[at, :] = dot_nt(du, wo_ref[...]).astype(bf16)
            sums_ref[0:1, :] += jnp.sum(db * hat, 0, keepdims=True)
            sums_ref[1:2, :] += jnp.sum(db, 0, keepdims=True)
            sums_ref[2:3, :] += jnp.sum(dx1, 0, keepdims=True)
            sums_ref[3:4, :] += jnp.sum(g, 0, keepdims=True)


def ffn_backward(g, slope, x1, down_w, up_w, out_w, gain, stream):
    rows, width = g.shape
    hidden = up_w.shape[-1]
    chunk = width
    return pl.pallas_call(
        functools.partial(ffn_backward_kernel, stream),
        grid=(hidden // chunk,),
        in_specs=[
            whole((rows, width)),
            pl.BlockSpec((rows, chunk), lambda f: (0, f)),
            whole((rows, width)),
            pl.BlockSpec((None, chunk, width), lambda f: (stream, f, 0)),
            pl.BlockSpec((None, width, chunk), lambda f: (stream, 0, f)),
            pl.BlockSpec((None, width, width), lambda f: (stream, 0, 0)),
            whole(gain.shape),
        ],
        out_specs=[
            pl.BlockSpec((None, rows, chunk), lambda f: (f, 0, 0)),
            whole((rows, width)),
            whole((rows, width)),
            whole((rows, width)),
            whole((4 + hidden // chunk, width)),
        ],
        out_shape=[
            jax.ShapeDtypeStruct((hidden // chunk, rows, chunk), bf16),
            jax.ShapeDtypeStruct((rows, width), f32),
            jax.ShapeDtypeStruct((rows, width), bf16),
            jax.ShapeDtypeStruct((rows, width), bf16),
            jax.ShapeDtypeStruct((4 + hidden // chunk, width), f32),
        ],
        scratch_shapes=[pltpu.VMEM((rows, width), f32)],
        compiler_params=params(44),
        cost_estimate=cost(
            2 * rows * width * (2 * hidden + width),
            4 * width * hidden + 4 * rows * hidden + 14 * rows * width,
        ),
        name="ffn_backward",
    )(g, slope, x1, down_w, up_w, out_w, gain)


def input_kernel(stream, dq_ref, dk_ref, dv_ref, w_ref, x_ref, dx1_ref, gain_ref, out_ref, sums_ref):
    width = x_ref.shape[1]

    @pl.when(pl.program_id(0) == 0)
    def _():
        sums_ref[...] = jnp.zeros_like(sums_ref)

    grad = dot_nt(dq_ref[...], w_ref[:, :width])
    grad = grad + dot_nt(dk_ref[...], w_ref[:, width : 2 * width])
    grad = grad + dot_nt(dv_ref[...], w_ref[:, 2 * width :])
    hat, rstd = normalised(x_ref[...].astype(f32))
    out_ref[...] = (
        dx1_ref[...] + norm_back(grad, hat, rstd, gain_ref[stream : stream + 1, :])
    ).astype(bf16)
    at = 4 * stream
    sums_ref[at : at + 1, :] += jnp.sum(grad * hat, 0, keepdims=True)
    sums_ref[at + 1 : at + 2, :] += jnp.sum(grad, 0, keepdims=True)


def input_grad(dq, dk, dv, weight, x, dx1, gain, stream):
    rows, width = x.shape
    block = row_block(rows)
    rows_spec = pl.BlockSpec((block, width), lambda i: (i, 0))
    return pl.pallas_call(
        functools.partial(input_kernel, stream),
        grid=(rows // block,),
        in_specs=[rows_spec] * 3
        + [
            pl.BlockSpec((None, width, 3 * width), lambda i: (stream, 0, 0)),
            rows_spec,
            rows_spec,
            whole(gain.shape),
        ],
        out_specs=[rows_spec, whole((8, width))],
        out_shape=[
            jax.ShapeDtypeStruct((rows, width), bf16),
            jax.ShapeDtypeStruct((8, width), f32),
        ],
        compiler_params=params(16),
        cost_estimate=cost(6 * rows * width * width, 14 * rows * width + 6 * width * width),
        name="input_grad",
    )(dq, dk, dv, weight, x, dx1, gain)


def after(value, *before):
    return lax.optimization_barrier((value,) + before)[0]


def beside(made, *flights):
    return lax.optimization_barrier((made,) + flights)


def moved(block, axis, step):
    size = lax.axis_size(axis)
    return lax.ppermute(block, axis, [(i, (i + step) % size) for i in range(size)])


def swapped(block, axis, mask):
    size = lax.axis_size(axis)
    return lax.ppermute(block, axis, [(i, i ^ mask) for i in range(size)])


def other_core(block):
    return swapped(block, "strip", 1)


def place():
    strip = lax.axis_index("strip")
    return lax.axis_size("strip") // 2, strip // 2, strip % 2


def pick(block, index, axis=0):
    return lax.dynamic_index_in_dim(block, index, axis, keepdims=False)


def added(blocks, kind=bf16):
    total = blocks[0].astype(f32)
    for block in blocks[1:]:
        total = total + block.astype(f32)
    return total.astype(kind)


def bit_of(axis, mask):
    return (lax.axis_index(axis) // mask) % 2


class Phase:
    def __init__(self, blocks, dims, axis, mask):
        bit = bit_of(axis, mask)
        theirs, self.mine = [
            [added([pick(term, half, dim) for term in terms]) for terms, dim in zip(blocks, dims)]
            for half in (1 - bit, bit)
        ]
        self.shapes = [block.shape for block in theirs]
        self.sent, self.got = exchange(theirs, axis, mask)

    def terms(self):
        got = parted(self.got, self.shapes)
        return [[mine, more] for mine, more in zip(self.mine, got)]

    def sums(self):
        return [added(terms) for terms in self.terms()]


def mapped(change, terms):
    return [change(term) for term in terms]


class Gather:
    def __init__(self, blocks, dims, axis, mask):
        self.bit = bit_of(axis, mask)
        self.blocks, self.dims = blocks, dims
        self.shapes = [block.shape for block in blocks]
        self.sent, self.got = exchange(blocks, axis, mask)

    def pairs(self):
        first = self.bit == 0
        return [
            jnp.stack([jnp.where(first, one, two), jnp.where(first, two, one)], dim)
            for one, two, dim in zip(self.blocks, parted(self.got, self.shapes), self.dims)
        ]


class PageGather:
    def __init__(self, blocks):
        self.shapes = [block.shape for block in blocks]
        rows = [block.reshape(-1, block.shape[-1]) for block in blocks]
        self.sent = jnp.concatenate(rows, 0)
        self.got = [swapped(self.sent, "page", mask) for mask in (1, 2, 3)]

    def whole(self):
        def ordered(bit, one, two, axis):
            first = bit == 0
            return jnp.stack([jnp.where(first, one, two), jnp.where(first, two, one)], axis)

        every = [parted(rows, self.shapes) for rows in [self.sent] + list(self.got)]
        result = []
        for mine, by_x, by_y, by_both in zip(*every):
            near = ordered(bit_of("page", 1), mine, by_x, 1)
            far = ordered(bit_of("page", 1), by_y, by_both, 1)
            result.append(from_page(ordered(bit_of("page", 2), near, far, 1)))
        return result


def parted(rows, shapes):
    if len(shapes) == 1:
        return [rows]
    blocks, at = [], 0
    for shape in shapes:
        count = 1
        for size in shape[:-1]:
            count *= size
        blocks.append(rows[at : at + count].reshape(shape))
        at += count
    return blocks


def exchange(blocks, axis, mask):
    if len(blocks) == 1:
        sent = blocks[0]
    else:
        sent = jnp.concatenate([block.reshape(-1, block.shape[-1]) for block in blocks], 0)
    return sent, swapped(sent, axis, mask)


def by_core(grad):
    strips = lax.axis_size("strip")
    return grad.reshape(strips // 2, 2, grad.shape[0] // strips, grad.shape[1])


def tiled(grad, width):
    count = grad.shape[-1] // width
    return jnp.stack([grad[..., i * width : (i + 1) * width] for i in range(count)], -3)


def untiled(blocks):
    return jnp.concatenate([blocks[i] for i in range(blocks.shape[0])], -1)


def by_page(blocks):
    rows = blocks.shape[-2]
    return blocks.reshape(blocks.shape[:-2] + (2, 2, rows // 4, blocks.shape[-1]))


def from_page(blocks):
    return blocks.reshape(blocks.shape[:-4] + (-1, blocks.shape[-1]))


def by_chip(blocks, axis):
    shape = blocks.shape
    return blocks.reshape(shape[:axis] + (shape[axis] // 2, 2) + shape[axis + 1 :])


def line_masks():
    size, _, _ = place()
    return [2 << i for i in range(size.bit_length() - 1)]


def line_phase(blocks, axes, mask):
    split = [
        [by_chip(term, axis) for term in terms] for terms, axis in zip(blocks, axes)
    ]
    return Phase(split, [axis + 1 for axis in axes], "strip", mask)


def line_first(blocks, axes):
    masks = line_masks()
    for mask in masks[:-2]:
        blocks = line_phase(blocks, axes, mask).terms()
    return line_phase(blocks, axes, masks[-2])


def line_last(blocks, axes):
    return line_phase(blocks, axes, line_masks()[-1])


def line_exchange(block):
    size, z, _ = place()
    return [pick(block, z)] + [
        moved(pick(block, (z + step) % size), "strip", 2 * step) for step in range(1, size)
    ]


def line_gather(block):
    size, _, _ = place()
    return [block] + [moved(block, "strip", 2 * step) for step in range(1, size)]


def line_order(blocks):
    size, z, _ = place()
    double = jnp.stack(blocks[:1] + blocks[:0:-1] + blocks[:1] + blocks[:0:-1])
    return lax.dynamic_slice_in_dim(double, (size - z) % size, size, 0)


def page_exchange(block):
    size = lax.axis_size("page")
    page = lax.axis_index("page")
    shares = block.reshape(size, block.shape[0] // size, block.shape[1])
    return [pick(shares, page)] + [
        swapped(pick(shares, page ^ mask), "page", mask) for mask in range(1, size)
    ]


def page_gather(block):
    size = lax.axis_size("page")
    return [block] + [swapped(block, "page", mask) for mask in range(1, size)]


def page_order(blocks):
    size = len(blocks)
    page = lax.axis_index("page")
    rows, columns = blocks[0].shape
    joined = jnp.zeros((size * rows, columns), f32)
    for mask, block in enumerate(blocks):
        joined = lax.dynamic_update_slice_in_dim(
            joined, block.astype(f32), (page ^ mask) * rows, 0
        )
    return joined


def core_order(mine, other):
    _, _, core = place()
    pair = jnp.stack(
        [jnp.where(core == 0, mine, other), jnp.where(core == 0, other, mine)], 1
    )
    return pair.reshape(-1, pair.shape[-1])


def merge_kernel(one_ref, two_ref, out_ref):
    width = one_ref.shape[1] - PAIR
    one_top = one_ref[:, width:]
    two_top = two_ref[:, width:]
    top = jnp.maximum(one_top, two_top)
    one_share = jnp.exp(one_top - top)
    two_share = jnp.exp(two_top - top)
    total = one_share + two_share
    shape = (PAIR, width)
    head = lax.broadcasted_iota(jnp.int32, shape, 1) // (width // HEADS)
    spread = (lax.broadcasted_iota(jnp.int32, shape, 0) == head).astype(f32)

    def over_heads(share):
        return jnp.dot(share / total, spread, precision=lax.Precision.HIGHEST)

    out_ref[:, :width] = one_ref[:, :width] * over_heads(one_share) + two_ref[
        :, :width
    ] * over_heads(two_share)
    out_ref[:, width:] = top + jnp.log(total)


def merged(one, two):
    shape = one.shape
    rows = one.size // shape[-1]
    out = pl.pallas_call(
        merge_kernel,
        out_shape=jax.ShapeDtypeStruct((rows, shape[-1]), f32),
        compiler_params=params(8),
        cost_estimate=cost(6 * one.size, 12 * one.size),
        name="merge",
    )(one.reshape(rows, -1), two.reshape(rows, -1))
    return out.reshape(shape)


def region_windows(rows):
    across = rows.shape[1] // WIN
    rolled = jnp.roll(rows, -SHIFT, axis=1)
    return rolled.reshape(WIN, across, WIN).transpose(1, 0, 2).reshape(across, CELLS)


def weight_grad(left, right):
    return dot_tn(left, right).astype(bf16)


def body(
    vis_tokens,
    query_tokens,
    region_ids,
    query_mask,
    answer_len,
    norm1_gain,
    norm1_bias,
    qkv_weight,
    out_weight,
    out_bias,
    norm2_gain,
    norm2_bias,
    up_weight,
    up_bias,
    down_weight,
    down_bias,
    vis_cotangent,
    query_cotangent,
):
    strips = lax.axis_size("strip")
    strip = lax.axis_index("strip")
    chips, z, core = place()
    local_rows, columns, features = vis_tokens.shape[1:]
    own_count = query_tokens.shape[1]
    query_count = query_mask.shape[1]
    total_rows = region_ids.shape[1]
    own_start = strip * own_count

    def own_rows(values):
        return lax.dynamic_slice_in_dim(values, own_start, own_count, 0)

    def own_columns(values):
        span = values.shape[1] // strips
        return lax.dynamic_slice_in_dim(values, strip * span, span, 1)

    tokens = line_gather(query_tokens[0])
    head_rows = moved(vis_tokens[0, :SHIFT], "strip", -1)
    tokens = line_order(tokens)
    query = core_order(tokens, other_core(tokens))

    key_open = query_mask[0] > 0
    key_ids = jnp.arange(query_count, dtype=jnp.int32)
    prompt = key_ids < query_count - answer_len[0]
    closed = jnp.where(key_open & prompt, 0.0, MASKED).astype(f32)[:, None]
    own_ids = own_start + jnp.arange(own_count, dtype=jnp.int32)
    allowed = own_rows(key_open)[:, None] & (
        own_rows(prompt)[:, None] | (own_ids[:, None] <= key_ids[None, :])
    )
    self_bias = jnp.where(allowed, 0.0, MASKED).astype(f32)
    row_ids = (strip * local_rows + SHIFT + jnp.arange(local_rows, dtype=jnp.int32)) % total_rows
    region = region_windows(jnp.take(region_ids[0], row_ids, axis=0))
    region_row = jnp.concatenate([region, region], 1)[:, None, :]
    region_col = region[:, :, None]

    query_norm, query_qkv = norm_qkv(query, norm1_gain, norm1_bias, qkv_weight, 1)
    (query_norm, query_qkv), head_rows = beside((query_norm, query_qkv), head_rows)
    own_qkv = own_rows(query_qkv)
    vis = enter(vis_tokens[0], head_rows)
    head_cot = moved(after(vis_cotangent[0, :SHIFT], vis), "strip", -1)
    vis_norm, vis_qkv = norm_qkv(vis, norm1_gain, norm1_bias, qkv_weight, 0)

    part = query_forward(query_qkv, own_qkv, vis_qkv, self_bias)
    part, head_cot = beside(part, head_cot)
    mine, theirs = [
        jnp.concatenate([pick(by_core(each), which, 1) for each in part], -1)
        for which in (core, 1 - core)
    ]
    others = other_core(theirs)
    vis_cot = enter(after(vis_cotangent[0], theirs), head_cot)
    vis_cot, mine, others = beside(vis_cot, mine, others)
    part = merged(mine, others)
    others = swapped(part, "strip", 2)

    vis_windows = window_forward(after(vis_qkv, part), query_qkv, region_row, region_col, closed)
    (vis_attn, vis_lse), part, others = beside(vis_windows, part, others)
    part = merged(part, others)
    mask = 4
    while 2 * mask < strips:
        part = merged(part, swapped(part, "strip", mask))
        mask = 2 * mask
    others = swapped(part, "strip", mask)
    cotangents = line_gather(after(query_cotangent[0], vis_attn))

    weights = (out_weight, out_bias, norm2_gain, norm2_bias, up_weight, up_bias, down_weight, down_bias)
    made = ffn_forward(vis, after(vis_attn, part), *weights, 0)
    made, part, others, cotangents = beside(made, part, others, cotangents)
    vis_x1, vis_b, vis_hid, vis_slope, vis_result = made
    part = merged(part, others)
    others = other_core(part)
    cotangents = line_order(cotangents)
    cot_others = other_core(cotangents)
    vis_down = weight_grad(after(vis_hid, part, cotangents), vis_cot)
    vis_down, part, others, cotangents, cot_others = beside(
        vis_down, part, others, cotangents, cot_others
    )
    down = by_core(vis_down)
    down = Phase([[down.reshape(chips, 2, -1, features // strips, features)]], [1], "strip", 1)

    made = ffn_backward(
        after(vis_cot, down.sent), vis_slope, vis_x1, down_weight, up_weight, out_weight, norm2_gain, 0
    )
    made, down.got = beside(made, down.got)
    vis_dz, vis_dx1, vis_du, vis_do, vis_sums = made
    (down,) = down.terms()
    down = Phase([mapped(by_page, down)], [3], "page", 1)
    hidden = up_weight.shape[-1] // features
    vis_b = after(vis_b, down.sent)
    up_a = [by_core(weight_grad(vis_b, vis_dz[i])) for i in range(hidden - 1)]
    up_a = Phase([[jnp.stack(up_a)]], [2], "strip", 1)
    up_b = [by_core(weight_grad(after(vis_b, up_a.sent), vis_dz[hidden - 1]))]
    up_b = Phase([[jnp.stack(up_b + [by_core(weight_grad(vis_attn, vis_du))])]], [2], "strip", 1)
    made = leave(after(vis_result, up_b.sent), columns)
    (vis_keep, vis_send), up_a.got, up_b.got = beside(made, up_a.got, up_b.got)
    vis_first = moved(vis_send, "strip", 1)
    up_a = line_first(up_a.terms(), [1])

    every = core_order(part, others)
    query_cot = core_order(cotangents, cot_others)
    every, up_sent = beside(every, up_a.sent)
    made = ffn_forward(query, every, *weights, 1)
    made, down.got = beside(made, down.got)
    query_x1, query_b, query_hid, query_slope, query_result = made
    (down,) = down.terms()
    down = Phase([down], [2], "page", 2)
    up_b = Phase([mapped(by_page, terms) for terms in up_b.terms()], [3], "page", 1)
    made = ffn_backward(
        query_cot,
        after(query_slope, up_b.sent, down.sent),
        query_x1,
        down_weight,
        up_weight,
        out_weight,
        norm2_gain,
        1,
    )
    made, up_a.got, up_b.got = beside(made, up_a.got, up_b.got)
    query_dz, query_dx1, query_du, query_do, query_sums = made
    (up_a,) = up_a.terms()
    (up_b,) = up_b.terms()
    up_a = Phase([mapped(by_page, up_a)], [3], "page", 1)
    up_b = Phase([up_b], [2], "page", 2)

    def query_grads(left, right):
        return weight_grad(own_columns(left), right)

    up_rows = features // strips
    query_dz = after(query_dz, up_a.sent, up_b.sent)
    one = jnp.concatenate(
        [
            jnp.stack([query_grads(query_b, query_dz[i]) for i in range(hidden)]),
            query_grads(every[:, :features].astype(bf16), query_du)[None],
            query_grads(query_hid, query_cot).reshape(-1, up_rows, features),
        ],
        0,
    )
    one, down.got = beside(one, down.got)
    one = Phase([[by_page(one)]], [2], "page", 1)
    down = line_first(down.terms(), [0])

    pairs = HEADS // 2
    half = pairs // 2

    def backward(values, first, begun=()):
        return attention_backward(
            values,
            query_qkv,
            own_qkv,
            vis_do,
            query_do,
            region_row,
            region_col,
            closed,
            self_bias,
            vis_lse,
            every,
            first,
            half,
            begun,
        )

    def head_grads(normed, grads, first):
        span = half * PAIR
        return jnp.stack(
            [
                by_core(weight_grad(normed, each[:, first * PAIR : first * PAIR + span]))
                for each in grads
            ],
            2,
        )

    back_one = backward(after(vis_qkv, one.sent, down.sent), 0)
    back_one, up_a.got, up_b.got, down.got, vis_first = beside(
        back_one, up_a.got, up_b.got, down.got, vis_first
    )
    first = Phase([[head_grads(vis_norm, back_one[:3], 0)]], [1], "strip", 1)
    first.sent, one.got = beside(first.sent, one.got)
    (up_a,) = up_a.terms()
    (one,) = one.terms()
    mixed_y = Phase([after(up_a, first.sent), one], [2, 1], "page", 2)
    up_b = line_first(up_b.terms(), [1])
    down = line_last(down.terms(), [0])
    down.sent, up_b.sent, mixed_y.sent, first.got = beside(
        down.sent, up_b.sent, mixed_y.sent, first.got
    )
    (first,) = first.terms()
    first = Phase([mapped(by_page, first)], [3], "page", 1)

    back_two = backward(
        after(vis_qkv, first.sent, mixed_y.sent, up_b.sent, down.sent), half, back_one[:3]
    )
    back_two, first.got, mixed_y.got, up_b.got, down.got = beside(
        back_two, first.got, mixed_y.got, up_b.got, down.got
    )
    part = jnp.stack(
        [by_core(each) for pair in zip(back_one[3:6], back_two[3:6]) for each in pair], 2
    )
    part = Phase([[part]], [1], "strip", 1)
    grads = head_grads(after(vis_norm, part.sent), back_two[:3], half)
    second = Phase([[grads]], [1], "strip", 1)
    second.sent, part.got = beside(second.sent, part.got)
    part = line_first(part.terms(), [0])
    up_a, one = mixed_y.terms()
    (up_b,) = up_b.terms()
    line = line_last([after(up_a, part.sent), up_b], [1, 1])
    line.sent, second.got = beside(line.sent, second.got)
    (second,) = second.terms()
    second = Phase([mapped(by_page, second)], [3], "page", 1)
    (down,) = down.sums()
    early = Gather([after(added(one), second.sent), down[0]], [1, 1], "page", 1)

    made = input_grad(
        after(back_two[0], part.sent, line.sent, second.sent, early.sent),
        back_two[1],
        back_two[2],
        qkv_weight,
        vis,
        vis_dx1,
        norm1_gain,
        0,
    )
    made, part.got = beside(made, part.got)
    vis_input, vis_head = made
    part = line_last(part.terms(), [0])
    made = leave(after(vis_input, part.sent), columns)
    made, part.got, second.got, line.got = beside(made, part.got, second.got, line.got)
    grad_keep, grad_send = made
    (part,) = part.terms()
    own_self = [jnp.zeros_like(back_one[6])] * 2 + [back_one[6], back_two[6], back_one[7], back_two[7]]
    own_dqkv = added(mapped(lambda term: term[0], part) + [jnp.stack(own_self)])
    masks = line_masks()
    lined = own_dqkv[None]
    for mask in reversed(masks[1:-1]):
        lined = Gather([lined], [1], "strip", mask).pairs()[0]
        lined = lined.reshape((-1,) + own_dqkv.shape)
    lined = Gather([lined], [0], "strip", masks[-1])
    qkv = Phase(
        [after(terms, lined.sent) for terms in first.terms() + second.terms()], [2, 2], "page", 2
    )
    made = input_grad(
        untiled(after(own_dqkv, lined.sent, qkv.sent)[0:2]),
        untiled(own_dqkv[2:4]),
        untiled(own_dqkv[4:6]),
        qkv_weight,
        query_tokens[0],
        own_rows(query_dx1),
        norm1_gain,
        1,
    )
    made, lined.got, early.got = beside(made, lined.got, early.got)
    own_input, own_head = made
    lined = lined.pairs()[0].reshape((-1,) + own_dqkv.shape)
    lined = Gather([lined], [1], "strip", masks[0])
    one, down = after(early.pairs(), lined.sent)
    down = Gather([down], [1], "page", 2)

    small = jnp.concatenate([vis_sums, vis_head + own_head], 0)
    small_others = other_core(small)
    lined.got, small_others, qkv.got = beside(lined.got, small_others, qkv.got)
    small = small + small_others
    lined = lined.pairs()[0].reshape((-1,) + own_dqkv.shape)
    lined_others = other_core(lined)
    grad_first = moved(after(grad_send, lined), "strip", 1)
    for mask in masks[:-2]:
        small = small + swapped(small, "strip", mask)
    small_others = swapped(small, "strip", masks[-2])
    qkv = line_first(after(qkv.terms(), lined), [0, 0])
    up_part, low_part = line.sums()
    up_gather = Gather([after(up_part, lined)[:, 0], low_part[:, 0]], [1, 1], "page", 1)
    lined_others, small_others, down.got = beside(lined_others, small_others, down.got)
    one_first = Gather([after(one, down.got)[:5]], [1], "page", 2)
    small = small + small_others
    query_dqkv = jnp.stack(
        [jnp.where(core == 0, lined, lined_others), jnp.where(core == 0, lined_others, lined)], 1
    )
    query_dqkv = [query_dqkv[:, :, i].reshape(query_count, -1) for i in range(6)]
    three = query_grads(query_norm, jnp.concatenate(query_dqkv, 1))
    three = Phase([[by_page(tiled(three, half * PAIR))]], [2], "page", 1)
    small_others = swapped(small, "strip", masks[-1])
    three.got, qkv.got, small_others, up_gather.got, one_first.got, grad_first = beside(
        three.got, qkv.got, small_others, up_gather.got, one_first.got, grad_first
    )
    three = Phase(three.terms(), [1], "page", 2)
    qkv = line_last(after(qkv.terms(), three.sent), [0, 0])
    small = jnp.concatenate([small + small_others, query_sums], 0)
    small_others = swapped(small, "page", 2)
    last = Gather([after(one, three.sent)[5:]] + up_gather.pairs(), [1, 1, 1], "page", 2)
    three.got, qkv.got, small_others = beside(three.got, qkv.got, small_others)
    late = PageGather([each[0] for each in qkv.sums()] + three.sums())
    small = small + small_others
    small_others = swapped(after(small, late.sent), "page", 1)
    small = small + small_others

    one_last, up_a, up_b = [from_page(each) for each in last.pairs()]
    (down,) = [from_page(each) for each in down.pairs()]
    one = jnp.concatenate([from_page(each) for each in one_first.pairs()] + [one_last], 0)
    up = jnp.concatenate([up_a, up_b], 0)
    up_grad = jnp.stack([untiled(up[:hidden]), untiled(one[:hidden])]).astype(f32)
    out_grad = jnp.stack([up[hidden], one[hidden]]).astype(f32)
    down_grad = jnp.stack([down, one[hidden + 1 :]]).astype(f32).reshape(2, -1, features)
    vis_final = jnp.concatenate([vis_first, vis_keep], 0)[None]
    grad_final = jnp.concatenate([grad_first, grad_keep], 0)[None]
    late.got, up_grad, out_grad, down_grad, vis_final, grad_final = beside(
        late.got, up_grad, out_grad, down_grad, vis_final, grad_final
    )
    first, second, three = late.whole()
    vis_qkv_grad = jnp.concatenate(
        [each[i] for i in range(3) for each in (first, second)], 1
    )
    qkv_grad = jnp.stack([vis_qkv_grad, untiled(three)]).astype(f32)

    count = vis_sums.shape[0]
    gain_two, bias_two, obias, dbias = [
        own_columns(jnp.stack([small[i], small[count + 8 + i]])) for i in range(4)
    ]
    gain_one, bias_one = [
        own_columns(jnp.stack([small[count + i], small[count + 4 + i]])) for i in range(2)
    ]
    ubias = jnp.stack([small[4:count].reshape(-1), small[count + 12 :].reshape(-1)])
    ubias = own_columns(ubias)

    return (
        vis_final,
        own_rows(query_result)[None],
        grad_final,
        own_input[None],
        gain_one,
        bias_one,
        qkv_grad,
        out_grad,
        obias,
        gain_two,
        bias_two,
        up_grad,
        ubias,
        down_grad,
        dbias,
    )


def solution(mesh):
    return jax.shard_map(
        body,
        mesh=mesh,
        in_specs=(
            P("page", "strip", None, None),
            P("page", "strip", None),
            P("page", None, None),
            P("page", None),
            P("page"),
            P(),
            P(),
            P(),
            P(),
            P(),
            P(),
            P(),
            P(),
            P(),
            P(),
            P(),
            P("page", "strip", None, None),
            P("page", "strip", None),
        ),
        out_specs=(
            P("page", "strip", None, None),
            P("page", "strip", None),
            P("page", "strip", None, None),
            P("page", "strip", None),
            P(None, "strip"),
            P(None, "strip"),
            P(None, "strip", None),
            P(None, "strip", None),
            P(None, "strip"),
            P(None, "strip"),
            P(None, "strip"),
            P(None, "strip", None),
            P(None, "strip"),
            P(None, "strip", None),
            P(None, "strip"),
        ),
        check_vma=False,
    )
```

```python
import functools

import jax
import jax.numpy as jnp
from jax import lax
from jax.experimental import pallas as pl
from jax.experimental.pallas import tpu as pltpu
from jax.sharding import PartitionSpec as P

HEADS = 12
WIN = 12
SHIFT = 6
CELLS = WIN * WIN
PAIR = 128
MASKED = -1000000000.0
MIB = 1024 * 1024

bf16 = jnp.bfloat16
f32 = jnp.float32


def params(mib):
    return pltpu.CompilerParams(vmem_limit_bytes=min(int(mib), 56) * MIB)


def row_block(rows):
    for size in range(336, 15, -16):
        if rows % size == 0:
            return size
    return rows


def dot_nn(a, b):
    return lax.dot_general(a, b, (((1,), (0,)), ((), ())), preferred_element_type=f32)


def dot_nt(a, b):
    return lax.dot_general(a, b, (((1,), (1,)), ((), ())), preferred_element_type=f32)


def dot_tn(a, b):
    return lax.dot_general(a, b, (((0,), (0,)), ((), ())), preferred_element_type=f32)


def cost(flops, moved, special=0):
    share = 20000
    return pl.CostEstimate(
        flops=int(flops) // share,
        bytes_accessed=int(moved) // share,
        transcendentals=int(special) // share,
    )


def whole(shape):
    return pl.BlockSpec(shape, lambda *_: (0,) * len(shape))


def once(shape, place=None):
    place = place or (lambda *_: (0,) * len(shape))
    return pl.BlockSpec(shape, place, pipeline_mode=pl.Buffered(1))


def normalised(values):
    center = values - jnp.mean(values, -1, keepdims=True)
    spread = jnp.mean(center * center, -1, keepdims=True)
    rstd = lax.rsqrt(spread + 1e-05)
    return center * rstd, rstd


def norm_back(grad, hat, rstd, gain):
    scaled = grad * gain
    mean_one = jnp.mean(scaled, -1, keepdims=True)
    mean_two = jnp.mean(scaled * hat, -1, keepdims=True)
    return rstd * (scaled - mean_one - hat * mean_two)


def enter_kernel(own_ref, head_ref, out_ref, row_ref, cells_ref):
    columns = own_ref.shape[1]
    for r in range(WIN):
        row = own_ref[SHIFT + r] if r < WIN - SHIFT else head_ref[r - (WIN - SHIFT)]
        row_ref[0:columns, :] = row.astype(f32)
        row_ref[columns : columns + SHIFT, :] = row_ref[0:SHIFT, :]
        for w in range(columns // WIN):
            at = w * CELLS + r * WIN
            cells_ref[at : at + WIN, :] = row_ref[w * WIN + SHIFT : (w + 1) * WIN + SHIFT, :]
    for w in range(columns // WIN):
        at = slice(w * CELLS, (w + 1) * CELLS)
        out_ref[at, :] = cells_ref[at, :].astype(bf16)


def enter(own, head):
    rows, columns, width = own.shape
    cells = rows * columns
    return pl.pallas_call(
        enter_kernel,
        out_shape=jax.ShapeDtypeStruct((cells, width), bf16),
        scratch_shapes=[
            pltpu.VMEM((columns + 2 * WIN, width), f32),
            pltpu.VMEM((cells, width), f32),
        ],
        compiler_params=params(14),
        cost_estimate=cost(0, 4 * cells * width),
        name="enter",
    )(own, head)


def leave_kernel(cells_ref, keep_ref, send_ref, row_ref, wide_ref):
    columns = keep_ref.shape[1]
    for w in range(columns // WIN):
        at = slice(w * CELLS, (w + 1) * CELLS)
        wide_ref[at, :] = cells_ref[at, :].astype(f32)
    for r in range(WIN):
        for w in range(columns // WIN):
            at = w * CELLS + r * WIN
            row_ref[w * WIN + SHIFT : (w + 1) * WIN + SHIFT, :] = wide_ref[at : at + WIN, :]
        row_ref[0:SHIFT, :] = row_ref[columns : columns + SHIFT, :]
        row = row_ref[0:columns, :].astype(bf16)
        if r < WIN - SHIFT:
            keep_ref[r] = row
        else:
            send_ref[r - (WIN - SHIFT)] = row


def leave(cells, columns):
    width = cells.shape[1]
    return pl.pallas_call(
        leave_kernel,
        out_shape=[
            jax.ShapeDtypeStruct((WIN - SHIFT, columns, width), bf16),
            jax.ShapeDtypeStruct((SHIFT, columns, width), bf16),
        ],
        scratch_shapes=[
            pltpu.VMEM((columns + 2 * WIN, width), f32),
            pltpu.VMEM(cells.shape, f32),
        ],
        compiler_params=params(14),
        cost_estimate=cost(0, 4 * cells.size),
        name="leave",
    )(cells)


def qkv_kernel(stream, x_ref, gain_ref, bias_ref, w_ref, a_ref, out_ref):
    rows, width = x_ref.shape
    block = row_block(rows)
    row = slice(stream, stream + 1)
    ats = [slice(i * block, (i + 1) * block) for i in range(rows // block)]

    @pl.when(pl.program_id(0) == 0)
    def _():
        for at in ats:
            hat, _ = normalised(x_ref[at, :].astype(f32))
            low = (hat * gain_ref[row, :] + bias_ref[row, :]).astype(bf16)
            a_ref[at, :] = low
            out_ref[at, :] = dot_nn(low, w_ref[...]).astype(bf16)

    @pl.when(pl.program_id(0) != 0)
    def _():
        for at in ats:
            out_ref[at, :] = dot_nn(a_ref[at, :], w_ref[...]).astype(bf16)


def norm_qkv(x, gain, bias, weight, stream):
    rows, width = x.shape
    full = weight.shape[-1]
    return pl.pallas_call(
        functools.partial(qkv_kernel, stream),
        grid=(full // width,),
        in_specs=[
            whole((rows, width)),
            whole(gain.shape),
            whole(bias.shape),
            pl.BlockSpec((None, width, width), lambda j: (stream, 0, j)),
        ],
        out_specs=[whole((rows, width)), pl.BlockSpec((rows, width), lambda j: (0, j))],
        out_shape=[
            jax.ShapeDtypeStruct((rows, width), bf16),
            jax.ShapeDtypeStruct((rows, full), bf16),
        ],
        compiler_params=params(8 + rows // 80),
        cost_estimate=cost(2 * rows * width * full, 2 * rows * (2 * width + full) + 2 * width * full),
        name="norm_qkv",
    )(x, gain, bias, weight)


def first_half(shape):
    return lax.broadcasted_iota(jnp.int32, shape, len(shape) - 1) < PAIR // 2


def stacked(block):
    left = first_half(block.shape)
    zero = jnp.zeros_like(block)
    return jnp.concatenate([jnp.where(left, block, zero), jnp.where(left, zero, block)], 0)


def row_sums(values):
    ones = jnp.ones((8, PAIR), f32)
    return lax.dot_general(
        ones,
        values,
        (((1,), (1,)), ((), ())),
        precision=lax.Precision.HIGHEST,
        preferred_element_type=f32,
    )[:1]


def joined(upright):
    rows = upright.shape[0] // 2
    return jnp.where(first_half((rows, PAIR)), upright[:rows], upright[rows:])


def unstacked(turned):
    return joined(turned.T)


def query_forward_kernel(
    qq_ref, k_ref, v_ref, ko_ref, vo_ref, bias_ref, out_ref, stats_ref, s_ref, lse_ref
):
    queries = qq_ref.shape[0]
    cells = k_ref.shape[0]
    own = ko_ref.shape[0]
    scaled = stacked(qq_ref[...] * 0.125)
    bias = bias_ref[...]
    self_score = dot_nt(ko_ref[...], scaled) + jnp.concatenate([bias, bias], 1)
    top = jnp.max(self_score, 0, keepdims=True)
    block = row_block(cells)
    blocks = [slice(i * block, (i + 1) * block) for i in range(cells // block)]
    for at in blocks:
        score = dot_nt(k_ref[at, :], scaled)
        s_ref[at, :] = score
        top = jnp.maximum(top, jnp.max(score, 0, keepdims=True))
    prob = jnp.exp(self_score - top)
    total = jnp.sum(prob, 0, keepdims=True)
    mixed = dot_nn(vo_ref[...].T, prob.astype(bf16))
    for at in blocks:
        prob = jnp.exp(s_ref[at, :] - top)
        total = total + jnp.sum(prob, 0, keepdims=True)
        mixed = mixed + dot_nn(v_ref[at, :].T, prob.astype(bf16))
    out_ref[...] = unstacked(mixed * (1.0 / total))
    lse = top + jnp.log(total)
    pair = pl.program_id(0)

    @pl.when(pair == 0)
    def _():
        lse_ref[...] = jnp.zeros_like(lse_ref)

    lse_ref[pl.ds(2 * pair, 1), :] = lse[:, :queries]
    lse_ref[pl.ds(2 * pair + 1, 1), :] = lse[:, queries:]

    @pl.when(pair == pl.num_programs(0) - 1)
    def _():
        stats_ref[...] = lse_ref[...].T


def query_forward(query_qkv, own_qkv, vis_qkv, self_bias):
    cells = vis_qkv.shape[0]
    queries = query_qkv.shape[0]
    own = own_qkv.shape[0]
    width = query_qkv.shape[1] // 3
    pairs = width // PAIR
    keys = cells + own

    def part(rows, j):
        return pl.BlockSpec((rows, PAIR), lambda p, j=j: (0, j * pairs + p))

    return pl.pallas_call(
        query_forward_kernel,
        grid=(pairs,),
        in_specs=[
            part(queries, 0),
            part(cells, 1),
            part(cells, 2),
            part(own, 1),
            part(own, 2),
            whole(self_bias.shape),
        ],
        out_specs=[part(queries, 0), whole((queries, PAIR))],
        out_shape=[
            jax.ShapeDtypeStruct((queries, width), f32),
            jax.ShapeDtypeStruct((queries, PAIR), f32),
        ],
        scratch_shapes=[
            pltpu.VMEM((cells, 2 * queries), f32),
            pltpu.VMEM((PAIR, queries), f32),
        ],
        compiler_params=params(10 + queries // 32),
        cost_estimate=cost(
            4 * 2 * queries * keys * width, 4 * cells * width, 2 * queries * keys * pairs
        ),
        name="query_forward",
    )(query_qkv, vis_qkv, vis_qkv, own_qkv, own_qkv, self_bias)


def window_forward_kernel(
    windows,
    q_ref,
    k_ref,
    v_ref,
    kq_ref,
    vq_ref,
    row_ref,
    col_ref,
    open_ref,
    out_ref,
    lse_ref,
    scaled_ref,
    near_ref,
    mixed_ref,
    far_ref,
):
    cells = [slice(w * CELLS, (w + 1) * CELLS) for w in range(windows)]
    lanes = [slice(2 * w * CELLS, 2 * (w + 1) * CELLS) for w in range(windows)]
    tops = []
    for w in range(windows):
        scaled = stacked(q_ref[cells[w], :] * 0.125)
        scaled_ref[lanes[w], :] = scaled
        near = dot_nt(k_ref[cells[w], :], scaled)
        near = jnp.where(col_ref[w] == row_ref[w], near, MASKED)
        near_ref[w] = near
        tops.append(jnp.max(near, 0, keepdims=True))
    far = dot_nt(kq_ref[...], scaled_ref[...]) + open_ref[...]
    top = jnp.maximum(jnp.concatenate(tops, 1), jnp.max(far, 0, keepdims=True))
    far = jnp.exp(far - top)
    total = jnp.sum(far, 0, keepdims=True)
    far_mixed = dot_nn(vq_ref[...].T, far.astype(bf16))
    totals = []
    for w in range(windows):
        near = jnp.exp(near_ref[w] - top[:, lanes[w]])
        totals.append(jnp.sum(near, 0, keepdims=True))
        mixed_ref[w] = dot_nn(v_ref[cells[w], :].T, near.astype(bf16))
    total = total + jnp.concatenate(totals, 1)
    share = 1.0 / total
    lse_ref[...] = top + jnp.log(total)
    far_ref[...] = far_mixed
    for w in range(windows):
        turned = (mixed_ref[w] + far_ref[:, lanes[w]]) * share[:, lanes[w]]
        out_ref[cells[w], :] = joined(turned.astype(bf16).T)


def window_forward(vis_qkv, query_qkv, region_row, region_col, closed):
    cells = vis_qkv.shape[0]
    queries = query_qkv.shape[0]
    width = vis_qkv.shape[1] // 3
    pairs = width // PAIR
    windows = cells // CELLS

    def part(rows, j):
        return pl.BlockSpec((rows, PAIR), lambda p, j=j: (0, j * pairs + p))

    return pl.pallas_call(
        functools.partial(window_forward_kernel, windows),
        grid=(pairs,),
        in_specs=[
            part(cells, 0),
            part(cells, 1),
            part(cells, 2),
            part(queries, 1),
            part(queries, 2),
            whole(region_row.shape),
            whole(region_col.shape),
            whole(closed.shape),
        ],
        out_specs=[
            part(cells, 0),
            pl.BlockSpec((None, 1, 2 * cells), lambda p: (p, 0, 0)),
        ],
        out_shape=[
            jax.ShapeDtypeStruct((cells, width), bf16),
            jax.ShapeDtypeStruct((pairs, 1, 2 * cells), f32),
        ],
        scratch_shapes=[
            pltpu.VMEM((2 * cells, PAIR), bf16),
            pltpu.VMEM((windows, CELLS, 2 * CELLS), f32),
            pltpu.VMEM((windows, PAIR, 2 * CELLS), f32),
            pltpu.VMEM((PAIR, 2 * cells), f32),
        ],
        compiler_params=params(12 + queries // 28),
        cost_estimate=cost(
            8 * cells * (CELLS + queries) * width,
            8 * cells * width,
            2 * pairs * cells * (CELLS + queries),
        ),
        name="window_forward",
    )(vis_qkv, vis_qkv, vis_qkv, query_qkv, query_qkv, region_row, region_col, closed)


def attention_backward_kernel(
    windows,
    first,
    q_ref,
    k_ref,
    v_ref,
    do_ref,
    qq_ref,
    kq_ref,
    vq_ref,
    doq_ref,
    ko_ref,
    vo_ref,
    row_ref,
    col_ref,
    open_ref,
    bias_ref,
    lse_ref,
    lseq_ref,
    mixq_ref,
    *rest,
):
    if len(rest) > 16:
        rest = rest[3:]
    attention_backward_body(
        windows,
        first,
        q_ref,
        k_ref,
        v_ref,
        do_ref,
        qq_ref,
        kq_ref,
        vq_ref,
        doq_ref,
        ko_ref,
        vo_ref,
        row_ref,
        col_ref,
        open_ref,
        bias_ref,
        lse_ref,
        lseq_ref,
        mixq_ref,
        *rest,
    )


def attention_backward_body(
    windows,
    first,
    q_ref,
    k_ref,
    v_ref,
    do_ref,
    qq_ref,
    kq_ref,
    vq_ref,
    doq_ref,
    ko_ref,
    vo_ref,
    row_ref,
    col_ref,
    open_ref,
    bias_ref,
    lse_ref,
    lseq_ref,
    mixq_ref,
    dq_ref,
    dk_ref,
    dv_ref,
    dqq_ref,
    dkq_ref,
    dvq_ref,
    dko_ref,
    dvo_ref,
    scaled_ref,
    grad_ref,
    near_ref,
    neart_ref,
    seenk_ref,
    seenv_ref,
    far_ref,
    stats_ref,
):
    cells = [slice(w * CELLS, (w + 1) * CELLS) for w in range(windows)]
    lanes = [slice(2 * w * CELLS, 2 * (w + 1) * CELLS) for w in range(windows)]
    lse = lse_ref[...]

    deltas = []
    for w in range(windows):
        scaled = stacked(q_ref[cells[w], :] * 0.125)
        grad = stacked(do_ref[cells[w], :])
        scaled_ref[lanes[w], :] = scaled
        grad_ref[lanes[w], :] = grad
        near = dot_nt(k_ref[cells[w], :], scaled)
        near = jnp.exp(jnp.where(col_ref[w] == row_ref[w], near, MASKED) - lse[:, lanes[w]])
        near_t = near * dot_nt(v_ref[cells[w], :], grad)
        near_ref[w] = near
        neart_ref[w] = near_t
        deltas.append(jnp.sum(near_t, 0, keepdims=True))
    kq = kq_ref[...]
    far = jnp.exp(dot_nt(kq, scaled_ref[...]) + open_ref[...] - lse)
    far_t = far * dot_nt(vq_ref[...], grad_ref[...])
    delta = jnp.concatenate(deltas, 1) + jnp.sum(far_t, 0, keepdims=True)
    far_d = (far_t - far * delta).astype(bf16)
    dkq_ref[...] = dot_nn(far_d, scaled_ref[...]).astype(bf16)
    dvq_ref[...] = dot_nn(far.astype(bf16), grad_ref[...]).astype(bf16)
    far_ref[...] = dot_nn(kq.T, far_d).T

    scaled_q = stacked(qq_ref[...] * 0.125)
    grad_q = stacked(doq_ref[...])
    stats_ref[...] = lseq_ref[...].T
    head = 2 * (first + pl.program_id(0))
    lse_q = jnp.concatenate(
        [stats_ref[pl.ds(head, 1), :], stats_ref[pl.ds(head + 1, 1), :]], 1
    )
    mix_q = mixq_ref[...]
    delta_q = row_sums(grad_q.astype(f32) * jnp.concatenate([mix_q, mix_q], 0))
    bias = bias_ref[...]
    prob = jnp.exp(dot_nt(ko_ref[...], scaled_q) + jnp.concatenate([bias, bias], 1) - lse_q)
    dscore = (prob * (dot_nt(vo_ref[...], grad_q) - delta_q)).astype(bf16)
    dko_ref[...] = dot_nn(dscore, scaled_q)
    dvo_ref[...] = dot_nn(prob.astype(bf16), grad_q)
    turned = dot_nn(ko_ref[...].T, dscore)
    rows = k_ref.shape[0]
    block = row_block(rows)
    for i in range(rows // block):
        at = slice(i * block, (i + 1) * block)
        k_rows = k_ref[at, :]
        prob = jnp.exp(dot_nt(k_rows, scaled_q) - lse_q)
        dscore = (prob * (dot_nt(v_ref[at, :], grad_q) - delta_q)).astype(bf16)
        seenk_ref[at, :] = dot_nn(dscore, scaled_q)
        seenv_ref[at, :] = dot_nn(prob.astype(bf16), grad_q)
        turned = turned + dot_nn(k_rows.T, dscore)
    dqq_ref[...] = (unstacked(turned) * 0.125).astype(bf16)

    for w in range(windows):
        near = near_ref[w]
        near_d = (neart_ref[w] - near * delta[:, lanes[w]]).astype(bf16)
        upright = dot_nn(k_ref[cells[w], :].T, near_d).T + far_ref[lanes[w], :]
        dq_ref[cells[w], :] = (joined(upright) * 0.125).astype(bf16)
        dk_ref[cells[w], :] = (
            dot_nn(near_d, scaled_ref[lanes[w], :]) + seenk_ref[cells[w], :]
        ).astype(bf16)
        dv_ref[cells[w], :] = (
            dot_nn(near.astype(bf16), grad_ref[lanes[w], :]) + seenv_ref[cells[w], :]
        ).astype(bf16)


def attention_backward(
    vis_qkv,
    query_qkv,
    own_qkv,
    grad,
    grad_q,
    region_row,
    region_col,
    closed,
    self_bias,
    lse,
    joint_q,
    first,
    count,
    begun=(),
):
    cells = vis_qkv.shape[0]
    queries = query_qkv.shape[0]
    own = own_qkv.shape[0]
    width = vis_qkv.shape[1] // 3
    pairs = width // PAIR
    windows = cells // CELLS

    def part(rows, j):
        return pl.BlockSpec((rows, PAIR), lambda p, j=j: (0, j * pairs + first + p))

    def result(rows):
        return pl.BlockSpec((rows, PAIR), lambda p: (0, p))

    def filled(rows):
        return pl.BlockSpec((rows, PAIR), lambda p: (0, first + p))

    def stats(array):
        return pl.BlockSpec((None,) + array.shape[1:], lambda p: (first + p, 0, 0))

    span = count * PAIR
    return pl.pallas_call(
        functools.partial(attention_backward_kernel, windows, first),
        grid=(count,),
        in_specs=[
            part(cells, 0),
            part(cells, 1),
            part(cells, 2),
            part(cells, 0),
            part(queries, 0),
            part(queries, 1),
            part(queries, 2),
            part(queries, 0),
            part(own, 1),
            part(own, 2),
            whole(region_row.shape),
            whole(region_col.shape),
            whole(closed.shape),
            whole(self_bias.shape),
            stats(lse),
            pl.BlockSpec((queries, PAIR), lambda p: (0, pairs)),
            part(queries, 0),
        ]
        + [pl.BlockSpec(memory_space=pl.ANY)] * len(begun),
        out_specs=[filled(cells)] * 3 + [result(queries)] * 3 + [result(own)] * 2,
        out_shape=[jax.ShapeDtypeStruct((cells, width), bf16)] * 3
        + [jax.ShapeDtypeStruct((queries, span), bf16)] * 3
        + [jax.ShapeDtypeStruct((own, span), f32)] * 2,
        scratch_shapes=[
            pltpu.VMEM((2 * cells, PAIR), bf16),
            pltpu.VMEM((2 * cells, PAIR), bf16),
            pltpu.VMEM((windows, CELLS, 2 * CELLS), f32),
            pltpu.VMEM((windows, CELLS, 2 * CELLS), f32),
            pltpu.VMEM((cells, PAIR), f32),
            pltpu.VMEM((cells, PAIR), f32),
            pltpu.VMEM((2 * cells, PAIR), f32),
            pltpu.VMEM((PAIR, queries), f32),
        ],
        compiler_params=params(16 + queries // 25),
        cost_estimate=cost(
            20 * cells * (CELLS + 2 * queries) * span,
            14 * cells * span,
            2 * count * cells * (CELLS + 2 * queries),
        ),
        input_output_aliases={17 + i: i for i in range(len(begun))},
        name="attention_backward",
    )(
        vis_qkv,
        vis_qkv,
        vis_qkv,
        grad,
        query_qkv,
        query_qkv,
        query_qkv,
        grad_q,
        own_qkv,
        own_qkv,
        region_row,
        region_col,
        closed,
        self_bias,
        lse,
        joint_q,
        joint_q,
        *begun,
    )


def gelu_pair(z):
    below = 0.5 + 0.5 * lax.erf(z * 0.7071067811865476)
    bell = jnp.exp(-0.5 * z * z)
    return z * below, below + z * bell * 0.3989422804014327


def ffn_forward_kernel(
    stream,
    x_ref,
    o_ref,
    wo_ref,
    bo_ref,
    gain_ref,
    bias_ref,
    wu_ref,
    bu_ref,
    wd_ref,
    bd_ref,
    x1_ref,
    b_ref,
    hid_ref,
    slope_ref,
    out_ref,
    sum_ref,
):
    rows, width = x_ref.shape
    block = row_block(rows)
    count = rows // block
    ats = [slice(i * block, (i + 1) * block) for i in range(count)]
    step = pl.program_id(0)
    row = slice(stream, stream + 1)

    @pl.when(step == 0)
    def _():
        for at in ats:
            x1 = x_ref[at, :].astype(f32) + dot_nn(o_ref[at, :].astype(bf16), wo_ref[...]) + bo_ref[row, :]
            x1_ref[at, :] = x1
            hat, _ = normalised(x1)
            b_ref[at, :] = (hat * gain_ref[row, :] + bias_ref[row, :]).astype(bf16)
            sum_ref[at, :] = x1 + bd_ref[row, :]

    def project(i):
        return dot_nn(b_ref[ats[i], :], wu_ref[...]) + bu_ref[row, :]

    z = project(0)
    for i in range(count):
        ahead = project(i + 1) if i + 1 < count else None
        hidden, slope = gelu_pair(z)
        hidden = hidden.astype(bf16)
        hid_ref[ats[i], :] = hidden
        slope_ref[ats[i], :] = slope.astype(bf16)
        sum_ref[ats[i], :] += dot_nn(hidden, wd_ref[...])
        z = ahead

    @pl.when(step == pl.num_programs(0) - 1)
    def _():
        out_ref[...] = sum_ref[...].astype(bf16)


def ffn_forward(x, attended, out_w, out_b, gain, bias, up_w, up_b, down_w, down_b, stream):
    rows, width = x.shape
    hidden = up_w.shape[-1]
    chunk = 768
    return pl.pallas_call(
        functools.partial(ffn_forward_kernel, stream),
        grid=(hidden // chunk,),
        in_specs=[
            once((rows, width)),
            once((rows, width)),
            once((None, width, width), lambda f: (stream, 0, 0)),
            whole(out_b.shape),
            whole(gain.shape),
            whole(bias.shape),
            pl.BlockSpec((None, width, chunk), lambda f: (stream, 0, f)),
            pl.BlockSpec((2, chunk), lambda f: (0, f)),
            pl.BlockSpec((None, chunk, width), lambda f: (stream, f, 0)),
            whole(down_b.shape),
        ],
        out_specs=[
            whole((rows, width)),
            whole((rows, width)),
            pl.BlockSpec((rows, chunk), lambda f: (0, f)),
            pl.BlockSpec((rows, chunk), lambda f: (0, f)),
            whole((rows, width)),
        ],
        out_shape=[
            jax.ShapeDtypeStruct((rows, width), f32),
            jax.ShapeDtypeStruct((rows, width), bf16),
            jax.ShapeDtypeStruct((rows, hidden), bf16),
            jax.ShapeDtypeStruct((rows, hidden), bf16),
            jax.ShapeDtypeStruct((rows, width), bf16),
        ],
        scratch_shapes=[pltpu.VMEM((rows, width), f32)],
        compiler_params=params(34 if stream == 0 else 56),
        cost_estimate=cost(
            2 * rows * width * (2 * hidden + width),
            4 * width * hidden + 4 * rows * hidden + 12 * rows * width,
            2 * rows * hidden,
        ),
        name="ffn_forward",
    )(x, attended, out_w, out_b, gain, bias, up_w, up_b, down_w, down_b)


def ffn_backward_kernel(
    stream,
    g_ref,
    slope_ref,
    x1_ref,
    wd_ref,
    wu_ref,
    wo_ref,
    gain_ref,
    dz_ref,
    dx1_ref,
    du_ref,
    do_ref,
    sums_ref,
    sum_ref,
):
    rows, width = g_ref.shape
    block = row_block(rows)
    count = rows // block
    ats = [slice(i * block, (i + 1) * block) for i in range(count)]
    step = pl.program_id(0)
    row = slice(stream, stream + 1)

    @pl.when(step == 0)
    def _():
        sum_ref[...] = jnp.zeros_like(sum_ref)

    up_bias = jnp.zeros((1, dz_ref.shape[1]), f32)

    def pulled(i):
        return dot_nt(g_ref[ats[i], :], wd_ref[...])

    grad = pulled(0)
    for i in range(count):
        ahead = pulled(i + 1) if i + 1 < count else None
        dz = grad * slope_ref[ats[i], :].astype(f32)
        low = dz.astype(bf16)
        dz_ref[ats[i], :] = low
        up_bias = up_bias + jnp.sum(dz, 0, keepdims=True)
        sum_ref[ats[i], :] += dot_nt(low, wu_ref[...])
        grad = ahead
    sums_ref[pl.ds(4 + step, 1), :] = up_bias

    @pl.when(step == pl.num_programs(0) - 1)
    def _():
        sums_ref[0:4, :] = jnp.zeros((4, width), f32)
        for at in ats:
            hat, rstd = normalised(x1_ref[at, :])
            db = sum_ref[at, :]
            g = g_ref[at, :].astype(f32)
            dx1 = g + norm_back(db, hat, rstd, gain_ref[row, :])
            dx1_ref[at, :] = dx1
            du = dx1.astype(bf16)
            du_ref[at, :] = du
            do_ref[at, :] = dot_nt(du, wo_ref[...]).astype(bf16)
            sums_ref[0:1, :] += jnp.sum(db * hat, 0, keepdims=True)
            sums_ref[1:2, :] += jnp.sum(db, 0, keepdims=True)
            sums_ref[2:3, :] += jnp.sum(dx1, 0, keepdims=True)
            sums_ref[3:4, :] += jnp.sum(g, 0, keepdims=True)


def ffn_backward(g, slope, x1, down_w, up_w, out_w, gain, stream):
    rows, width = g.shape
    hidden = up_w.shape[-1]
    chunk = width
    return pl.pallas_call(
        functools.partial(ffn_backward_kernel, stream),
        grid=(hidden // chunk,),
        in_specs=[
            once((rows, width)),
            pl.BlockSpec((rows, chunk), lambda f: (0, f)),
            once((rows, width)),
            pl.BlockSpec((None, chunk, width), lambda f: (stream, f, 0)),
            pl.BlockSpec((None, width, chunk), lambda f: (stream, 0, f)),
            once((None, width, width), lambda f: (stream, 0, 0)),
            whole(gain.shape),
        ],
        out_specs=[
            pl.BlockSpec((None, rows, chunk), lambda f: (f, 0, 0)),
            whole((rows, width)),
            whole((rows, width)),
            whole((rows, width)),
            whole((4 + hidden // chunk, width)),
        ],
        out_shape=[
            jax.ShapeDtypeStruct((hidden // chunk, rows, chunk), bf16),
            jax.ShapeDtypeStruct((rows, width), f32),
            jax.ShapeDtypeStruct((rows, width), bf16),
            jax.ShapeDtypeStruct((rows, width), bf16),
            jax.ShapeDtypeStruct((4 + hidden // chunk, width), f32),
        ],
        scratch_shapes=[pltpu.VMEM((rows, width), f32)],
        compiler_params=params(34 if stream == 0 else 56),
        cost_estimate=cost(
            2 * rows * width * (2 * hidden + width),
            4 * width * hidden + 4 * rows * hidden + 14 * rows * width,
        ),
        name="ffn_backward",
    )(g, slope, x1, down_w, up_w, out_w, gain)


def input_kernel(stream, dq_ref, dk_ref, dv_ref, w_ref, x_ref, dx1_ref, gain_ref, out_ref, sums_ref):
    width = x_ref.shape[1]

    @pl.when(pl.program_id(0) == 0)
    def _():
        sums_ref[...] = jnp.zeros_like(sums_ref)

    grad = dot_nt(dq_ref[...], w_ref[:, :width])
    grad = grad + dot_nt(dk_ref[...], w_ref[:, width : 2 * width])
    grad = grad + dot_nt(dv_ref[...], w_ref[:, 2 * width :])
    hat, rstd = normalised(x_ref[...].astype(f32))
    out_ref[...] = (
        dx1_ref[...] + norm_back(grad, hat, rstd, gain_ref[stream : stream + 1, :])
    ).astype(bf16)
    at = 4 * stream
    sums_ref[at : at + 1, :] += jnp.sum(grad * hat, 0, keepdims=True)
    sums_ref[at + 1 : at + 2, :] += jnp.sum(grad, 0, keepdims=True)


def input_grad(dq, dk, dv, weight, x, dx1, gain, stream):
    rows, width = x.shape
    block = row_block(rows)
    rows_spec = pl.BlockSpec((block, width), lambda i: (i, 0))
    return pl.pallas_call(
        functools.partial(input_kernel, stream),
        grid=(rows // block,),
        in_specs=[rows_spec] * 3
        + [
            pl.BlockSpec((None, width, 3 * width), lambda i: (stream, 0, 0)),
            rows_spec,
            rows_spec,
            whole(gain.shape),
        ],
        out_specs=[rows_spec, whole((8, width))],
        out_shape=[
            jax.ShapeDtypeStruct((rows, width), bf16),
            jax.ShapeDtypeStruct((8, width), f32),
        ],
        compiler_params=params(16),
        cost_estimate=cost(6 * rows * width * width, 14 * rows * width + 6 * width * width),
        name="input_grad",
    )(dq, dk, dv, weight, x, dx1, gain)


def after(value, *before):
    return lax.optimization_barrier((value,) + before)[0]


def beside(made, *flights):
    return lax.optimization_barrier((made,) + flights)


def moved(block, axis, step):
    size = lax.axis_size(axis)
    return lax.ppermute(block, axis, [(i, (i + step) % size) for i in range(size)])


def swapped(block, axis, mask):
    size = lax.axis_size(axis)
    return lax.ppermute(block, axis, [(i, i ^ mask) for i in range(size)])


def other_core(block):
    return swapped(block, "strip", 1)


def place():
    strip = lax.axis_index("strip")
    return lax.axis_size("strip") // 2, strip // 2, strip % 2


def pick(block, index, axis=0):
    return lax.dynamic_index_in_dim(block, index, axis, keepdims=False)


def added(blocks, kind=bf16):
    total = blocks[0].astype(f32)
    for block in blocks[1:]:
        total = total + block.astype(f32)
    return total.astype(kind)


def bit_of(axis, mask):
    return (lax.axis_index(axis) // mask) % 2


class Phase:
    def __init__(self, blocks, dims, axis, mask):
        bit = bit_of(axis, mask)
        theirs, self.mine = [
            [added([pick(term, half, dim) for term in terms]) for terms, dim in zip(blocks, dims)]
            for half in (1 - bit, bit)
        ]
        self.shapes = [block.shape for block in theirs]
        self.sent, self.got = exchange(theirs, axis, mask)

    def terms(self):
        got = parted(self.got, self.shapes)
        return [[mine, more] for mine, more in zip(self.mine, got)]

    def sums(self):
        return [added(terms) for terms in self.terms()]


def mapped(change, terms):
    return [change(term) for term in terms]


class Gather:
    def __init__(self, blocks, dims, axis, mask):
        self.bit = bit_of(axis, mask)
        self.blocks, self.dims = blocks, dims
        self.shapes = [block.shape for block in blocks]
        self.sent, self.got = exchange(blocks, axis, mask)

    def pairs(self):
        first = self.bit == 0
        return [
            jnp.stack([jnp.where(first, one, two), jnp.where(first, two, one)], dim)
            for one, two, dim in zip(self.blocks, parted(self.got, self.shapes), self.dims)
        ]


class PageGather:
    def __init__(self, blocks):
        self.shapes = [block.shape for block in blocks]
        rows = [block.reshape(-1, block.shape[-1]) for block in blocks]
        self.sent = jnp.concatenate(rows, 0)
        self.got = [swapped(self.sent, "page", mask) for mask in (1, 2, 3)]

    def whole(self):
        def ordered(bit, one, two, axis):
            first = bit == 0
            return jnp.stack([jnp.where(first, one, two), jnp.where(first, two, one)], axis)

        every = [parted(rows, self.shapes) for rows in [self.sent] + list(self.got)]
        result = []
        for mine, by_x, by_y, by_both in zip(*every):
            near = ordered(bit_of("page", 1), mine, by_x, 1)
            far = ordered(bit_of("page", 1), by_y, by_both, 1)
            result.append(from_page(ordered(bit_of("page", 2), near, far, 1)))
        return result


def parted(rows, shapes):
    if len(shapes) == 1:
        return [rows]
    blocks, at = [], 0
    for shape in shapes:
        count = 1
        for size in shape[:-1]:
            count *= size
        blocks.append(rows[at : at + count].reshape(shape))
        at += count
    return blocks


def exchange(blocks, axis, mask):
    if len(blocks) == 1:
        sent = blocks[0]
    else:
        sent = jnp.concatenate([block.reshape(-1, block.shape[-1]) for block in blocks], 0)
    return sent, swapped(sent, axis, mask)


def by_core(grad):
    strips = lax.axis_size("strip")
    return grad.reshape(strips // 2, 2, grad.shape[0] // strips, grad.shape[1])


def tiled(grad, width):
    count = grad.shape[-1] // width
    return jnp.stack([grad[..., i * width : (i + 1) * width] for i in range(count)], -3)


def untiled(blocks):
    return jnp.concatenate([blocks[i] for i in range(blocks.shape[0])], -1)


def by_page(blocks):
    rows = blocks.shape[-2]
    return blocks.reshape(blocks.shape[:-2] + (2, 2, rows // 4, blocks.shape[-1]))


def from_page(blocks):
    return blocks.reshape(blocks.shape[:-4] + (-1, blocks.shape[-1]))


def by_chip(blocks, axis):
    shape = blocks.shape
    return blocks.reshape(shape[:axis] + (shape[axis] // 2, 2) + shape[axis + 1 :])


def line_masks():
    size, _, _ = place()
    return [2 << i for i in range(size.bit_length() - 1)]


def line_phase(blocks, axes, mask):
    split = [
        [by_chip(term, axis) for term in terms] for terms, axis in zip(blocks, axes)
    ]
    return Phase(split, [axis + 1 for axis in axes], "strip", mask)


def line_first(blocks, axes):
    masks = line_masks()
    for mask in masks[:-2]:
        blocks = line_phase(blocks, axes, mask).terms()
    return line_phase(blocks, axes, masks[-2])


def line_last(blocks, axes):
    return line_phase(blocks, axes, line_masks()[-1])


def line_exchange(block):
    size, z, _ = place()
    return [pick(block, z)] + [
        moved(pick(block, (z + step) % size), "strip", 2 * step) for step in range(1, size)
    ]


def line_gather(block):
    size, _, _ = place()
    return [block] + [moved(block, "strip", 2 * step) for step in range(1, size)]


def line_order(blocks):
    size, z, _ = place()
    double = jnp.stack(blocks[:1] + blocks[:0:-1] + blocks[:1] + blocks[:0:-1])
    return lax.dynamic_slice_in_dim(double, (size - z) % size, size, 0)


def page_exchange(block):
    size = lax.axis_size("page")
    page = lax.axis_index("page")
    shares = block.reshape(size, block.shape[0] // size, block.shape[1])
    return [pick(shares, page)] + [
        swapped(pick(shares, page ^ mask), "page", mask) for mask in range(1, size)
    ]


def page_gather(block):
    size = lax.axis_size("page")
    return [block] + [swapped(block, "page", mask) for mask in range(1, size)]


def page_order(blocks):
    size = len(blocks)
    page = lax.axis_index("page")
    rows, columns = blocks[0].shape
    joined = jnp.zeros((size * rows, columns), f32)
    for mask, block in enumerate(blocks):
        joined = lax.dynamic_update_slice_in_dim(
            joined, block.astype(f32), (page ^ mask) * rows, 0
        )
    return joined


def core_order(mine, other):
    _, _, core = place()
    pair = jnp.stack(
        [jnp.where(core == 0, mine, other), jnp.where(core == 0, other, mine)], 1
    )
    return pair.reshape(-1, pair.shape[-1])


def merge_kernel(one_ref, two_ref, out_ref):
    width = one_ref.shape[1] - PAIR
    one_top = one_ref[:, width:]
    two_top = two_ref[:, width:]
    top = jnp.maximum(one_top, two_top)
    one_share = jnp.exp(one_top - top)
    two_share = jnp.exp(two_top - top)
    total = one_share + two_share
    shape = (PAIR, width)
    head = lax.broadcasted_iota(jnp.int32, shape, 1) // (width // HEADS)
    spread = (lax.broadcasted_iota(jnp.int32, shape, 0) == head).astype(f32)

    def over_heads(share):
        return jnp.dot(share / total, spread, precision=lax.Precision.HIGHEST)

    out_ref[:, :width] = one_ref[:, :width] * over_heads(one_share) + two_ref[
        :, :width
    ] * over_heads(two_share)
    out_ref[:, width:] = top + jnp.log(total)


def merged(one, two):
    shape = one.shape
    rows = one.size // shape[-1]
    out = pl.pallas_call(
        merge_kernel,
        out_shape=jax.ShapeDtypeStruct((rows, shape[-1]), f32),
        compiler_params=params(8),
        cost_estimate=cost(6 * one.size, 12 * one.size),
        name="merge",
    )(one.reshape(rows, -1), two.reshape(rows, -1))
    return out.reshape(shape)


def region_windows(rows):
    across = rows.shape[1] // WIN
    rolled = jnp.roll(rows, -SHIFT, axis=1)
    return rolled.reshape(WIN, across, WIN).transpose(1, 0, 2).reshape(across, CELLS)


def weight_grad(left, right):
    return dot_tn(left, right).astype(bf16)


def body(
    vis_tokens,
    query_tokens,
    region_ids,
    query_mask,
    answer_len,
    norm1_gain,
    norm1_bias,
    qkv_weight,
    out_weight,
    out_bias,
    norm2_gain,
    norm2_bias,
    up_weight,
    up_bias,
    down_weight,
    down_bias,
    vis_cotangent,
    query_cotangent,
):
    strips = lax.axis_size("strip")
    strip = lax.axis_index("strip")
    chips, z, core = place()
    local_rows, columns, features = vis_tokens.shape[1:]
    own_count = query_tokens.shape[1]
    query_count = query_mask.shape[1]
    total_rows = region_ids.shape[1]
    own_start = strip * own_count

    def own_rows(values):
        return lax.dynamic_slice_in_dim(values, own_start, own_count, 0)

    def own_columns(values):
        span = values.shape[1] // strips
        return lax.dynamic_slice_in_dim(values, strip * span, span, 1)

    tokens = line_gather(query_tokens[0])
    head_rows = moved(vis_tokens[0, :SHIFT], "strip", -1)
    tokens = line_order(tokens)
    query = core_order(tokens, other_core(tokens))

    key_open = query_mask[0] > 0
    key_ids = jnp.arange(query_count, dtype=jnp.int32)
    prompt = key_ids < query_count - answer_len[0]
    closed = jnp.where(key_open & prompt, 0.0, MASKED).astype(f32)[:, None]
    own_ids = own_start + jnp.arange(own_count, dtype=jnp.int32)
    allowed = own_rows(key_open)[:, None] & (
        own_rows(prompt)[:, None] | (own_ids[:, None] <= key_ids[None, :])
    )
    self_bias = jnp.where(allowed, 0.0, MASKED).astype(f32)
    row_ids = (strip * local_rows + SHIFT + jnp.arange(local_rows, dtype=jnp.int32)) % total_rows
    region = region_windows(jnp.take(region_ids[0], row_ids, axis=0))
    region_row = jnp.concatenate([region, region], 1)[:, None, :]
    region_col = region[:, :, None]

    query_norm, query_qkv = norm_qkv(query, norm1_gain, norm1_bias, qkv_weight, 1)
    (query_norm, query_qkv), head_rows = beside((query_norm, query_qkv), head_rows)
    own_qkv = own_rows(query_qkv)
    vis = enter(vis_tokens[0], head_rows)
    head_cot = moved(after(vis_cotangent[0, :SHIFT], vis), "strip", -1)
    vis_norm, vis_qkv = norm_qkv(vis, norm1_gain, norm1_bias, qkv_weight, 0)

    part = query_forward(query_qkv, own_qkv, vis_qkv, self_bias)
    part, head_cot = beside(part, head_cot)
    mine, theirs = [
        jnp.concatenate([pick(by_core(each), which, 1) for each in part], -1)
        for which in (core, 1 - core)
    ]
    others = other_core(theirs)
    vis_cot = enter(after(vis_cotangent[0], theirs), head_cot)
    vis_cot, mine, others = beside(vis_cot, mine, others)
    part = merged(mine, others)
    others = swapped(part, "strip", 2)

    vis_windows = window_forward(after(vis_qkv, part), query_qkv, region_row, region_col, closed)
    (vis_attn, vis_lse), part, others = beside(vis_windows, part, others)
    part = merged(part, others)
    mask = 4
    while 2 * mask < strips:
        part = merged(part, swapped(part, "strip", mask))
        mask = 2 * mask
    others = swapped(part, "strip", mask)
    cotangents = line_gather(after(query_cotangent[0], vis_attn))

    weights = (out_weight, out_bias, norm2_gain, norm2_bias, up_weight, up_bias, down_weight, down_bias)
    made = ffn_forward(vis, after(vis_attn, part), *weights, 0)
    made, part, others, cotangents = beside(made, part, others, cotangents)
    vis_x1, vis_b, vis_hid, vis_slope, vis_result = made
    part = merged(part, others)
    others = other_core(part)
    cotangents = line_order(cotangents)
    cot_others = other_core(cotangents)
    vis_down = weight_grad(after(vis_hid, part, cotangents), vis_cot)
    vis_down, part, others, cotangents, cot_others = beside(
        vis_down, part, others, cotangents, cot_others
    )
    down = by_core(vis_down)
    down = Phase([[down.reshape(chips, 2, -1, features // strips, features)]], [1], "strip", 1)

    made = ffn_backward(
        after(vis_cot, down.sent), vis_slope, vis_x1, down_weight, up_weight, out_weight, norm2_gain, 0
    )
    made, down.got = beside(made, down.got)
    vis_dz, vis_dx1, vis_du, vis_do, vis_sums = made
    (down,) = down.terms()
    down = Phase([mapped(by_page, down)], [3], "page", 1)
    hidden = up_weight.shape[-1] // features
    vis_b = after(vis_b, down.sent)
    up_a = [by_core(weight_grad(vis_b, vis_dz[i])) for i in range(hidden - 1)]
    up_a = Phase([[jnp.stack(up_a)]], [2], "strip", 1)
    up_b = [by_core(weight_grad(after(vis_b, up_a.sent), vis_dz[hidden - 1]))]
    up_b = Phase([[jnp.stack(up_b + [by_core(weight_grad(vis_attn, vis_du))])]], [2], "strip", 1)
    made = leave(after(vis_result, up_b.sent), columns)
    (vis_keep, vis_send), up_a.got, up_b.got = beside(made, up_a.got, up_b.got)
    vis_first = moved(vis_send, "strip", 1)
    up_a = line_first(up_a.terms(), [1])

    every = core_order(part, others)
    query_cot = core_order(cotangents, cot_others)
    every, up_sent = beside(every, up_a.sent)
    made = ffn_forward(query, every, *weights, 1)
    made, down.got = beside(made, down.got)
    query_x1, query_b, query_hid, query_slope, query_result = made
    (down,) = down.terms()
    down = Phase([down], [2], "page", 2)
    up_b = Phase([mapped(by_page, terms) for terms in up_b.terms()], [3], "page", 1)
    made = ffn_backward(
        query_cot,
        after(query_slope, up_b.sent, down.sent),
        query_x1,
        down_weight,
        up_weight,
        out_weight,
        norm2_gain,
        1,
    )
    made, up_a.got, up_b.got = beside(made, up_a.got, up_b.got)
    query_dz, query_dx1, query_du, query_do, query_sums = made
    (up_a,) = up_a.terms()
    (up_b,) = up_b.terms()
    up_a = Phase([mapped(by_page, up_a)], [3], "page", 1)
    up_b = Phase([up_b], [2], "page", 2)

    def query_grads(left, right):
        return weight_grad(own_columns(left), right)

    up_rows = features // strips
    query_dz = after(query_dz, up_a.sent, up_b.sent)
    one = jnp.concatenate(
        [
            jnp.stack([query_grads(query_b, query_dz[i]) for i in range(hidden)]),
            query_grads(every[:, :features].astype(bf16), query_du)[None],
            query_grads(query_hid, query_cot).reshape(-1, up_rows, features),
        ],
        0,
    )
    one, down.got = beside(one, down.got)
    one = Phase([[by_page(one)]], [2], "page", 1)
    down = line_first(down.terms(), [0])

    pairs = HEADS // 2
    half = pairs // 2

    def backward(values, first, begun=()):
        return attention_backward(
            values,
            query_qkv,
            own_qkv,
            vis_do,
            query_do,
            region_row,
            region_col,
            closed,
            self_bias,
            vis_lse,
            every,
            first,
            half,
            begun,
        )

    def head_grads(normed, grads, first):
        span = half * PAIR
        return jnp.stack(
            [
                by_core(weight_grad(normed, each[:, first * PAIR : first * PAIR + span]))
                for each in grads
            ],
            2,
        )

    back_one = backward(after(vis_qkv, one.sent, down.sent), 0)
    back_one, up_a.got, up_b.got, down.got, vis_first = beside(
        back_one, up_a.got, up_b.got, down.got, vis_first
    )
    first = Phase([[head_grads(vis_norm, back_one[:3], 0)]], [1], "strip", 1)
    first.sent, one.got = beside(first.sent, one.got)
    (up_a,) = up_a.terms()
    (one,) = one.terms()
    mixed_y = Phase([after(up_a, first.sent), one], [2, 1], "page", 2)
    up_b = line_first(up_b.terms(), [1])
    down = line_last(down.terms(), [0])
    down.sent, up_b.sent, mixed_y.sent, first.got = beside(
        down.sent, up_b.sent, mixed_y.sent, first.got
    )
    (first,) = first.terms()
    first = Phase([mapped(by_page, first)], [3], "page", 1)

    back_two = backward(
        after(vis_qkv, first.sent, mixed_y.sent, up_b.sent, down.sent), half, back_one[:3]
    )
    back_two, first.got, mixed_y.got, up_b.got, down.got = beside(
        back_two, first.got, mixed_y.got, up_b.got, down.got
    )
    part = jnp.stack(
        [by_core(each) for pair in zip(back_one[3:6], back_two[3:6]) for each in pair], 2
    )
    part = Phase([[part]], [1], "strip", 1)
    grads = head_grads(after(vis_norm, part.sent), back_two[:3], half)
    second = Phase([[grads]], [1], "strip", 1)
    second.sent, part.got = beside(second.sent, part.got)
    part = line_first(part.terms(), [0])
    up_a, one = mixed_y.terms()
    (up_b,) = up_b.terms()
    line = line_last([after(up_a, part.sent), up_b], [1, 1])
    line.sent, second.got = beside(line.sent, second.got)
    (second,) = second.terms()
    second = Phase([mapped(by_page, second)], [3], "page", 1)
    (down,) = down.sums()
    one = after(added(one), second.sent)
    early = Gather([one[:5], down[0]], [1, 1], "page", 1)
    early_y = Gather([one[5:]], [1], "page", 2)

    made = input_grad(
        after(back_two[0], part.sent, line.sent, second.sent, early.sent, early_y.sent),
        back_two[1],
        back_two[2],
        qkv_weight,
        vis,
        vis_dx1,
        norm1_gain,
        0,
    )
    made, part.got = beside(made, part.got)
    vis_input, vis_head = made
    part = line_last(part.terms(), [0])
    made = leave(after(vis_input, part.sent), columns)
    made, part.got, second.got, line.got = beside(made, part.got, second.got, line.got)
    grad_keep, grad_send = made
    (part,) = part.terms()
    own_self = [jnp.zeros_like(back_one[6])] * 2 + [back_one[6], back_two[6], back_one[7], back_two[7]]
    own_dqkv = added(mapped(lambda term: term[0], part) + [jnp.stack(own_self)])
    masks = line_masks()
    lined = own_dqkv[None]
    for mask in reversed(masks[1:-1]):
        lined = Gather([lined], [1], "strip", mask).pairs()[0]
        lined = lined.reshape((-1,) + own_dqkv.shape)
    lined = Gather([lined], [0], "strip", masks[-1])
    qkv = Phase(
        [after(terms, lined.sent) for terms in first.terms() + second.terms()], [2, 2], "page", 2
    )
    made = input_grad(
        untiled(after(own_dqkv, lined.sent, qkv.sent)[0:2]),
        untiled(own_dqkv[2:4]),
        untiled(own_dqkv[4:6]),
        qkv_weight,
        query_tokens[0],
        own_rows(query_dx1),
        norm1_gain,
        1,
    )
    made, lined.got, early.got, early_y.got = beside(made, lined.got, early.got, early_y.got)
    own_input, own_head = made
    lined = lined.pairs()[0].reshape((-1,) + own_dqkv.shape)
    lined = Gather([lined], [1], "strip", masks[0])
    one, down = after(early.pairs(), lined.sent)
    (one_b,) = after(early_y.pairs(), lined.sent)
    down = Gather([down], [1], "page", 2)

    small = jnp.concatenate([vis_sums, vis_head + own_head], 0)
    small_others = other_core(small)
    lined.got, small_others, qkv.got = beside(lined.got, small_others, qkv.got)
    small = small + small_others
    lined = lined.pairs()[0].reshape((-1,) + own_dqkv.shape)
    lined_others = other_core(lined)
    for mask in masks[:-2]:
        small = small + swapped(small, "strip", mask)
    small_others = swapped(small, "strip", masks[-2])
    qkv = line_first(after(qkv.terms(), lined), [0, 0])
    up_part, low_part = line.sums()
    up_gather = Gather([after(up_part, lined)[:, 0], low_part[:, 0]], [1, 1], "page", 1)
    grad_near = moved(after(grad_send[: SHIFT // 2], lined), "strip", 1)
    lined_others, small_others, down.got = beside(lined_others, small_others, down.got)
    one_first = Gather([after(one, down.got)], [1], "page", 2)
    small = small + small_others
    query_dqkv = jnp.stack(
        [jnp.where(core == 0, lined, lined_others), jnp.where(core == 0, lined_others, lined)], 1
    )
    query_dqkv = [query_dqkv[:, :, i].reshape(query_count, -1) for i in range(6)]
    three = query_grads(query_norm, jnp.concatenate(query_dqkv, 1))
    three = Phase([[by_page(tiled(three, half * PAIR))]], [2], "page", 1)
    small_others = swapped(small, "strip", masks[-1])
    three.got, qkv.got, small_others, up_gather.got, one_first.got, grad_near = beside(
        three.got, qkv.got, small_others, up_gather.got, one_first.got, grad_near
    )
    three = Phase(three.terms(), [1], "page", 2)
    qkv = line_last(after(qkv.terms(), three.sent), [0, 0])
    small = jnp.concatenate([small + small_others, query_sums], 0)
    last = Gather(after(up_gather.pairs(), three.sent), [1, 1], "page", 2)
    one_last = Gather([after(one_b, three.sent)], [2], "page", 1)
    three.got, qkv.got, small = beside(three.got, qkv.got, small)
    grad_far = moved(after(grad_send[SHIFT // 2 :], three.got), "strip", 1)
    small = tiled(small.astype(bf16), half * PAIR)
    late = PageGather([each[0] for each in qkv.sums()] + three.sums() + [small])

    up_a, up_b = [from_page(each) for each in last.pairs()]
    (one_last,) = [from_page(each) for each in one_last.pairs()]
    (down,) = [from_page(each) for each in down.pairs()]
    one = jnp.concatenate([from_page(each) for each in one_first.pairs()] + [one_last], 0)
    up = jnp.concatenate([up_a, up_b], 0)
    up_grad = jnp.stack([untiled(up[:hidden]), untiled(one[:hidden])]).astype(f32)
    out_grad = jnp.stack([up[hidden], one[hidden]]).astype(f32)
    down_grad = jnp.stack([down, one[hidden + 1 :]]).astype(f32).reshape(2, -1, features)
    vis_final = jnp.concatenate([vis_first, vis_keep], 0)[None]
    grad_final = jnp.concatenate([grad_near, grad_far, grad_keep], 0)[None]
    late.got, up_grad, out_grad, down_grad, vis_final, grad_final = beside(
        late.got, up_grad, out_grad, down_grad, vis_final, grad_final
    )
    first, second, three, small = late.whole()
    tiles, rows, span = small.shape
    pages = lax.axis_size("page")
    small = untiled(small.reshape(tiles, pages, rows // pages, span).astype(f32).sum(1))
    vis_qkv_grad = jnp.concatenate(
        [each[i] for i in range(3) for each in (first, second)], 1
    )
    qkv_grad = jnp.stack([vis_qkv_grad, untiled(three)]).astype(f32)

    count = vis_sums.shape[0]
    gain_two, bias_two, obias, dbias = [
        own_columns(jnp.stack([small[i], small[count + 8 + i]])) for i in range(4)
    ]
    gain_one, bias_one = [
        own_columns(jnp.stack([small[count + i], small[count + 4 + i]])) for i in range(2)
    ]
    ubias = jnp.stack([small[4:count].reshape(-1), small[count + 12 :].reshape(-1)])
    ubias = own_columns(ubias)

    return (
        vis_final,
        own_rows(query_result)[None],
        grad_final,
        own_input[None],
        gain_one,
        bias_one,
        qkv_grad,
        out_grad,
        obias,
        gain_two,
        bias_two,
        up_grad,
        ubias,
        down_grad,
        dbias,
    )


def solution(mesh):
    return jax.shard_map(
        body,
        mesh=mesh,
        in_specs=(
            P("page", "strip", None, None),
            P("page", "strip", None),
            P("page", None, None),
            P("page", None),
            P("page"),
            P(),
            P(),
            P(),
            P(),
            P(),
            P(),
            P(),
            P(),
            P(),
            P(),
            P(),
            P("page", "strip", None, None),
            P("page", "strip", None),
        ),
        out_specs=(
            P("page", "strip", None, None),
            P("page", "strip", None),
            P("page", "strip", None, None),
            P("page", "strip", None),
            P(None, "strip"),
            P(None, "strip"),
            P(None, "strip", None),
            P(None, "strip", None),
            P(None, "strip"),
            P(None, "strip"),
            P(None, "strip"),
            P(None, "strip", None),
            P(None, "strip"),
            P(None, "strip", None),
            P(None, "strip"),
        ),
        check_vma=False,
    )
```

```python
import functools

import jax
import jax.numpy as jnp
from jax import lax
from jax.experimental import pallas as pl
from jax.experimental.pallas import tpu as pltpu
from jax.sharding import PartitionSpec as P

HEADS = 12
WIN = 12
SHIFT = 6
CELLS = WIN * WIN
PAIR = 128
MASKED = -1000000000.0
MIB = 1024 * 1024

bf16 = jnp.bfloat16
f32 = jnp.float32


def params(mib):
    return pltpu.CompilerParams(vmem_limit_bytes=min(int(mib), 56) * MIB)


def row_block(rows):
    for size in range(336, 15, -16):
        if rows % size == 0:
            return size
    return rows


def dot_nn(a, b):
    return lax.dot_general(a, b, (((1,), (0,)), ((), ())), preferred_element_type=f32)


def dot_nt(a, b):
    return lax.dot_general(a, b, (((1,), (1,)), ((), ())), preferred_element_type=f32)


def dot_tn(a, b):
    return lax.dot_general(a, b, (((0,), (0,)), ((), ())), preferred_element_type=f32)


def cost(flops, moved, special=0):
    share = 20000
    return pl.CostEstimate(
        flops=int(flops) // share,
        bytes_accessed=int(moved) // share,
        transcendentals=int(special) // share,
    )


def whole(shape):
    return pl.BlockSpec(shape, lambda *_: (0,) * len(shape))


def once(shape, place=None):
    place = place or (lambda *_: (0,) * len(shape))
    return pl.BlockSpec(shape, place, pipeline_mode=pl.Buffered(1))


def normalised(values):
    center = values - jnp.mean(values, -1, keepdims=True)
    spread = jnp.mean(center * center, -1, keepdims=True)
    rstd = lax.rsqrt(spread + 1e-05)
    return center * rstd, rstd


def norm_back(grad, hat, rstd, gain):
    scaled = grad * gain
    mean_one = jnp.mean(scaled, -1, keepdims=True)
    mean_two = jnp.mean(scaled * hat, -1, keepdims=True)
    return rstd * (scaled - mean_one - hat * mean_two)


def enter_kernel(own_ref, head_ref, out_ref, row_ref, cells_ref):
    columns = own_ref.shape[1]
    for r in range(WIN):
        row = own_ref[SHIFT + r] if r < WIN - SHIFT else head_ref[r - (WIN - SHIFT)]
        row_ref[0:columns, :] = row.astype(f32)
        row_ref[columns : columns + SHIFT, :] = row_ref[0:SHIFT, :]
        for w in range(columns // WIN):
            at = w * CELLS + r * WIN
            cells_ref[at : at + WIN, :] = row_ref[w * WIN + SHIFT : (w + 1) * WIN + SHIFT, :]
    for w in range(columns // WIN):
        at = slice(w * CELLS, (w + 1) * CELLS)
        out_ref[at, :] = cells_ref[at, :].astype(bf16)


def enter(own, head):
    rows, columns, width = own.shape
    cells = rows * columns
    return pl.pallas_call(
        enter_kernel,
        out_shape=jax.ShapeDtypeStruct((cells, width), bf16),
        scratch_shapes=[
            pltpu.VMEM((columns + 2 * WIN, width), f32),
            pltpu.VMEM((cells, width), f32),
        ],
        compiler_params=params(14),
        cost_estimate=cost(0, 4 * cells * width),
        name="enter",
    )(own, head)


def leave_kernel(cells_ref, keep_ref, send_ref, row_ref, wide_ref):
    columns = keep_ref.shape[1]
    for w in range(columns // WIN):
        at = slice(w * CELLS, (w + 1) * CELLS)
        wide_ref[at, :] = cells_ref[at, :].astype(f32)
    for r in range(WIN):
        for w in range(columns // WIN):
            at = w * CELLS + r * WIN
            row_ref[w * WIN + SHIFT : (w + 1) * WIN + SHIFT, :] = wide_ref[at : at + WIN, :]
        row_ref[0:SHIFT, :] = row_ref[columns : columns + SHIFT, :]
        row = row_ref[0:columns, :].astype(bf16)
        if r < WIN - SHIFT:
            keep_ref[r] = row
        else:
            send_ref[r - (WIN - SHIFT)] = row


def leave(cells, columns):
    width = cells.shape[1]
    return pl.pallas_call(
        leave_kernel,
        out_shape=[
            jax.ShapeDtypeStruct((WIN - SHIFT, columns, width), bf16),
            jax.ShapeDtypeStruct((SHIFT, columns, width), bf16),
        ],
        scratch_shapes=[
            pltpu.VMEM((columns + 2 * WIN, width), f32),
            pltpu.VMEM(cells.shape, f32),
        ],
        compiler_params=params(14),
        cost_estimate=cost(0, 4 * cells.size),
        name="leave",
    )(cells)


def qkv_kernel(stream, x_ref, gain_ref, bias_ref, w_ref, a_ref, out_ref):
    rows, width = x_ref.shape
    block = row_block(rows)
    row = slice(stream, stream + 1)
    ats = [slice(i * block, (i + 1) * block) for i in range(rows // block)]

    @pl.when(pl.program_id(0) == 0)
    def _():
        for at in ats:
            hat, _ = normalised(x_ref[at, :].astype(f32))
            low = (hat * gain_ref[row, :] + bias_ref[row, :]).astype(bf16)
            a_ref[at, :] = low
            out_ref[at, :] = dot_nn(low, w_ref[...]).astype(bf16)

    @pl.when(pl.program_id(0) != 0)
    def _():
        for at in ats:
            out_ref[at, :] = dot_nn(a_ref[at, :], w_ref[...]).astype(bf16)


def norm_qkv(x, gain, bias, weight, stream):
    rows, width = x.shape
    full = weight.shape[-1]
    return pl.pallas_call(
        functools.partial(qkv_kernel, stream),
        grid=(full // width,),
        in_specs=[
            whole((rows, width)),
            whole(gain.shape),
            whole(bias.shape),
            pl.BlockSpec((None, width, width), lambda j: (stream, 0, j)),
        ],
        out_specs=[whole((rows, width)), pl.BlockSpec((rows, width), lambda j: (0, j))],
        out_shape=[
            jax.ShapeDtypeStruct((rows, width), bf16),
            jax.ShapeDtypeStruct((rows, full), bf16),
        ],
        compiler_params=params(8 + rows // 80),
        cost_estimate=cost(2 * rows * width * full, 2 * rows * (2 * width + full) + 2 * width * full),
        name="norm_qkv",
    )(x, gain, bias, weight)


def first_half(shape):
    return lax.broadcasted_iota(jnp.int32, shape, len(shape) - 1) < PAIR // 2


def stacked(block):
    left = first_half(block.shape)
    zero = jnp.zeros_like(block)
    return jnp.concatenate([jnp.where(left, block, zero), jnp.where(left, zero, block)], 0)


def row_sums(values):
    ones = jnp.ones((8, PAIR), f32)
    return lax.dot_general(
        ones,
        values,
        (((1,), (1,)), ((), ())),
        precision=lax.Precision.HIGHEST,
        preferred_element_type=f32,
    )[:1]


def joined(upright):
    rows = upright.shape[0] // 2
    return jnp.where(first_half((rows, PAIR)), upright[:rows], upright[rows:])


def unstacked(turned):
    return joined(turned.T)


def query_forward_kernel(
    qq_ref, k_ref, v_ref, ko_ref, vo_ref, bias_ref, out_ref, stats_ref, s_ref, lse_ref
):
    queries = qq_ref.shape[0]
    cells = k_ref.shape[0]
    own = ko_ref.shape[0]
    scaled = stacked(qq_ref[...] * 0.125)
    bias = bias_ref[...]
    self_score = dot_nt(ko_ref[...], scaled) + jnp.concatenate([bias, bias], 1)
    top = jnp.max(self_score, 0, keepdims=True)
    block = row_block(cells)
    blocks = [slice(i * block, (i + 1) * block) for i in range(cells // block)]
    for at in blocks:
        score = dot_nt(k_ref[at, :], scaled)
        s_ref[at, :] = score
        top = jnp.maximum(top, jnp.max(score, 0, keepdims=True))
    prob = jnp.exp(self_score - top)
    total = jnp.sum(prob, 0, keepdims=True)
    mixed = dot_nn(vo_ref[...].T, prob.astype(bf16))
    for at in blocks:
        prob = jnp.exp(s_ref[at, :] - top)
        total = total + jnp.sum(prob, 0, keepdims=True)
        mixed = mixed + dot_nn(v_ref[at, :].T, prob.astype(bf16))
    out_ref[...] = unstacked(mixed * (1.0 / total))
    lse = top + jnp.log(total)
    pair = pl.program_id(0)

    @pl.when(pair == 0)
    def _():
        lse_ref[...] = jnp.zeros_like(lse_ref)

    lse_ref[pl.ds(2 * pair, 1), :] = lse[:, :queries]
    lse_ref[pl.ds(2 * pair + 1, 1), :] = lse[:, queries:]

    @pl.when(pair == pl.num_programs(0) - 1)
    def _():
        stats_ref[...] = lse_ref[...].T


def query_forward(query_qkv, own_qkv, vis_qkv, self_bias):
    cells = vis_qkv.shape[0]
    queries = query_qkv.shape[0]
    own = own_qkv.shape[0]
    width = query_qkv.shape[1] // 3
    pairs = width // PAIR
    keys = cells + own

    def part(rows, j):
        return pl.BlockSpec((rows, PAIR), lambda p, j=j: (0, j * pairs + p))

    return pl.pallas_call(
        query_forward_kernel,
        grid=(pairs,),
        in_specs=[
            part(queries, 0),
            part(cells, 1),
            part(cells, 2),
            part(own, 1),
            part(own, 2),
            whole(self_bias.shape),
        ],
        out_specs=[part(queries, 0), whole((queries, PAIR))],
        out_shape=[
            jax.ShapeDtypeStruct((queries, width), f32),
            jax.ShapeDtypeStruct((queries, PAIR), f32),
        ],
        scratch_shapes=[
            pltpu.VMEM((cells, 2 * queries), f32),
            pltpu.VMEM((PAIR, queries), f32),
        ],
        compiler_params=params(10 + queries // 32),
        cost_estimate=cost(
            4 * 2 * queries * keys * width, 4 * cells * width, 2 * queries * keys * pairs
        ),
        name="query_forward",
    )(query_qkv, vis_qkv, vis_qkv, own_qkv, own_qkv, self_bias)


def window_forward_kernel(
    windows,
    q_ref,
    k_ref,
    v_ref,
    kq_ref,
    vq_ref,
    row_ref,
    col_ref,
    open_ref,
    out_ref,
    lse_ref,
    scaled_ref,
    near_ref,
    mixed_ref,
    far_ref,
):
    cells = [slice(w * CELLS, (w + 1) * CELLS) for w in range(windows)]
    lanes = [slice(2 * w * CELLS, 2 * (w + 1) * CELLS) for w in range(windows)]
    tops = []
    for w in range(windows):
        scaled = stacked(q_ref[cells[w], :] * 0.125)
        scaled_ref[lanes[w], :] = scaled
        near = dot_nt(k_ref[cells[w], :], scaled)
        near = jnp.where(col_ref[w] == row_ref[w], near, MASKED)
        near_ref[w] = near
        tops.append(jnp.max(near, 0, keepdims=True))
    far = dot_nt(kq_ref[...], scaled_ref[...]) + open_ref[...]
    top = jnp.maximum(jnp.concatenate(tops, 1), jnp.max(far, 0, keepdims=True))
    far = jnp.exp(far - top)
    total = jnp.sum(far, 0, keepdims=True)
    far_mixed = dot_nn(vq_ref[...].T, far.astype(bf16))
    totals = []
    for w in range(windows):
        near = jnp.exp(near_ref[w] - top[:, lanes[w]])
        totals.append(jnp.sum(near, 0, keepdims=True))
        mixed_ref[w] = dot_nn(v_ref[cells[w], :].T, near.astype(bf16))
    total = total + jnp.concatenate(totals, 1)
    share = 1.0 / total
    lse_ref[...] = top + jnp.log(total)
    far_ref[...] = far_mixed
    for w in range(windows):
        turned = (mixed_ref[w] + far_ref[:, lanes[w]]) * share[:, lanes[w]]
        out_ref[cells[w], :] = joined(turned.astype(bf16).T)


def window_forward(vis_qkv, query_qkv, region_row, region_col, closed):
    cells = vis_qkv.shape[0]
    queries = query_qkv.shape[0]
    width = vis_qkv.shape[1] // 3
    pairs = width // PAIR
    windows = cells // CELLS

    def part(rows, j):
        return pl.BlockSpec((rows, PAIR), lambda p, j=j: (0, j * pairs + p))

    return pl.pallas_call(
        functools.partial(window_forward_kernel, windows),
        grid=(pairs,),
        in_specs=[
            part(cells, 0),
            part(cells, 1),
            part(cells, 2),
            part(queries, 1),
            part(queries, 2),
            whole(region_row.shape),
            whole(region_col.shape),
            whole(closed.shape),
        ],
        out_specs=[
            part(cells, 0),
            pl.BlockSpec((None, 1, 2 * cells), lambda p: (p, 0, 0)),
        ],
        out_shape=[
            jax.ShapeDtypeStruct((cells, width), bf16),
            jax.ShapeDtypeStruct((pairs, 1, 2 * cells), f32),
        ],
        scratch_shapes=[
            pltpu.VMEM((2 * cells, PAIR), bf16),
            pltpu.VMEM((windows, CELLS, 2 * CELLS), f32),
            pltpu.VMEM((windows, PAIR, 2 * CELLS), f32),
            pltpu.VMEM((PAIR, 2 * cells), f32),
        ],
        compiler_params=params(12 + queries // 28),
        cost_estimate=cost(
            8 * cells * (CELLS + queries) * width,
            8 * cells * width,
            2 * pairs * cells * (CELLS + queries),
        ),
        name="window_forward",
    )(vis_qkv, vis_qkv, vis_qkv, query_qkv, query_qkv, region_row, region_col, closed)


def attention_backward_kernel(
    windows,
    first,
    q_ref,
    k_ref,
    v_ref,
    do_ref,
    qq_ref,
    kq_ref,
    vq_ref,
    doq_ref,
    ko_ref,
    vo_ref,
    row_ref,
    col_ref,
    open_ref,
    bias_ref,
    lse_ref,
    lseq_ref,
    mixq_ref,
    *rest,
):
    if len(rest) > 16:
        rest = rest[3:]
    attention_backward_body(
        windows,
        first,
        q_ref,
        k_ref,
        v_ref,
        do_ref,
        qq_ref,
        kq_ref,
        vq_ref,
        doq_ref,
        ko_ref,
        vo_ref,
        row_ref,
        col_ref,
        open_ref,
        bias_ref,
        lse_ref,
        lseq_ref,
        mixq_ref,
        *rest,
    )


def attention_backward_body(
    windows,
    first,
    q_ref,
    k_ref,
    v_ref,
    do_ref,
    qq_ref,
    kq_ref,
    vq_ref,
    doq_ref,
    ko_ref,
    vo_ref,
    row_ref,
    col_ref,
    open_ref,
    bias_ref,
    lse_ref,
    lseq_ref,
    mixq_ref,
    dq_ref,
    dk_ref,
    dv_ref,
    dqq_ref,
    dkq_ref,
    dvq_ref,
    dko_ref,
    dvo_ref,
    scaled_ref,
    grad_ref,
    near_ref,
    neart_ref,
    seenk_ref,
    seenv_ref,
    far_ref,
    stats_ref,
):
    cells = [slice(w * CELLS, (w + 1) * CELLS) for w in range(windows)]
    lanes = [slice(2 * w * CELLS, 2 * (w + 1) * CELLS) for w in range(windows)]
    lse = lse_ref[...]

    deltas = []
    for w in range(windows):
        scaled = stacked(q_ref[cells[w], :] * 0.125)
        grad = stacked(do_ref[cells[w], :])
        scaled_ref[lanes[w], :] = scaled
        grad_ref[lanes[w], :] = grad
        near = dot_nt(k_ref[cells[w], :], scaled)
        near = jnp.exp(jnp.where(col_ref[w] == row_ref[w], near, MASKED) - lse[:, lanes[w]])
        near_t = near * dot_nt(v_ref[cells[w], :], grad)
        near_ref[w] = near
        neart_ref[w] = near_t
        deltas.append(jnp.sum(near_t, 0, keepdims=True))
    kq = kq_ref[...]
    far = jnp.exp(dot_nt(kq, scaled_ref[...]) + open_ref[...] - lse)
    far_t = far * dot_nt(vq_ref[...], grad_ref[...])
    delta = jnp.concatenate(deltas, 1) + jnp.sum(far_t, 0, keepdims=True)
    far_d = (far_t - far * delta).astype(bf16)
    dkq_ref[...] = dot_nn(far_d, scaled_ref[...]).astype(bf16)
    dvq_ref[...] = dot_nn(far.astype(bf16), grad_ref[...]).astype(bf16)
    far_ref[...] = dot_nn(kq.T, far_d).T

    scaled_q = stacked(qq_ref[...] * 0.125)
    grad_q = stacked(doq_ref[...])
    stats_ref[...] = lseq_ref[...].T
    head = 2 * (first + pl.program_id(0))
    lse_q = jnp.concatenate(
        [stats_ref[pl.ds(head, 1), :], stats_ref[pl.ds(head + 1, 1), :]], 1
    )
    mix_q = mixq_ref[...]
    delta_q = row_sums(grad_q.astype(f32) * jnp.concatenate([mix_q, mix_q], 0))
    bias = bias_ref[...]
    prob = jnp.exp(dot_nt(ko_ref[...], scaled_q) + jnp.concatenate([bias, bias], 1) - lse_q)
    dscore = (prob * (dot_nt(vo_ref[...], grad_q) - delta_q)).astype(bf16)
    dko_ref[...] = dot_nn(dscore, scaled_q)
    dvo_ref[...] = dot_nn(prob.astype(bf16), grad_q)
    turned = dot_nn(ko_ref[...].T, dscore)
    rows = k_ref.shape[0]
    block = row_block(rows)
    for i in range(rows // block):
        at = slice(i * block, (i + 1) * block)
        k_rows = k_ref[at, :]
        prob = jnp.exp(dot_nt(k_rows, scaled_q) - lse_q)
        dscore = (prob * (dot_nt(v_ref[at, :], grad_q) - delta_q)).astype(bf16)
        seenk_ref[at, :] = dot_nn(dscore, scaled_q)
        seenv_ref[at, :] = dot_nn(prob.astype(bf16), grad_q)
        turned = turned + dot_nn(k_rows.T, dscore)
    dqq_ref[...] = (unstacked(turned) * 0.125).astype(bf16)

    for w in range(windows):
        near = near_ref[w]
        near_d = (neart_ref[w] - near * delta[:, lanes[w]]).astype(bf16)
        upright = dot_nn(k_ref[cells[w], :].T, near_d).T + far_ref[lanes[w], :]
        dq_ref[cells[w], :] = (joined(upright) * 0.125).astype(bf16)
        dk_ref[cells[w], :] = (
            dot_nn(near_d, scaled_ref[lanes[w], :]) + seenk_ref[cells[w], :]
        ).astype(bf16)
        dv_ref[cells[w], :] = (
            dot_nn(near.astype(bf16), grad_ref[lanes[w], :]) + seenv_ref[cells[w], :]
        ).astype(bf16)


def attention_backward(
    vis_qkv,
    query_qkv,
    own_qkv,
    grad,
    grad_q,
    region_row,
    region_col,
    closed,
    self_bias,
    lse,
    joint_q,
    first,
    count,
    begun=(),
):
    cells = vis_qkv.shape[0]
    queries = query_qkv.shape[0]
    own = own_qkv.shape[0]
    width = vis_qkv.shape[1] // 3
    pairs = width // PAIR
    windows = cells // CELLS

    def part(rows, j):
        return pl.BlockSpec((rows, PAIR), lambda p, j=j: (0, j * pairs + first + p))

    def result(rows):
        return pl.BlockSpec((rows, PAIR), lambda p: (0, p))

    def filled(rows):
        return pl.BlockSpec((rows, PAIR), lambda p: (0, first + p))

    def stats(array):
        return pl.BlockSpec((None,) + array.shape[1:], lambda p: (first + p, 0, 0))

    span = count * PAIR
    return pl.pallas_call(
        functools.partial(attention_backward_kernel, windows, first),
        grid=(count,),
        in_specs=[
            part(cells, 0),
            part(cells, 1),
            part(cells, 2),
            part(cells, 0),
            part(queries, 0),
            part(queries, 1),
            part(queries, 2),
            part(queries, 0),
            part(own, 1),
            part(own, 2),
            whole(region_row.shape),
            whole(region_col.shape),
            whole(closed.shape),
            whole(self_bias.shape),
            stats(lse),
            pl.BlockSpec((queries, PAIR), lambda p: (0, pairs)),
            part(queries, 0),
        ]
        + [pl.BlockSpec(memory_space=pl.ANY)] * len(begun),
        out_specs=[filled(cells)] * 3 + [result(queries)] * 3 + [result(own)] * 2,
        out_shape=[jax.ShapeDtypeStruct((cells, width), bf16)] * 3
        + [jax.ShapeDtypeStruct((queries, span), bf16)] * 3
        + [jax.ShapeDtypeStruct((own, span), f32)] * 2,
        scratch_shapes=[
            pltpu.VMEM((2 * cells, PAIR), bf16),
            pltpu.VMEM((2 * cells, PAIR), bf16),
            pltpu.VMEM((windows, CELLS, 2 * CELLS), f32),
            pltpu.VMEM((windows, CELLS, 2 * CELLS), f32),
            pltpu.VMEM((cells, PAIR), f32),
            pltpu.VMEM((cells, PAIR), f32),
            pltpu.VMEM((2 * cells, PAIR), f32),
            pltpu.VMEM((PAIR, queries), f32),
        ],
        compiler_params=params(16 + queries // 25),
        cost_estimate=cost(
            20 * cells * (CELLS + 2 * queries) * span,
            14 * cells * span,
            2 * count * cells * (CELLS + 2 * queries),
        ),
        input_output_aliases={17 + i: i for i in range(len(begun))},
        name="attention_backward",
    )(
        vis_qkv,
        vis_qkv,
        vis_qkv,
        grad,
        query_qkv,
        query_qkv,
        query_qkv,
        grad_q,
        own_qkv,
        own_qkv,
        region_row,
        region_col,
        closed,
        self_bias,
        lse,
        joint_q,
        joint_q,
        *begun,
    )


def gelu_pair(z):
    below = 0.5 + 0.5 * lax.erf(z * 0.7071067811865476)
    bell = jnp.exp(-0.5 * z * z)
    return z * below, below + z * bell * 0.3989422804014327


def ffn_forward_kernel(
    stream,
    x_ref,
    o_ref,
    wo_ref,
    bo_ref,
    gain_ref,
    bias_ref,
    wu_ref,
    bu_ref,
    wd_ref,
    bd_ref,
    x1_ref,
    b_ref,
    hid_ref,
    slope_ref,
    out_ref,
    sum_ref,
):
    rows, width = x_ref.shape
    block = row_block(rows)
    count = rows // block
    ats = [slice(i * block, (i + 1) * block) for i in range(count)]
    step = pl.program_id(0)
    row = slice(stream, stream + 1)

    @pl.when(step == 0)
    def _():
        for at in ats:
            x1 = x_ref[at, :].astype(f32) + dot_nn(o_ref[at, :].astype(bf16), wo_ref[...]) + bo_ref[row, :]
            x1_ref[at, :] = x1
            hat, _ = normalised(x1)
            b_ref[at, :] = (hat * gain_ref[row, :] + bias_ref[row, :]).astype(bf16)
            sum_ref[at, :] = x1 + bd_ref[row, :]

    def project(i):
        return dot_nn(b_ref[ats[i], :], wu_ref[...]) + bu_ref[row, :]

    z = project(0)
    for i in range(count):
        ahead = project(i + 1) if i + 1 < count else None
        hidden, slope = gelu_pair(z)
        hidden = hidden.astype(bf16)
        hid_ref[ats[i], :] = hidden
        slope_ref[ats[i], :] = slope.astype(bf16)
        sum_ref[ats[i], :] += dot_nn(hidden, wd_ref[...])
        z = ahead

    @pl.when(step == pl.num_programs(0) - 1)
    def _():
        out_ref[...] = sum_ref[...].astype(bf16)


def ffn_forward(x, attended, out_w, out_b, gain, bias, up_w, up_b, down_w, down_b, stream):
    rows, width = x.shape
    hidden = up_w.shape[-1]
    chunk = 768
    return pl.pallas_call(
        functools.partial(ffn_forward_kernel, stream),
        grid=(hidden // chunk,),
        in_specs=[
            once((rows, width)),
            once((rows, width)),
            once((None, width, width), lambda f: (stream, 0, 0)),
            whole(out_b.shape),
            whole(gain.shape),
            whole(bias.shape),
            pl.BlockSpec((None, width, chunk), lambda f: (stream, 0, f)),
            pl.BlockSpec((2, chunk), lambda f: (0, f)),
            pl.BlockSpec((None, chunk, width), lambda f: (stream, f, 0)),
            whole(down_b.shape),
        ],
        out_specs=[
            whole((rows, width)),
            whole((rows, width)),
            pl.BlockSpec((rows, chunk), lambda f: (0, f)),
            pl.BlockSpec((rows, chunk), lambda f: (0, f)),
            whole((rows, width)),
        ],
        out_shape=[
            jax.ShapeDtypeStruct((rows, width), f32),
            jax.ShapeDtypeStruct((rows, width), bf16),
            jax.ShapeDtypeStruct((rows, hidden), bf16),
            jax.ShapeDtypeStruct((rows, hidden), bf16),
            jax.ShapeDtypeStruct((rows, width), bf16),
        ],
        scratch_shapes=[pltpu.VMEM((rows, width), f32)],
        compiler_params=params(34 if stream == 0 else 56),
        cost_estimate=cost(
            2 * rows * width * (2 * hidden + width),
            4 * width * hidden + 4 * rows * hidden + 12 * rows * width,
            2 * rows * hidden,
        ),
        name="ffn_forward",
    )(x, attended, out_w, out_b, gain, bias, up_w, up_b, down_w, down_b)


def ffn_backward_kernel(
    stream,
    g_ref,
    slope_ref,
    x1_ref,
    wd_ref,
    wu_ref,
    wo_ref,
    gain_ref,
    dz_ref,
    dx1_ref,
    du_ref,
    do_ref,
    sums_ref,
    sum_ref,
):
    rows, width = g_ref.shape
    block = row_block(rows)
    count = rows // block
    ats = [slice(i * block, (i + 1) * block) for i in range(count)]
    step = pl.program_id(0)
    row = slice(stream, stream + 1)

    @pl.when(step == 0)
    def _():
        sum_ref[...] = jnp.zeros_like(sum_ref)

    up_bias = jnp.zeros((1, dz_ref.shape[1]), f32)

    def pulled(i):
        return dot_nt(g_ref[ats[i], :], wd_ref[...])

    grad = pulled(0)
    for i in range(count):
        ahead = pulled(i + 1) if i + 1 < count else None
        dz = grad * slope_ref[ats[i], :].astype(f32)
        low = dz.astype(bf16)
        dz_ref[ats[i], :] = low
        up_bias = up_bias + jnp.sum(dz, 0, keepdims=True)
        sum_ref[ats[i], :] += dot_nt(low, wu_ref[...])
        grad = ahead
    sums_ref[pl.ds(4 + step, 1), :] = up_bias

    @pl.when(step == pl.num_programs(0) - 1)
    def _():
        sums_ref[0:4, :] = jnp.zeros((4, width), f32)
        for at in ats:
            hat, rstd = normalised(x1_ref[at, :])
            db = sum_ref[at, :]
            g = g_ref[at, :].astype(f32)
            dx1 = g + norm_back(db, hat, rstd, gain_ref[row, :])
            dx1_ref[at, :] = dx1
            du = dx1.astype(bf16)
            du_ref[at, :] = du
            do_ref[at, :] = dot_nt(du, wo_ref[...]).astype(bf16)
            sums_ref[0:1, :] += jnp.sum(db * hat, 0, keepdims=True)
            sums_ref[1:2, :] += jnp.sum(db, 0, keepdims=True)
            sums_ref[2:3, :] += jnp.sum(dx1, 0, keepdims=True)
            sums_ref[3:4, :] += jnp.sum(g, 0, keepdims=True)


def ffn_backward(g, slope, x1, down_w, up_w, out_w, gain, stream):
    rows, width = g.shape
    hidden = up_w.shape[-1]
    chunk = width
    return pl.pallas_call(
        functools.partial(ffn_backward_kernel, stream),
        grid=(hidden // chunk,),
        in_specs=[
            once((rows, width)),
            pl.BlockSpec((rows, chunk), lambda f: (0, f)),
            once((rows, width)),
            pl.BlockSpec((None, chunk, width), lambda f: (stream, f, 0)),
            pl.BlockSpec((None, width, chunk), lambda f: (stream, 0, f)),
            once((None, width, width), lambda f: (stream, 0, 0)),
            whole(gain.shape),
        ],
        out_specs=[
            pl.BlockSpec((None, rows, chunk), lambda f: (f, 0, 0)),
            whole((rows, width)),
            whole((rows, width)),
            whole((rows, width)),
            whole((4 + hidden // chunk, width)),
        ],
        out_shape=[
            jax.ShapeDtypeStruct((hidden // chunk, rows, chunk), bf16),
            jax.ShapeDtypeStruct((rows, width), f32),
            jax.ShapeDtypeStruct((rows, width), bf16),
            jax.ShapeDtypeStruct((rows, width), bf16),
            jax.ShapeDtypeStruct((4 + hidden // chunk, width), f32),
        ],
        scratch_shapes=[pltpu.VMEM((rows, width), f32)],
        compiler_params=params(34 if stream == 0 else 56),
        cost_estimate=cost(
            2 * rows * width * (2 * hidden + width),
            4 * width * hidden + 4 * rows * hidden + 14 * rows * width,
        ),
        name="ffn_backward",
    )(g, slope, x1, down_w, up_w, out_w, gain)


def input_kernel(stream, dq_ref, dk_ref, dv_ref, w_ref, x_ref, dx1_ref, gain_ref, out_ref, sums_ref):
    width = x_ref.shape[1]

    @pl.when(pl.program_id(0) == 0)
    def _():
        sums_ref[...] = jnp.zeros_like(sums_ref)

    grad = dot_nt(dq_ref[...], w_ref[:, :width])
    grad = grad + dot_nt(dk_ref[...], w_ref[:, width : 2 * width])
    grad = grad + dot_nt(dv_ref[...], w_ref[:, 2 * width :])
    hat, rstd = normalised(x_ref[...].astype(f32))
    out_ref[...] = (
        dx1_ref[...] + norm_back(grad, hat, rstd, gain_ref[stream : stream + 1, :])
    ).astype(bf16)
    at = 4 * stream
    sums_ref[at : at + 1, :] += jnp.sum(grad * hat, 0, keepdims=True)
    sums_ref[at + 1 : at + 2, :] += jnp.sum(grad, 0, keepdims=True)


def input_grad(dq, dk, dv, weight, x, dx1, gain, stream):
    rows, width = x.shape
    block = row_block(rows)
    rows_spec = pl.BlockSpec((block, width), lambda i: (i, 0))
    return pl.pallas_call(
        functools.partial(input_kernel, stream),
        grid=(rows // block,),
        in_specs=[rows_spec] * 3
        + [
            pl.BlockSpec((None, width, 3 * width), lambda i: (stream, 0, 0)),
            rows_spec,
            rows_spec,
            whole(gain.shape),
        ],
        out_specs=[rows_spec, whole((8, width))],
        out_shape=[
            jax.ShapeDtypeStruct((rows, width), bf16),
            jax.ShapeDtypeStruct((8, width), f32),
        ],
        compiler_params=params(16),
        cost_estimate=cost(6 * rows * width * width, 14 * rows * width + 6 * width * width),
        name="input_grad",
    )(dq, dk, dv, weight, x, dx1, gain)


def after(value, *before):
    return lax.optimization_barrier((value,) + before)[0]


def beside(made, *flights):
    return lax.optimization_barrier((made,) + flights)


def moved(block, axis, step):
    size = lax.axis_size(axis)
    return lax.ppermute(block, axis, [(i, (i + step) % size) for i in range(size)])


def swapped(block, axis, mask):
    size = lax.axis_size(axis)
    return lax.ppermute(block, axis, [(i, i ^ mask) for i in range(size)])


def other_core(block):
    return swapped(block, "strip", 1)


def place():
    strip = lax.axis_index("strip")
    return lax.axis_size("strip") // 2, strip // 2, strip % 2


def pick(block, index, axis=0):
    return lax.dynamic_index_in_dim(block, index, axis, keepdims=False)


def added(blocks, kind=bf16):
    total = blocks[0].astype(f32)
    for block in blocks[1:]:
        total = total + block.astype(f32)
    return total.astype(kind)


def bit_of(axis, mask):
    return (lax.axis_index(axis) // mask) % 2


class Phase:
    def __init__(self, blocks, dims, axis, mask):
        bit = bit_of(axis, mask)
        theirs, self.mine = [
            [added([pick(term, half, dim) for term in terms]) for terms, dim in zip(blocks, dims)]
            for half in (1 - bit, bit)
        ]
        self.shapes = [block.shape for block in theirs]
        self.sent, self.got = exchange(theirs, axis, mask)

    def terms(self):
        got = parted(self.got, self.shapes)
        return [[mine, more] for mine, more in zip(self.mine, got)]

    def sums(self):
        return [added(terms) for terms in self.terms()]


def mapped(change, terms):
    return [change(term) for term in terms]


class Gather:
    def __init__(self, blocks, dims, axis, mask):
        self.bit = bit_of(axis, mask)
        self.blocks, self.dims = blocks, dims
        self.shapes = [block.shape for block in blocks]
        self.sent, self.got = exchange(blocks, axis, mask)

    def pairs(self):
        first = self.bit == 0
        return [
            jnp.stack([jnp.where(first, one, two), jnp.where(first, two, one)], dim)
            for one, two, dim in zip(self.blocks, parted(self.got, self.shapes), self.dims)
        ]


class PageGather:
    def __init__(self, blocks):
        self.shapes = [block.shape for block in blocks]
        rows = [block.reshape(-1, block.shape[-1]) for block in blocks]
        self.sent = jnp.concatenate(rows, 0)
        self.got = [swapped(self.sent, "page", mask) for mask in (1, 2, 3)]

    def whole(self):
        def ordered(bit, one, two, axis):
            first = bit == 0
            return jnp.stack([jnp.where(first, one, two), jnp.where(first, two, one)], axis)

        every = [parted(rows, self.shapes) for rows in [self.sent] + list(self.got)]
        result = []
        for mine, by_x, by_y, by_both in zip(*every):
            near = ordered(bit_of("page", 1), mine, by_x, 1)
            far = ordered(bit_of("page", 1), by_y, by_both, 1)
            result.append(from_page(ordered(bit_of("page", 2), near, far, 1)))
        return result


def parted(rows, shapes):
    if len(shapes) == 1:
        return [rows]
    blocks, at = [], 0
    for shape in shapes:
        count = 1
        for size in shape[:-1]:
            count *= size
        blocks.append(rows[at : at + count].reshape(shape))
        at += count
    return blocks


def exchange(blocks, axis, mask):
    if len(blocks) == 1:
        sent = blocks[0]
    else:
        sent = jnp.concatenate([block.reshape(-1, block.shape[-1]) for block in blocks], 0)
    return sent, swapped(sent, axis, mask)


def by_core(grad):
    strips = lax.axis_size("strip")
    return grad.reshape(strips // 2, 2, grad.shape[0] // strips, grad.shape[1])


def tiled(grad, width):
    count = grad.shape[-1] // width
    return jnp.stack([grad[..., i * width : (i + 1) * width] for i in range(count)], -3)


def untiled(blocks):
    return jnp.concatenate([blocks[i] for i in range(blocks.shape[0])], -1)


def by_page(blocks):
    rows = blocks.shape[-2]
    return blocks.reshape(blocks.shape[:-2] + (2, 2, rows // 4, blocks.shape[-1]))


def from_page(blocks):
    return blocks.reshape(blocks.shape[:-4] + (-1, blocks.shape[-1]))


def by_chip(blocks, axis):
    shape = blocks.shape
    return blocks.reshape(shape[:axis] + (shape[axis] // 2, 2) + shape[axis + 1 :])


def line_masks():
    size, _, _ = place()
    return [2 << i for i in range(size.bit_length() - 1)]


def line_phase(blocks, axes, mask):
    split = [
        [by_chip(term, axis) for term in terms] for terms, axis in zip(blocks, axes)
    ]
    return Phase(split, [axis + 1 for axis in axes], "strip", mask)


def line_first(blocks, axes):
    masks = line_masks()
    for mask in masks[:-2]:
        blocks = line_phase(blocks, axes, mask).terms()
    return line_phase(blocks, axes, masks[-2])


def line_last(blocks, axes):
    return line_phase(blocks, axes, line_masks()[-1])


def line_exchange(block):
    size, z, _ = place()
    return [pick(block, z)] + [
        moved(pick(block, (z + step) % size), "strip", 2 * step) for step in range(1, size)
    ]


def line_gather(block):
    size, _, _ = place()
    return [block] + [moved(block, "strip", 2 * step) for step in range(1, size)]


def line_order(blocks):
    size, z, _ = place()
    double = jnp.stack(blocks[:1] + blocks[:0:-1] + blocks[:1] + blocks[:0:-1])
    return lax.dynamic_slice_in_dim(double, (size - z) % size, size, 0)


def page_exchange(block):
    size = lax.axis_size("page")
    page = lax.axis_index("page")
    shares = block.reshape(size, block.shape[0] // size, block.shape[1])
    return [pick(shares, page)] + [
        swapped(pick(shares, page ^ mask), "page", mask) for mask in range(1, size)
    ]


def page_gather(block):
    size = lax.axis_size("page")
    return [block] + [swapped(block, "page", mask) for mask in range(1, size)]


def page_order(blocks):
    size = len(blocks)
    page = lax.axis_index("page")
    rows, columns = blocks[0].shape
    joined = jnp.zeros((size * rows, columns), f32)
    for mask, block in enumerate(blocks):
        joined = lax.dynamic_update_slice_in_dim(
            joined, block.astype(f32), (page ^ mask) * rows, 0
        )
    return joined


def core_order(mine, other):
    _, _, core = place()
    pair = jnp.stack(
        [jnp.where(core == 0, mine, other), jnp.where(core == 0, other, mine)], 1
    )
    return pair.reshape(-1, pair.shape[-1])


def merge_kernel(one_ref, two_ref, out_ref):
    width = one_ref.shape[1] - PAIR
    one_top = one_ref[:, width:]
    two_top = two_ref[:, width:]
    top = jnp.maximum(one_top, two_top)
    one_share = jnp.exp(one_top - top)
    two_share = jnp.exp(two_top - top)
    total = one_share + two_share
    shape = (PAIR, width)
    head = lax.broadcasted_iota(jnp.int32, shape, 1) // (width // HEADS)
    spread = (lax.broadcasted_iota(jnp.int32, shape, 0) == head).astype(f32)

    def over_heads(share):
        return jnp.dot(share / total, spread, precision=lax.Precision.HIGHEST)

    out_ref[:, :width] = one_ref[:, :width] * over_heads(one_share) + two_ref[
        :, :width
    ] * over_heads(two_share)
    out_ref[:, width:] = top + jnp.log(total)


def merged(one, two):
    shape = one.shape
    rows = one.size // shape[-1]
    out = pl.pallas_call(
        merge_kernel,
        out_shape=jax.ShapeDtypeStruct((rows, shape[-1]), f32),
        compiler_params=params(8),
        cost_estimate=cost(6 * one.size, 12 * one.size),
        name="merge",
    )(one.reshape(rows, -1), two.reshape(rows, -1))
    return out.reshape(shape)


def region_windows(rows):
    across = rows.shape[1] // WIN
    rolled = jnp.roll(rows, -SHIFT, axis=1)
    return rolled.reshape(WIN, across, WIN).transpose(1, 0, 2).reshape(across, CELLS)


def weight_grad(left, right):
    return dot_tn(left, right).astype(bf16)


def body(
    vis_tokens,
    query_tokens,
    region_ids,
    query_mask,
    answer_len,
    norm1_gain,
    norm1_bias,
    qkv_weight,
    out_weight,
    out_bias,
    norm2_gain,
    norm2_bias,
    up_weight,
    up_bias,
    down_weight,
    down_bias,
    vis_cotangent,
    query_cotangent,
):
    strips = lax.axis_size("strip")
    strip = lax.axis_index("strip")
    chips, z, core = place()
    local_rows, columns, features = vis_tokens.shape[1:]
    own_count = query_tokens.shape[1]
    query_count = query_mask.shape[1]
    total_rows = region_ids.shape[1]
    own_start = strip * own_count

    def own_rows(values):
        return lax.dynamic_slice_in_dim(values, own_start, own_count, 0)

    def own_columns(values):
        span = values.shape[1] // strips
        return lax.dynamic_slice_in_dim(values, strip * span, span, 1)

    tokens = line_gather(query_tokens[0])
    head_rows = moved(vis_tokens[0, :SHIFT], "strip", -1)
    tokens = line_order(tokens)
    query = core_order(tokens, other_core(tokens))

    key_open = query_mask[0] > 0
    key_ids = jnp.arange(query_count, dtype=jnp.int32)
    prompt = key_ids < query_count - answer_len[0]
    closed = jnp.where(key_open & prompt, 0.0, MASKED).astype(f32)[:, None]
    own_ids = own_start + jnp.arange(own_count, dtype=jnp.int32)
    allowed = own_rows(key_open)[:, None] & (
        own_rows(prompt)[:, None] | (own_ids[:, None] <= key_ids[None, :])
    )
    self_bias = jnp.where(allowed, 0.0, MASKED).astype(f32)
    row_ids = (strip * local_rows + SHIFT + jnp.arange(local_rows, dtype=jnp.int32)) % total_rows
    region = region_windows(jnp.take(region_ids[0], row_ids, axis=0))
    region_row = jnp.concatenate([region, region], 1)[:, None, :]
    region_col = region[:, :, None]

    query_norm, query_qkv = norm_qkv(query, norm1_gain, norm1_bias, qkv_weight, 1)
    (query_norm, query_qkv), head_rows = beside((query_norm, query_qkv), head_rows)
    own_qkv = own_rows(query_qkv)
    vis = enter(vis_tokens[0], head_rows)
    head_cot = moved(after(vis_cotangent[0, :SHIFT], vis), "strip", -1)
    vis_norm, vis_qkv = norm_qkv(vis, norm1_gain, norm1_bias, qkv_weight, 0)

    part = query_forward(query_qkv, own_qkv, vis_qkv, self_bias)
    part, head_cot = beside(part, head_cot)
    mine, theirs = [
        jnp.concatenate([pick(by_core(each), which, 1) for each in part], -1)
        for which in (core, 1 - core)
    ]
    others = other_core(theirs)
    vis_cot = enter(after(vis_cotangent[0], theirs), head_cot)
    vis_cot, mine, others = beside(vis_cot, mine, others)
    part = merged(mine, others)
    others = swapped(part, "strip", 2)

    vis_windows = window_forward(after(vis_qkv, part), query_qkv, region_row, region_col, closed)
    (vis_attn, vis_lse), part, others = beside(vis_windows, part, others)
    part = merged(part, others)
    mask = 4
    while 2 * mask < strips:
        part = merged(part, swapped(part, "strip", mask))
        mask = 2 * mask
    others = swapped(part, "strip", mask)

    weights = (out_weight, out_bias, norm2_gain, norm2_bias, up_weight, up_bias, down_weight, down_bias)
    made = ffn_forward(vis, after(vis_attn, part), *weights, 0)
    made, part, others = beside(made, part, others)
    vis_x1, vis_b, vis_hid, vis_slope, vis_result = made
    part = merged(part, others)
    others = other_core(part)
    vis_down = weight_grad(after(vis_hid, part), vis_cot)
    vis_down, part, others = beside(vis_down, part, others)
    cotangents = line_gather(after(query_cotangent[0], part))
    down = by_core(vis_down)
    down = Phase([[down.reshape(chips, 2, -1, features // strips, features)]], [1], "strip", 1)

    made = ffn_backward(
        after(vis_cot, down.sent), vis_slope, vis_x1, down_weight, up_weight, out_weight, norm2_gain, 0
    )
    made, down.got, cotangents = beside(made, down.got, cotangents)
    cotangents = line_order(cotangents)
    cot_others = other_core(cotangents)
    vis_dz, vis_dx1, vis_du, vis_do, vis_sums = made
    (down,) = down.terms()
    down = Phase([mapped(by_page, down)], [3], "page", 1)
    hidden = up_weight.shape[-1] // features
    vis_b = after(vis_b, down.sent)
    up_a = [by_core(weight_grad(vis_b, vis_dz[i])) for i in range(hidden - 1)]
    up_a = Phase([[jnp.stack(up_a)]], [2], "strip", 1)
    up_b = [by_core(weight_grad(after(vis_b, up_a.sent), vis_dz[hidden - 1]))]
    up_b = Phase([[jnp.stack(up_b + [by_core(weight_grad(vis_attn, vis_du))])]], [2], "strip", 1)
    made = leave(after(vis_result, up_b.sent), columns)
    (vis_keep, vis_send), up_a.got, up_b.got = beside(made, up_a.got, up_b.got)
    vis_first = moved(vis_send, "strip", 1)
    up_a = line_first(up_a.terms(), [1])

    every = core_order(part, others)
    every, up_sent = beside(every, up_a.sent)
    made = ffn_forward(query, every, *weights, 1)
    made, down.got, cot_others = beside(made, down.got, cot_others)
    query_cot = core_order(cotangents, cot_others)
    query_x1, query_b, query_hid, query_slope, query_result = made
    (down,) = down.terms()
    down = Phase([down], [2], "page", 2)
    up_b = Phase([mapped(by_page, terms) for terms in up_b.terms()], [3], "page", 1)
    made = ffn_backward(
        query_cot,
        after(query_slope, up_b.sent, down.sent),
        query_x1,
        down_weight,
        up_weight,
        out_weight,
        norm2_gain,
        1,
    )
    made, up_a.got, up_b.got = beside(made, up_a.got, up_b.got)
    query_dz, query_dx1, query_du, query_do, query_sums = made
    (up_a,) = up_a.terms()
    (up_b,) = up_b.terms()
    up_a = Phase([mapped(by_page, up_a)], [3], "page", 1)
    up_b = Phase([up_b], [2], "page", 2)

    def query_grads(left, right):
        return weight_grad(own_columns(left), right)

    up_rows = features // strips
    query_dz = after(query_dz, up_a.sent, up_b.sent)
    one = jnp.concatenate(
        [
            jnp.stack([query_grads(query_b, query_dz[i]) for i in range(hidden)]),
            query_grads(every[:, :features].astype(bf16), query_du)[None],
            query_grads(query_hid, query_cot).reshape(-1, up_rows, features),
        ],
        0,
    )
    one, down.got = beside(one, down.got)
    one = Phase([[by_page(one)]], [2], "page", 1)
    down = line_first(down.terms(), [0])

    pairs = HEADS // 2
    half = pairs // 2

    def backward(values, first, begun=()):
        return attention_backward(
            values,
            query_qkv,
            own_qkv,
            vis_do,
            query_do,
            region_row,
            region_col,
            closed,
            self_bias,
            vis_lse,
            every,
            first,
            half,
            begun,
        )

    def head_grads(normed, grads, first):
        span = half * PAIR
        return jnp.stack(
            [
                by_core(weight_grad(normed, each[:, first * PAIR : first * PAIR + span]))
                for each in grads
            ],
            2,
        )

    back_one = backward(after(vis_qkv, one.sent, down.sent), 0)
    back_one, up_a.got, up_b.got, down.got, vis_first = beside(
        back_one, up_a.got, up_b.got, down.got, vis_first
    )
    first = Phase([[head_grads(vis_norm, back_one[:3], 0)]], [1], "strip", 1)
    first.sent, one.got = beside(first.sent, one.got)
    (up_a,) = up_a.terms()
    (one,) = one.terms()
    mixed_y = Phase([after(up_a, first.sent), one], [2, 1], "page", 2)
    up_b = line_first(up_b.terms(), [1])
    down = line_last(down.terms(), [0])
    down.sent, up_b.sent, mixed_y.sent, first.got = beside(
        down.sent, up_b.sent, mixed_y.sent, first.got
    )
    (first,) = first.terms()
    first = Phase([mapped(by_page, first)], [3], "page", 1)

    back_two = backward(
        after(vis_qkv, first.sent, mixed_y.sent, up_b.sent, down.sent), half, back_one[:3]
    )
    back_two, first.got, mixed_y.got, up_b.got, down.got = beside(
        back_two, first.got, mixed_y.got, up_b.got, down.got
    )
    part = jnp.stack(
        [by_core(each) for pair in zip(back_one[3:6], back_two[3:6]) for each in pair], 2
    )
    part = Phase([[part]], [1], "strip", 1)
    grads = head_grads(after(vis_norm, part.sent), back_two[:3], half)
    second = Phase([[grads]], [1], "strip", 1)
    second.sent, part.got = beside(second.sent, part.got)
    part = line_first(part.terms(), [0])
    up_a, one = mixed_y.terms()
    (up_b,) = up_b.terms()
    line = line_last([after(up_a, part.sent), up_b], [1, 1])
    line.sent, second.got = beside(line.sent, second.got)
    (second,) = second.terms()
    second = Phase([mapped(by_page, second)], [3], "page", 1)
    (down,) = down.sums()
    one = after(added(one), second.sent)
    early = Gather([one[:5], down[0]], [1, 1], "page", 1)
    early_y = Gather([one[5:]], [1], "page", 2)

    made = input_grad(
        after(back_two[0], part.sent, line.sent, second.sent, early.sent, early_y.sent),
        back_two[1],
        back_two[2],
        qkv_weight,
        vis,
        vis_dx1,
        norm1_gain,
        0,
    )
    made, part.got = beside(made, part.got)
    vis_input, vis_head = made
    part = line_last(part.terms(), [0])
    made = leave(after(vis_input, part.sent), columns)
    made, part.got, second.got, line.got = beside(made, part.got, second.got, line.got)
    grad_keep, grad_send = made
    (part,) = part.terms()
    own_self = [jnp.zeros_like(back_one[6])] * 2 + [back_one[6], back_two[6], back_one[7], back_two[7]]
    own_dqkv = added(mapped(lambda term: term[0], part) + [jnp.stack(own_self)])
    masks = line_masks()
    lined = own_dqkv[None]
    for mask in reversed(masks[1:-1]):
        lined = Gather([lined], [1], "strip", mask).pairs()[0]
        lined = lined.reshape((-1,) + own_dqkv.shape)
    lined = Gather([lined], [0], "strip", masks[-1])
    qkv = Phase(
        [after(terms, lined.sent) for terms in first.terms() + second.terms()], [2, 2], "page", 2
    )
    made = input_grad(
        untiled(after(own_dqkv, lined.sent, qkv.sent)[0:2]),
        untiled(own_dqkv[2:4]),
        untiled(own_dqkv[4:6]),
        qkv_weight,
        query_tokens[0],
        own_rows(query_dx1),
        norm1_gain,
        1,
    )
    made, lined.got, early.got, early_y.got = beside(made, lined.got, early.got, early_y.got)
    own_input, own_head = made
    lined = lined.pairs()[0].reshape((-1,) + own_dqkv.shape)
    lined = Gather([lined], [1], "strip", masks[0])
    one, down = after(early.pairs(), lined.sent)
    (one_b,) = after(early_y.pairs(), lined.sent)
    down = Gather([down], [1], "page", 2)

    small = jnp.concatenate([vis_sums, vis_head + own_head], 0)
    small_others = other_core(small)
    lined.got, small_others, qkv.got = beside(lined.got, small_others, qkv.got)
    small = small + small_others
    lined = lined.pairs()[0].reshape((-1,) + own_dqkv.shape)
    lined_others = other_core(lined)
    for mask in masks[:-2]:
        small = small + swapped(small, "strip", mask)
    small_others = swapped(small, "strip", masks[-2])
    qkv = line_first(after(qkv.terms(), lined), [0, 0])
    up_part, low_part = line.sums()
    up_gather = Gather([after(up_part, lined)[:, 0], low_part[:, 0]], [1, 1], "page", 1)
    grad_near = moved(after(grad_send[: SHIFT // 2], lined), "strip", 1)
    lined_others, small_others, down.got = beside(lined_others, small_others, down.got)
    one_first = Gather([after(one, down.got)], [1], "page", 2)
    small = small + small_others
    query_dqkv = jnp.stack(
        [jnp.where(core == 0, lined, lined_others), jnp.where(core == 0, lined_others, lined)], 1
    )
    query_dqkv = [query_dqkv[:, :, i].reshape(query_count, -1) for i in range(6)]
    three = query_grads(query_norm, jnp.concatenate(query_dqkv, 1))
    three = Phase([[by_page(tiled(three, half * PAIR))]], [2], "page", 1)
    small_others = swapped(small, "strip", masks[-1])
    three.got, qkv.got, small_others, up_gather.got, one_first.got, grad_near = beside(
        three.got, qkv.got, small_others, up_gather.got, one_first.got, grad_near
    )
    three = Phase(three.terms(), [1], "page", 2)
    qkv = line_last(after(qkv.terms(), three.sent), [0, 0])
    small = jnp.concatenate([small + small_others, query_sums], 0)
    last = Gather(after(up_gather.pairs(), three.sent), [1, 1], "page", 2)
    one_last = Gather([after(one_b, three.sent)], [2], "page", 1)
    three.got, qkv.got, small = beside(three.got, qkv.got, small)
    grad_far = moved(after(grad_send[SHIFT // 2 :], three.got), "strip", 1)
    small = tiled(small.astype(bf16), half * PAIR)
    late = PageGather([each[0] for each in qkv.sums()] + three.sums() + [small])

    up_a, up_b = [from_page(each) for each in last.pairs()]
    (one_last,) = [from_page(each) for each in one_last.pairs()]
    (down,) = [from_page(each) for each in down.pairs()]
    one = jnp.concatenate([from_page(each) for each in one_first.pairs()] + [one_last], 0)
    up = jnp.concatenate([up_a, up_b], 0)
    up_grad = jnp.stack([untiled(up[:hidden]), untiled(one[:hidden])]).astype(f32)
    out_grad = jnp.stack([up[hidden], one[hidden]]).astype(f32)
    down_grad = jnp.stack([down, one[hidden + 1 :]]).astype(f32).reshape(2, -1, features)
    vis_final = jnp.concatenate([vis_first, vis_keep], 0)[None]
    grad_final = jnp.concatenate([grad_near, grad_far, grad_keep], 0)[None]
    late.got, up_grad, out_grad, down_grad, vis_final, grad_final = beside(
        late.got, up_grad, out_grad, down_grad, vis_final, grad_final
    )
    first, second, three, small = late.whole()
    tiles, rows, span = small.shape
    pages = lax.axis_size("page")
    small = untiled(small.reshape(tiles, pages, rows // pages, span).astype(f32).sum(1))
    vis_qkv_grad = jnp.concatenate(
        [each[i] for i in range(3) for each in (first, second)], 1
    )
    qkv_grad = jnp.stack([vis_qkv_grad, untiled(three)]).astype(f32)

    count = vis_sums.shape[0]
    gain_two, bias_two, obias, dbias = [
        own_columns(jnp.stack([small[i], small[count + 8 + i]])) for i in range(4)
    ]
    gain_one, bias_one = [
        own_columns(jnp.stack([small[count + i], small[count + 4 + i]])) for i in range(2)
    ]
    ubias = jnp.stack([small[4:count].reshape(-1), small[count + 12 :].reshape(-1)])
    ubias = own_columns(ubias)

    return (
        vis_final,
        own_rows(query_result)[None],
        grad_final,
        own_input[None],
        gain_one,
        bias_one,
        qkv_grad,
        out_grad,
        obias,
        gain_two,
        bias_two,
        up_grad,
        ubias,
        down_grad,
        dbias,
    )


def solution(mesh):
    return jax.shard_map(
        body,
        mesh=mesh,
        in_specs=(
            P("page", "strip", None, None),
            P("page", "strip", None),
            P("page", None, None),
            P("page", None),
            P("page"),
            P(),
            P(),
            P(),
            P(),
            P(),
            P(),
            P(),
            P(),
            P(),
            P(),
            P(),
            P("page", "strip", None, None),
            P("page", "strip", None),
        ),
        out_specs=(
            P("page", "strip", None, None),
            P("page", "strip", None),
            P("page", "strip", None, None),
            P("page", "strip", None),
            P(None, "strip"),
            P(None, "strip"),
            P(None, "strip", None),
            P(None, "strip", None),
            P(None, "strip"),
            P(None, "strip"),
            P(None, "strip"),
            P(None, "strip", None),
            P(None, "strip"),
            P(None, "strip", None),
            P(None, "strip"),
        ),
        check_vma=False,
    )
```

```python
import functools

import jax
import jax.numpy as jnp
from jax import lax
from jax.experimental import pallas as pl
from jax.experimental.pallas import tpu as pltpu
from jax.sharding import PartitionSpec as P

HEADS = 12
WIN = 12
SHIFT = 6
CELLS = WIN * WIN
PAIR = 128
MASKED = -1000000000.0
MIB = 1024 * 1024

bf16 = jnp.bfloat16
f32 = jnp.float32


def params(mib):
    return pltpu.CompilerParams(vmem_limit_bytes=min(int(mib), 56) * MIB)


def row_block(rows):
    for size in range(336, 15, -16):
        if rows % size == 0:
            return size
    return rows


def dot_nn(a, b):
    return lax.dot_general(a, b, (((1,), (0,)), ((), ())), preferred_element_type=f32)


def dot_nt(a, b):
    return lax.dot_general(a, b, (((1,), (1,)), ((), ())), preferred_element_type=f32)


def dot_tn(a, b):
    return lax.dot_general(a, b, (((0,), (0,)), ((), ())), preferred_element_type=f32)


def cost(flops, moved, special=0):
    share = 20000
    return pl.CostEstimate(
        flops=int(flops) // share,
        bytes_accessed=int(moved) // share,
        transcendentals=int(special) // share,
    )


def whole(shape):
    return pl.BlockSpec(shape, lambda *_: (0,) * len(shape))


def once(shape, place=None):
    place = place or (lambda *_: (0,) * len(shape))
    return pl.BlockSpec(shape, place, pipeline_mode=pl.Buffered(1))


def normalised(values):
    center = values - jnp.mean(values, -1, keepdims=True)
    spread = jnp.mean(center * center, -1, keepdims=True)
    rstd = lax.rsqrt(spread + 1e-05)
    return center * rstd, rstd


def norm_back(grad, hat, rstd, gain):
    scaled = grad * gain
    mean_one = jnp.mean(scaled, -1, keepdims=True)
    mean_two = jnp.mean(scaled * hat, -1, keepdims=True)
    return rstd * (scaled - mean_one - hat * mean_two)


def enter_kernel(own_ref, head_ref, out_ref, row_ref, cells_ref):
    columns = own_ref.shape[1]
    for r in range(WIN):
        row = own_ref[SHIFT + r] if r < WIN - SHIFT else head_ref[r - (WIN - SHIFT)]
        row_ref[0:columns, :] = row.astype(f32)
        row_ref[columns : columns + SHIFT, :] = row_ref[0:SHIFT, :]
        for w in range(columns // WIN):
            at = w * CELLS + r * WIN
            cells_ref[at : at + WIN, :] = row_ref[w * WIN + SHIFT : (w + 1) * WIN + SHIFT, :]
    for w in range(columns // WIN):
        at = slice(w * CELLS, (w + 1) * CELLS)
        out_ref[at, :] = cells_ref[at, :].astype(bf16)


def enter(own, head):
    rows, columns, width = own.shape
    cells = rows * columns
    return pl.pallas_call(
        enter_kernel,
        out_shape=jax.ShapeDtypeStruct((cells, width), bf16),
        scratch_shapes=[
            pltpu.VMEM((columns + 2 * WIN, width), f32),
            pltpu.VMEM((cells, width), f32),
        ],
        compiler_params=params(14),
        cost_estimate=cost(0, 4 * cells * width),
        name="enter",
    )(own, head)


def leave_kernel(cells_ref, keep_ref, send_ref, row_ref, wide_ref):
    columns = keep_ref.shape[1]
    for w in range(columns // WIN):
        at = slice(w * CELLS, (w + 1) * CELLS)
        wide_ref[at, :] = cells_ref[at, :].astype(f32)
    for r in range(WIN):
        for w in range(columns // WIN):
            at = w * CELLS + r * WIN
            row_ref[w * WIN + SHIFT : (w + 1) * WIN + SHIFT, :] = wide_ref[at : at + WIN, :]
        row_ref[0:SHIFT, :] = row_ref[columns : columns + SHIFT, :]
        row = row_ref[0:columns, :].astype(bf16)
        if r < WIN - SHIFT:
            keep_ref[r] = row
        else:
            send_ref[r - (WIN - SHIFT)] = row


def leave(cells, columns):
    width = cells.shape[1]
    return pl.pallas_call(
        leave_kernel,
        out_shape=[
            jax.ShapeDtypeStruct((WIN - SHIFT, columns, width), bf16),
            jax.ShapeDtypeStruct((SHIFT, columns, width), bf16),
        ],
        scratch_shapes=[
            pltpu.VMEM((columns + 2 * WIN, width), f32),
            pltpu.VMEM(cells.shape, f32),
        ],
        compiler_params=params(14),
        cost_estimate=cost(0, 4 * cells.size),
        name="leave",
    )(cells)


def qkv_kernel(stream, x_ref, gain_ref, bias_ref, w_ref, a_ref, out_ref):
    rows, width = x_ref.shape
    block = row_block(rows)
    row = slice(stream, stream + 1)
    ats = [slice(i * block, (i + 1) * block) for i in range(rows // block)]

    @pl.when(pl.program_id(0) == 0)
    def _():
        for at in ats:
            hat, _ = normalised(x_ref[at, :].astype(f32))
            low = (hat * gain_ref[row, :] + bias_ref[row, :]).astype(bf16)
            a_ref[at, :] = low
            out_ref[at, :] = dot_nn(low, w_ref[...]).astype(bf16)

    @pl.when(pl.program_id(0) != 0)
    def _():
        for at in ats:
            out_ref[at, :] = dot_nn(a_ref[at, :], w_ref[...]).astype(bf16)


def norm_qkv(x, gain, bias, weight, stream):
    rows, width = x.shape
    full = weight.shape[-1]
    return pl.pallas_call(
        functools.partial(qkv_kernel, stream),
        grid=(full // width,),
        in_specs=[
            whole((rows, width)),
            whole(gain.shape),
            whole(bias.shape),
            pl.BlockSpec((None, width, width), lambda j: (stream, 0, j)),
        ],
        out_specs=[whole((rows, width)), pl.BlockSpec((rows, width), lambda j: (0, j))],
        out_shape=[
            jax.ShapeDtypeStruct((rows, width), bf16),
            jax.ShapeDtypeStruct((rows, full), bf16),
        ],
        compiler_params=params(8 + rows // 80),
        cost_estimate=cost(2 * rows * width * full, 2 * rows * (2 * width + full) + 2 * width * full),
        name="norm_qkv",
    )(x, gain, bias, weight)


def first_half(shape):
    return lax.broadcasted_iota(jnp.int32, shape, len(shape) - 1) < PAIR // 2


def stacked(block):
    left = first_half(block.shape)
    zero = jnp.zeros_like(block)
    return jnp.concatenate([jnp.where(left, block, zero), jnp.where(left, zero, block)], 0)


def row_sums(values):
    ones = jnp.ones((8, PAIR), f32)
    return lax.dot_general(
        ones,
        values,
        (((1,), (1,)), ((), ())),
        precision=lax.Precision.HIGHEST,
        preferred_element_type=f32,
    )[:1]


def joined(upright):
    rows = upright.shape[0] // 2
    return jnp.where(first_half((rows, PAIR)), upright[:rows], upright[rows:])


def unstacked(turned):
    return joined(turned.T)


def query_forward_kernel(
    qq_ref, k_ref, v_ref, ko_ref, vo_ref, bias_ref, out_ref, stats_ref, s_ref, lse_ref
):
    queries = qq_ref.shape[0]
    cells = k_ref.shape[0]
    own = ko_ref.shape[0]
    scaled = stacked(qq_ref[...] * 0.125)
    bias = bias_ref[...]
    self_score = dot_nt(ko_ref[...], scaled) + jnp.concatenate([bias, bias], 1)
    top = jnp.max(self_score, 0, keepdims=True)
    block = row_block(cells)
    blocks = [slice(i * block, (i + 1) * block) for i in range(cells // block)]
    for at in blocks:
        score = dot_nt(k_ref[at, :], scaled)
        s_ref[at, :] = score
        top = jnp.maximum(top, jnp.max(score, 0, keepdims=True))
    prob = jnp.exp(self_score - top)
    total = jnp.sum(prob, 0, keepdims=True)
    mixed = dot_nn(vo_ref[...].T, prob.astype(bf16))
    for at in blocks:
        prob = jnp.exp(s_ref[at, :] - top)
        total = total + jnp.sum(prob, 0, keepdims=True)
        mixed = mixed + dot_nn(v_ref[at, :].T, prob.astype(bf16))
    out_ref[...] = unstacked(mixed * (1.0 / total))
    lse = top + jnp.log(total)
    pair = pl.program_id(0)

    @pl.when(pair == 0)
    def _():
        lse_ref[...] = jnp.zeros_like(lse_ref)

    lse_ref[pl.ds(2 * pair, 1), :] = lse[:, :queries]
    lse_ref[pl.ds(2 * pair + 1, 1), :] = lse[:, queries:]

    @pl.when(pair == pl.num_programs(0) - 1)
    def _():
        stats_ref[...] = lse_ref[...].T


def query_forward(query_qkv, own_qkv, vis_qkv, self_bias):
    cells = vis_qkv.shape[0]
    queries = query_qkv.shape[0]
    own = own_qkv.shape[0]
    width = query_qkv.shape[1] // 3
    pairs = width // PAIR
    keys = cells + own

    def part(rows, j):
        return pl.BlockSpec((rows, PAIR), lambda p, j=j: (0, j * pairs + p))

    return pl.pallas_call(
        query_forward_kernel,
        grid=(pairs,),
        in_specs=[
            part(queries, 0),
            part(cells, 1),
            part(cells, 2),
            part(own, 1),
            part(own, 2),
            whole(self_bias.shape),
        ],
        out_specs=[part(queries, 0), whole((queries, PAIR))],
        out_shape=[
            jax.ShapeDtypeStruct((queries, width), f32),
            jax.ShapeDtypeStruct((queries, PAIR), f32),
        ],
        scratch_shapes=[
            pltpu.VMEM((cells, 2 * queries), f32),
            pltpu.VMEM((PAIR, queries), f32),
        ],
        compiler_params=params(10 + queries // 32),
        cost_estimate=cost(
            4 * 2 * queries * keys * width, 4 * cells * width, 2 * queries * keys * pairs
        ),
        name="query_forward",
    )(query_qkv, vis_qkv, vis_qkv, own_qkv, own_qkv, self_bias)


def window_forward_kernel(
    windows,
    q_ref,
    k_ref,
    v_ref,
    kq_ref,
    vq_ref,
    row_ref,
    col_ref,
    open_ref,
    out_ref,
    lse_ref,
    scaled_ref,
    near_ref,
    mixed_ref,
    far_ref,
):
    cells = [slice(w * CELLS, (w + 1) * CELLS) for w in range(windows)]
    lanes = [slice(2 * w * CELLS, 2 * (w + 1) * CELLS) for w in range(windows)]
    tops = []
    for w in range(windows):
        scaled = stacked(q_ref[cells[w], :] * 0.125)
        scaled_ref[lanes[w], :] = scaled
        near = dot_nt(k_ref[cells[w], :], scaled)
        near = jnp.where(col_ref[w] == row_ref[w], near, MASKED)
        near_ref[w] = near
        tops.append(jnp.max(near, 0, keepdims=True))
    far = dot_nt(kq_ref[...], scaled_ref[...]) + open_ref[...]
    top = jnp.maximum(jnp.concatenate(tops, 1), jnp.max(far, 0, keepdims=True))
    far = jnp.exp(far - top)
    total = jnp.sum(far, 0, keepdims=True)
    far_mixed = dot_nn(vq_ref[...].T, far.astype(bf16))
    totals = []
    for w in range(windows):
        near = jnp.exp(near_ref[w] - top[:, lanes[w]])
        totals.append(jnp.sum(near, 0, keepdims=True))
        mixed_ref[w] = dot_nn(v_ref[cells[w], :].T, near.astype(bf16))
    total = total + jnp.concatenate(totals, 1)
    share = 1.0 / total
    lse_ref[...] = top + jnp.log(total)
    far_ref[...] = far_mixed
    for w in range(windows):
        turned = (mixed_ref[w] + far_ref[:, lanes[w]]) * share[:, lanes[w]]
        out_ref[cells[w], :] = joined(turned.astype(bf16).T)


def window_forward(vis_qkv, query_qkv, region_row, region_col, closed):
    cells = vis_qkv.shape[0]
    queries = query_qkv.shape[0]
    width = vis_qkv.shape[1] // 3
    pairs = width // PAIR
    windows = cells // CELLS

    def part(rows, j):
        return pl.BlockSpec((rows, PAIR), lambda p, j=j: (0, j * pairs + p))

    return pl.pallas_call(
        functools.partial(window_forward_kernel, windows),
        grid=(pairs,),
        in_specs=[
            part(cells, 0),
            part(cells, 1),
            part(cells, 2),
            part(queries, 1),
            part(queries, 2),
            whole(region_row.shape),
            whole(region_col.shape),
            whole(closed.shape),
        ],
        out_specs=[
            part(cells, 0),
            pl.BlockSpec((None, 1, 2 * cells), lambda p: (p, 0, 0)),
        ],
        out_shape=[
            jax.ShapeDtypeStruct((cells, width), bf16),
            jax.ShapeDtypeStruct((pairs, 1, 2 * cells), f32),
        ],
        scratch_shapes=[
            pltpu.VMEM((2 * cells, PAIR), bf16),
            pltpu.VMEM((windows, CELLS, 2 * CELLS), f32),
            pltpu.VMEM((windows, PAIR, 2 * CELLS), f32),
            pltpu.VMEM((PAIR, 2 * cells), f32),
        ],
        compiler_params=params(56),
        cost_estimate=cost(
            8 * cells * (CELLS + queries) * width,
            8 * cells * width,
            2 * pairs * cells * (CELLS + queries),
        ),
        name="window_forward",
    )(vis_qkv, vis_qkv, vis_qkv, query_qkv, query_qkv, region_row, region_col, closed)


def attention_backward_kernel(
    windows,
    first,
    q_ref,
    k_ref,
    v_ref,
    do_ref,
    qq_ref,
    kq_ref,
    vq_ref,
    doq_ref,
    ko_ref,
    vo_ref,
    row_ref,
    col_ref,
    open_ref,
    bias_ref,
    lse_ref,
    lseq_ref,
    mixq_ref,
    *rest,
):
    if len(rest) > 16:
        rest = rest[3:]
    attention_backward_body(
        windows,
        first,
        q_ref,
        k_ref,
        v_ref,
        do_ref,
        qq_ref,
        kq_ref,
        vq_ref,
        doq_ref,
        ko_ref,
        vo_ref,
        row_ref,
        col_ref,
        open_ref,
        bias_ref,
        lse_ref,
        lseq_ref,
        mixq_ref,
        *rest,
    )


def attention_backward_body(
    windows,
    first,
    q_ref,
    k_ref,
    v_ref,
    do_ref,
    qq_ref,
    kq_ref,
    vq_ref,
    doq_ref,
    ko_ref,
    vo_ref,
    row_ref,
    col_ref,
    open_ref,
    bias_ref,
    lse_ref,
    lseq_ref,
    mixq_ref,
    dq_ref,
    dk_ref,
    dv_ref,
    dqq_ref,
    dkq_ref,
    dvq_ref,
    dko_ref,
    dvo_ref,
    scaled_ref,
    grad_ref,
    near_ref,
    neart_ref,
    seenk_ref,
    seenv_ref,
    far_ref,
    stats_ref,
):
    cells = [slice(w * CELLS, (w + 1) * CELLS) for w in range(windows)]
    lanes = [slice(2 * w * CELLS, 2 * (w + 1) * CELLS) for w in range(windows)]
    lse = lse_ref[...]

    deltas = []
    for w in range(windows):
        scaled = stacked(q_ref[cells[w], :] * 0.125)
        grad = stacked(do_ref[cells[w], :])
        scaled_ref[lanes[w], :] = scaled
        grad_ref[lanes[w], :] = grad
        near = dot_nt(k_ref[cells[w], :], scaled)
        near = jnp.exp(jnp.where(col_ref[w] == row_ref[w], near, MASKED) - lse[:, lanes[w]])
        near_t = near * dot_nt(v_ref[cells[w], :], grad)
        near_ref[w] = near
        neart_ref[w] = near_t
        deltas.append(jnp.sum(near_t, 0, keepdims=True))
    kq = kq_ref[...]
    far = jnp.exp(dot_nt(kq, scaled_ref[...]) + open_ref[...] - lse)
    far_t = far * dot_nt(vq_ref[...], grad_ref[...])
    delta = jnp.concatenate(deltas, 1) + jnp.sum(far_t, 0, keepdims=True)
    far_d = (far_t - far * delta).astype(bf16)
    dkq_ref[...] = dot_nn(far_d, scaled_ref[...]).astype(bf16)
    dvq_ref[...] = dot_nn(far.astype(bf16), grad_ref[...]).astype(bf16)
    far_ref[...] = dot_nn(kq.T, far_d).T

    scaled_q = stacked(qq_ref[...] * 0.125)
    grad_q = stacked(doq_ref[...])
    stats_ref[...] = lseq_ref[...].T
    head = 2 * (first + pl.program_id(0))
    lse_q = jnp.concatenate(
        [stats_ref[pl.ds(head, 1), :], stats_ref[pl.ds(head + 1, 1), :]], 1
    )
    mix_q = mixq_ref[...]
    delta_q = row_sums(grad_q.astype(f32) * jnp.concatenate([mix_q, mix_q], 0))
    bias = bias_ref[...]
    prob = jnp.exp(dot_nt(ko_ref[...], scaled_q) + jnp.concatenate([bias, bias], 1) - lse_q)
    dscore = (prob * (dot_nt(vo_ref[...], grad_q) - delta_q)).astype(bf16)
    dko_ref[...] = dot_nn(dscore, scaled_q)
    dvo_ref[...] = dot_nn(prob.astype(bf16), grad_q)
    turned = dot_nn(ko_ref[...].T, dscore)
    rows = k_ref.shape[0]
    block = row_block(rows)
    for i in range(rows // block):
        at = slice(i * block, (i + 1) * block)
        k_rows = k_ref[at, :]
        prob = jnp.exp(dot_nt(k_rows, scaled_q) - lse_q)
        dscore = (prob * (dot_nt(v_ref[at, :], grad_q) - delta_q)).astype(bf16)
        seenk_ref[at, :] = dot_nn(dscore, scaled_q)
        seenv_ref[at, :] = dot_nn(prob.astype(bf16), grad_q)
        turned = turned + dot_nn(k_rows.T, dscore)
    dqq_ref[...] = (unstacked(turned) * 0.125).astype(bf16)

    for w in range(windows):
        near = near_ref[w]
        near_d = (neart_ref[w] - near * delta[:, lanes[w]]).astype(bf16)
        upright = dot_nn(k_ref[cells[w], :].T, near_d).T + far_ref[lanes[w], :]
        dq_ref[cells[w], :] = (joined(upright) * 0.125).astype(bf16)
        dk_ref[cells[w], :] = (
            dot_nn(near_d, scaled_ref[lanes[w], :]) + seenk_ref[cells[w], :]
        ).astype(bf16)
        dv_ref[cells[w], :] = (
            dot_nn(near.astype(bf16), grad_ref[lanes[w], :]) + seenv_ref[cells[w], :]
        ).astype(bf16)


def attention_backward(
    vis_qkv,
    query_qkv,
    own_qkv,
    grad,
    grad_q,
    region_row,
    region_col,
    closed,
    self_bias,
    lse,
    joint_q,
    first,
    count,
    begun=(),
):
    cells = vis_qkv.shape[0]
    queries = query_qkv.shape[0]
    own = own_qkv.shape[0]
    width = vis_qkv.shape[1] // 3
    pairs = width // PAIR
    windows = cells // CELLS

    def part(rows, j):
        return pl.BlockSpec((rows, PAIR), lambda p, j=j: (0, j * pairs + first + p))

    def result(rows):
        return pl.BlockSpec((rows, PAIR), lambda p: (0, p))

    def filled(rows):
        return pl.BlockSpec((rows, PAIR), lambda p: (0, first + p))

    def stats(array):
        return pl.BlockSpec((None,) + array.shape[1:], lambda p: (first + p, 0, 0))

    span = count * PAIR
    return pl.pallas_call(
        functools.partial(attention_backward_kernel, windows, first),
        grid=(count,),
        in_specs=[
            part(cells, 0),
            part(cells, 1),
            part(cells, 2),
            part(cells, 0),
            part(queries, 0),
            part(queries, 1),
            part(queries, 2),
            part(queries, 0),
            part(own, 1),
            part(own, 2),
            whole(region_row.shape),
            whole(region_col.shape),
            whole(closed.shape),
            whole(self_bias.shape),
            stats(lse),
            pl.BlockSpec((queries, PAIR), lambda p: (0, pairs)),
            part(queries, 0),
        ]
        + [pl.BlockSpec(memory_space=pl.ANY)] * len(begun),
        out_specs=[filled(cells)] * 3 + [result(queries)] * 3 + [result(own)] * 2,
        out_shape=[jax.ShapeDtypeStruct((cells, width), bf16)] * 3
        + [jax.ShapeDtypeStruct((queries, span), bf16)] * 3
        + [jax.ShapeDtypeStruct((own, span), f32)] * 2,
        scratch_shapes=[
            pltpu.VMEM((2 * cells, PAIR), bf16),
            pltpu.VMEM((2 * cells, PAIR), bf16),
            pltpu.VMEM((windows, CELLS, 2 * CELLS), f32),
            pltpu.VMEM((windows, CELLS, 2 * CELLS), f32),
            pltpu.VMEM((cells, PAIR), f32),
            pltpu.VMEM((cells, PAIR), f32),
            pltpu.VMEM((2 * cells, PAIR), f32),
            pltpu.VMEM((PAIR, queries), f32),
        ],
        compiler_params=params(16 + queries // 25),
        cost_estimate=cost(
            20 * cells * (CELLS + 2 * queries) * span,
            14 * cells * span,
            2 * count * cells * (CELLS + 2 * queries),
        ),
        input_output_aliases={17 + i: i for i in range(len(begun))},
        name="attention_backward",
    )(
        vis_qkv,
        vis_qkv,
        vis_qkv,
        grad,
        query_qkv,
        query_qkv,
        query_qkv,
        grad_q,
        own_qkv,
        own_qkv,
        region_row,
        region_col,
        closed,
        self_bias,
        lse,
        joint_q,
        joint_q,
        *begun,
    )


def gelu_pair(z):
    below = 0.5 + 0.5 * lax.erf(z * 0.7071067811865476)
    bell = jnp.exp(-0.5 * z * z)
    return z * below, below + z * bell * 0.3989422804014327


def ffn_forward_kernel(
    stream,
    x_ref,
    o_ref,
    wo_ref,
    bo_ref,
    gain_ref,
    bias_ref,
    wu_ref,
    bu_ref,
    wd_ref,
    bd_ref,
    x1_ref,
    b_ref,
    hid_ref,
    slope_ref,
    out_ref,
    sum_ref,
):
    rows, width = x_ref.shape
    block = row_block(rows)
    count = rows // block
    ats = [slice(i * block, (i + 1) * block) for i in range(count)]
    step = pl.program_id(0)
    row = slice(stream, stream + 1)

    @pl.when(step == 0)
    def _():
        for at in ats:
            x1 = x_ref[at, :].astype(f32) + dot_nn(o_ref[at, :].astype(bf16), wo_ref[...]) + bo_ref[row, :]
            x1_ref[at, :] = x1
            hat, _ = normalised(x1)
            b_ref[at, :] = (hat * gain_ref[row, :] + bias_ref[row, :]).astype(bf16)
            sum_ref[at, :] = x1 + bd_ref[row, :]

    def project(i):
        return dot_nn(b_ref[ats[i], :], wu_ref[...]) + bu_ref[row, :]

    z = project(0)
    for i in range(count):
        ahead = project(i + 1) if i + 1 < count else None
        hidden, slope = gelu_pair(z)
        hidden = hidden.astype(bf16)
        hid_ref[ats[i], :] = hidden
        slope_ref[ats[i], :] = slope.astype(bf16)
        sum_ref[ats[i], :] += dot_nn(hidden, wd_ref[...])
        z = ahead

    @pl.when(step == pl.num_programs(0) - 1)
    def _():
        out_ref[...] = sum_ref[...].astype(bf16)


def ffn_forward(x, attended, out_w, out_b, gain, bias, up_w, up_b, down_w, down_b, stream):
    rows, width = x.shape
    hidden = up_w.shape[-1]
    chunk = 768
    return pl.pallas_call(
        functools.partial(ffn_forward_kernel, stream),
        grid=(hidden // chunk,),
        in_specs=[
            once((rows, width)),
            once((rows, width)),
            once((None, width, width), lambda f: (stream, 0, 0)),
            whole(out_b.shape),
            whole(gain.shape),
            whole(bias.shape),
            pl.BlockSpec((None, width, chunk), lambda f: (stream, 0, f)),
            pl.BlockSpec((2, chunk), lambda f: (0, f)),
            pl.BlockSpec((None, chunk, width), lambda f: (stream, f, 0)),
            whole(down_b.shape),
        ],
        out_specs=[
            whole((rows, width)),
            whole((rows, width)),
            pl.BlockSpec((rows, chunk), lambda f: (0, f)),
            pl.BlockSpec((rows, chunk), lambda f: (0, f)),
            whole((rows, width)),
        ],
        out_shape=[
            jax.ShapeDtypeStruct((rows, width), f32),
            jax.ShapeDtypeStruct((rows, width), bf16),
            jax.ShapeDtypeStruct((rows, hidden), bf16),
            jax.ShapeDtypeStruct((rows, hidden), bf16),
            jax.ShapeDtypeStruct((rows, width), bf16),
        ],
        scratch_shapes=[pltpu.VMEM((rows, width), f32)],
        compiler_params=params(34 if stream == 0 else 56),
        cost_estimate=cost(
            2 * rows * width * (2 * hidden + width),
            4 * width * hidden + 4 * rows * hidden + 12 * rows * width,
            2 * rows * hidden,
        ),
        name="ffn_forward",
    )(x, attended, out_w, out_b, gain, bias, up_w, up_b, down_w, down_b)


def ffn_backward_kernel(
    stream,
    g_ref,
    slope_ref,
    x1_ref,
    wd_ref,
    wu_ref,
    wo_ref,
    gain_ref,
    dz_ref,
    dx1_ref,
    du_ref,
    do_ref,
    sums_ref,
    sum_ref,
):
    rows, width = g_ref.shape
    block = row_block(rows)
    count = rows // block
    ats = [slice(i * block, (i + 1) * block) for i in range(count)]
    step = pl.program_id(0)
    row = slice(stream, stream + 1)

    @pl.when(step == 0)
    def _():
        sum_ref[...] = jnp.zeros_like(sum_ref)

    up_bias = jnp.zeros((1, dz_ref.shape[1]), f32)

    def pulled(i):
        return dot_nt(g_ref[ats[i], :], wd_ref[...])

    grad = pulled(0)
    for i in range(count):
        ahead = pulled(i + 1) if i + 1 < count else None
        dz = grad * slope_ref[ats[i], :].astype(f32)
        low = dz.astype(bf16)
        dz_ref[ats[i], :] = low
        up_bias = up_bias + jnp.sum(dz, 0, keepdims=True)
        sum_ref[ats[i], :] += dot_nt(low, wu_ref[...])
        grad = ahead
    sums_ref[pl.ds(4 + step, 1), :] = up_bias

    @pl.when(step == pl.num_programs(0) - 1)
    def _():
        sums_ref[0:4, :] = jnp.zeros((4, width), f32)
        for at in ats:
            hat, rstd = normalised(x1_ref[at, :])
            db = sum_ref[at, :]
            g = g_ref[at, :].astype(f32)
            dx1 = g + norm_back(db, hat, rstd, gain_ref[row, :])
            dx1_ref[at, :] = dx1
            du = dx1.astype(bf16)
            du_ref[at, :] = du
            do_ref[at, :] = dot_nt(du, wo_ref[...]).astype(bf16)
            sums_ref[0:1, :] += jnp.sum(db * hat, 0, keepdims=True)
            sums_ref[1:2, :] += jnp.sum(db, 0, keepdims=True)
            sums_ref[2:3, :] += jnp.sum(dx1, 0, keepdims=True)
            sums_ref[3:4, :] += jnp.sum(g, 0, keepdims=True)


def ffn_backward(g, slope, x1, down_w, up_w, out_w, gain, stream):
    rows, width = g.shape
    hidden = up_w.shape[-1]
    chunk = width
    return pl.pallas_call(
        functools.partial(ffn_backward_kernel, stream),
        grid=(hidden // chunk,),
        in_specs=[
            once((rows, width)),
            pl.BlockSpec((rows, chunk), lambda f: (0, f)),
            once((rows, width)),
            pl.BlockSpec((None, chunk, width), lambda f: (stream, f, 0)),
            pl.BlockSpec((None, width, chunk), lambda f: (stream, 0, f)),
            once((None, width, width), lambda f: (stream, 0, 0)),
            whole(gain.shape),
        ],
        out_specs=[
            pl.BlockSpec((None, rows, chunk), lambda f: (f, 0, 0)),
            whole((rows, width)),
            whole((rows, width)),
            whole((rows, width)),
            whole((4 + hidden // chunk, width)),
        ],
        out_shape=[
            jax.ShapeDtypeStruct((hidden // chunk, rows, chunk), bf16),
            jax.ShapeDtypeStruct((rows, width), f32),
            jax.ShapeDtypeStruct((rows, width), bf16),
            jax.ShapeDtypeStruct((rows, width), bf16),
            jax.ShapeDtypeStruct((4 + hidden // chunk, width), f32),
        ],
        scratch_shapes=[pltpu.VMEM((rows, width), f32)],
        compiler_params=params(34 if stream == 0 else 56),
        cost_estimate=cost(
            2 * rows * width * (2 * hidden + width),
            4 * width * hidden + 4 * rows * hidden + 14 * rows * width,
        ),
        name="ffn_backward",
    )(g, slope, x1, down_w, up_w, out_w, gain)


def input_kernel(stream, dq_ref, dk_ref, dv_ref, w_ref, x_ref, dx1_ref, gain_ref, out_ref, sums_ref):
    width = x_ref.shape[1]

    @pl.when(pl.program_id(0) == 0)
    def _():
        sums_ref[...] = jnp.zeros_like(sums_ref)

    grad = dot_nt(dq_ref[...], w_ref[:, :width])
    grad = grad + dot_nt(dk_ref[...], w_ref[:, width : 2 * width])
    grad = grad + dot_nt(dv_ref[...], w_ref[:, 2 * width :])
    hat, rstd = normalised(x_ref[...].astype(f32))
    out_ref[...] = (
        dx1_ref[...] + norm_back(grad, hat, rstd, gain_ref[stream : stream + 1, :])
    ).astype(bf16)
    at = 4 * stream
    sums_ref[at : at + 1, :] += jnp.sum(grad * hat, 0, keepdims=True)
    sums_ref[at + 1 : at + 2, :] += jnp.sum(grad, 0, keepdims=True)


def input_grad(dq, dk, dv, weight, x, dx1, gain, stream):
    rows, width = x.shape
    block = row_block(rows)
    rows_spec = pl.BlockSpec((block, width), lambda i: (i, 0))
    return pl.pallas_call(
        functools.partial(input_kernel, stream),
        grid=(rows // block,),
        in_specs=[rows_spec] * 3
        + [
            pl.BlockSpec((None, width, 3 * width), lambda i: (stream, 0, 0)),
            rows_spec,
            rows_spec,
            whole(gain.shape),
        ],
        out_specs=[rows_spec, whole((8, width))],
        out_shape=[
            jax.ShapeDtypeStruct((rows, width), bf16),
            jax.ShapeDtypeStruct((8, width), f32),
        ],
        compiler_params=params(16),
        cost_estimate=cost(6 * rows * width * width, 14 * rows * width + 6 * width * width),
        name="input_grad",
    )(dq, dk, dv, weight, x, dx1, gain)


def after(value, *before):
    return lax.optimization_barrier((value,) + before)[0]


def beside(made, *flights):
    return lax.optimization_barrier((made,) + flights)


def moved(block, axis, step):
    size = lax.axis_size(axis)
    return lax.ppermute(block, axis, [(i, (i + step) % size) for i in range(size)])


def swapped(block, axis, mask):
    size = lax.axis_size(axis)
    return lax.ppermute(block, axis, [(i, i ^ mask) for i in range(size)])


def other_core(block):
    return swapped(block, "strip", 1)


def place():
    strip = lax.axis_index("strip")
    return lax.axis_size("strip") // 2, strip // 2, strip % 2


def pick(block, index, axis=0):
    return lax.dynamic_index_in_dim(block, index, axis, keepdims=False)


def added(blocks, kind=bf16):
    total = blocks[0].astype(f32)
    for block in blocks[1:]:
        total = total + block.astype(f32)
    return total.astype(kind)


def bit_of(axis, mask):
    return (lax.axis_index(axis) // mask) % 2


class Phase:
    def __init__(self, blocks, dims, axis, mask):
        bit = bit_of(axis, mask)
        theirs, self.mine = [
            [added([pick(term, half, dim) for term in terms]) for terms, dim in zip(blocks, dims)]
            for half in (1 - bit, bit)
        ]
        self.shapes = [block.shape for block in theirs]
        self.sent, self.got = exchange(theirs, axis, mask)

    def terms(self):
        got = parted(self.got, self.shapes)
        return [[mine, more] for mine, more in zip(self.mine, got)]

    def sums(self):
        return [added(terms) for terms in self.terms()]


def mapped(change, terms):
    return [change(term) for term in terms]


class Gather:
    def __init__(self, blocks, dims, axis, mask):
        self.bit = bit_of(axis, mask)
        self.blocks, self.dims = blocks, dims
        self.shapes = [block.shape for block in blocks]
        self.sent, self.got = exchange(blocks, axis, mask)

    def pairs(self):
        first = self.bit == 0
        return [
            jnp.stack([jnp.where(first, one, two), jnp.where(first, two, one)], dim)
            for one, two, dim in zip(self.blocks, parted(self.got, self.shapes), self.dims)
        ]


class PageGather:
    def __init__(self, blocks):
        self.shapes = [block.shape for block in blocks]
        rows = [block.reshape(-1, block.shape[-1]) for block in blocks]
        self.sent = jnp.concatenate(rows, 0)
        self.got = [swapped(self.sent, "page", mask) for mask in (1, 2, 3)]

    def whole(self):
        def ordered(bit, one, two, axis):
            first = bit == 0
            return jnp.stack([jnp.where(first, one, two), jnp.where(first, two, one)], axis)

        every = [parted(rows, self.shapes) for rows in [self.sent] + list(self.got)]
        result = []
        for mine, by_x, by_y, by_both in zip(*every):
            near = ordered(bit_of("page", 1), mine, by_x, 1)
            far = ordered(bit_of("page", 1), by_y, by_both, 1)
            result.append(from_page(ordered(bit_of("page", 2), near, far, 1)))
        return result


def parted(rows, shapes):
    if len(shapes) == 1:
        return [rows]
    blocks, at = [], 0
    for shape in shapes:
        count = 1
        for size in shape[:-1]:
            count *= size
        blocks.append(rows[at : at + count].reshape(shape))
        at += count
    return blocks


def exchange(blocks, axis, mask):
    if len(blocks) == 1:
        sent = blocks[0]
    else:
        sent = jnp.concatenate([block.reshape(-1, block.shape[-1]) for block in blocks], 0)
    return sent, swapped(sent, axis, mask)


def by_core(grad):
    strips = lax.axis_size("strip")
    return grad.reshape(strips // 2, 2, grad.shape[0] // strips, grad.shape[1])


def tiled(grad, width):
    count = grad.shape[-1] // width
    return jnp.stack([grad[..., i * width : (i + 1) * width] for i in range(count)], -3)


def untiled(blocks):
    return jnp.concatenate([blocks[i] for i in range(blocks.shape[0])], -1)


def by_page(blocks):
    rows = blocks.shape[-2]
    return blocks.reshape(blocks.shape[:-2] + (2, 2, rows // 4, blocks.shape[-1]))


def from_page(blocks):
    return blocks.reshape(blocks.shape[:-4] + (-1, blocks.shape[-1]))


def by_chip(blocks, axis):
    shape = blocks.shape
    return blocks.reshape(shape[:axis] + (shape[axis] // 2, 2) + shape[axis + 1 :])


def line_masks():
    size, _, _ = place()
    return [2 << i for i in range(size.bit_length() - 1)]


def line_phase(blocks, axes, mask):
    split = [
        [by_chip(term, axis) for term in terms] for terms, axis in zip(blocks, axes)
    ]
    return Phase(split, [axis + 1 for axis in axes], "strip", mask)


def line_first(blocks, axes):
    masks = line_masks()
    for mask in masks[:-2]:
        blocks = line_phase(blocks, axes, mask).terms()
    return line_phase(blocks, axes, masks[-2])


def line_last(blocks, axes):
    return line_phase(blocks, axes, line_masks()[-1])


def line_exchange(block):
    size, z, _ = place()
    return [pick(block, z)] + [
        moved(pick(block, (z + step) % size), "strip", 2 * step) for step in range(1, size)
    ]


def line_gather(block):
    size, _, _ = place()
    return [block] + [moved(block, "strip", 2 * step) for step in range(1, size)]


def line_order(blocks):
    size, z, _ = place()
    double = jnp.stack(blocks[:1] + blocks[:0:-1] + blocks[:1] + blocks[:0:-1])
    return lax.dynamic_slice_in_dim(double, (size - z) % size, size, 0)


def page_exchange(block):
    size = lax.axis_size("page")
    page = lax.axis_index("page")
    shares = block.reshape(size, block.shape[0] // size, block.shape[1])
    return [pick(shares, page)] + [
        swapped(pick(shares, page ^ mask), "page", mask) for mask in range(1, size)
    ]


def page_gather(block):
    size = lax.axis_size("page")
    return [block] + [swapped(block, "page", mask) for mask in range(1, size)]


def page_order(blocks):
    size = len(blocks)
    page = lax.axis_index("page")
    rows, columns = blocks[0].shape
    joined = jnp.zeros((size * rows, columns), f32)
    for mask, block in enumerate(blocks):
        joined = lax.dynamic_update_slice_in_dim(
            joined, block.astype(f32), (page ^ mask) * rows, 0
        )
    return joined


def core_order(mine, other):
    _, _, core = place()
    pair = jnp.stack(
        [jnp.where(core == 0, mine, other), jnp.where(core == 0, other, mine)], 1
    )
    return pair.reshape(-1, pair.shape[-1])


def merge_kernel(one_ref, two_ref, out_ref):
    width = one_ref.shape[1] - PAIR
    one_top = one_ref[:, width:]
    two_top = two_ref[:, width:]
    top = jnp.maximum(one_top, two_top)
    one_share = jnp.exp(one_top - top)
    two_share = jnp.exp(two_top - top)
    total = one_share + two_share
    shape = (PAIR, width)
    head = lax.broadcasted_iota(jnp.int32, shape, 1) // (width // HEADS)
    spread = (lax.broadcasted_iota(jnp.int32, shape, 0) == head).astype(f32)

    def over_heads(share):
        return jnp.dot(share / total, spread, precision=lax.Precision.HIGHEST)

    out_ref[:, :width] = one_ref[:, :width] * over_heads(one_share) + two_ref[
        :, :width
    ] * over_heads(two_share)
    out_ref[:, width:] = top + jnp.log(total)


def merged(one, two):
    shape = one.shape
    rows = one.size // shape[-1]
    out = pl.pallas_call(
        merge_kernel,
        out_shape=jax.ShapeDtypeStruct((rows, shape[-1]), f32),
        compiler_params=params(8),
        cost_estimate=cost(6 * one.size, 12 * one.size),
        name="merge",
    )(one.reshape(rows, -1), two.reshape(rows, -1))
    return out.reshape(shape)


def region_windows(rows):
    across = rows.shape[1] // WIN
    rolled = jnp.roll(rows, -SHIFT, axis=1)
    return rolled.reshape(WIN, across, WIN).transpose(1, 0, 2).reshape(across, CELLS)


def weight_grad(left, right):
    return dot_tn(left, right).astype(bf16)


def body(
    vis_tokens,
    query_tokens,
    region_ids,
    query_mask,
    answer_len,
    norm1_gain,
    norm1_bias,
    qkv_weight,
    out_weight,
    out_bias,
    norm2_gain,
    norm2_bias,
    up_weight,
    up_bias,
    down_weight,
    down_bias,
    vis_cotangent,
    query_cotangent,
):
    strips = lax.axis_size("strip")
    strip = lax.axis_index("strip")
    chips, z, core = place()
    local_rows, columns, features = vis_tokens.shape[1:]
    own_count = query_tokens.shape[1]
    query_count = query_mask.shape[1]
    total_rows = region_ids.shape[1]
    own_start = strip * own_count

    def own_rows(values):
        return lax.dynamic_slice_in_dim(values, own_start, own_count, 0)

    def own_columns(values):
        span = values.shape[1] // strips
        return lax.dynamic_slice_in_dim(values, strip * span, span, 1)

    tokens = line_gather(query_tokens[0])
    head_rows = moved(vis_tokens[0, :SHIFT], "strip", -1)
    tokens = line_order(tokens)
    query = core_order(tokens, other_core(tokens))

    key_open = query_mask[0] > 0
    key_ids = jnp.arange(query_count, dtype=jnp.int32)
    prompt = key_ids < query_count - answer_len[0]
    closed = jnp.where(key_open & prompt, 0.0, MASKED).astype(f32)[:, None]
    own_ids = own_start + jnp.arange(own_count, dtype=jnp.int32)
    allowed = own_rows(key_open)[:, None] & (
        own_rows(prompt)[:, None] | (own_ids[:, None] <= key_ids[None, :])
    )
    self_bias = jnp.where(allowed, 0.0, MASKED).astype(f32)
    row_ids = (strip * local_rows + SHIFT + jnp.arange(local_rows, dtype=jnp.int32)) % total_rows
    region = region_windows(jnp.take(region_ids[0], row_ids, axis=0))
    region_row = jnp.concatenate([region, region], 1)[:, None, :]
    region_col = region[:, :, None]

    query_norm, query_qkv = norm_qkv(query, norm1_gain, norm1_bias, qkv_weight, 1)
    (query_norm, query_qkv), head_rows = beside((query_norm, query_qkv), head_rows)
    own_qkv = own_rows(query_qkv)
    vis = enter(vis_tokens[0], head_rows)
    head_cot = moved(after(vis_cotangent[0, :SHIFT], vis), "strip", -1)
    vis_norm, vis_qkv = norm_qkv(vis, norm1_gain, norm1_bias, qkv_weight, 0)

    part = query_forward(query_qkv, own_qkv, vis_qkv, self_bias)
    part, head_cot = beside(part, head_cot)
    mine, theirs = [
        jnp.concatenate([pick(by_core(each), which, 1) for each in part], -1)
        for which in (core, 1 - core)
    ]
    others = other_core(theirs)
    vis_cot = enter(after(vis_cotangent[0], theirs), head_cot)
    vis_cot, mine, others = beside(vis_cot, mine, others)
    part = merged(mine, others)
    others = swapped(part, "strip", 2)

    vis_windows = window_forward(after(vis_qkv, part), query_qkv, region_row, region_col, closed)
    (vis_attn, vis_lse), part, others = beside(vis_windows, part, others)
    part = merged(part, others)
    mask = 4
    while 2 * mask < strips:
        part = merged(part, swapped(part, "strip", mask))
        mask = 2 * mask
    others = swapped(part, "strip", mask)

    weights = (out_weight, out_bias, norm2_gain, norm2_bias, up_weight, up_bias, down_weight, down_bias)
    made = ffn_forward(vis, after(vis_attn, part), *weights, 0)
    vis_x1, vis_b, vis_hid, vis_slope, vis_result = made
    vis_down = weight_grad(vis_hid, vis_cot)
    vis_down, part, others = beside(vis_down, part, others)
    part = merged(part, others)
    others = other_core(part)
    cotangents = line_gather(after(query_cotangent[0], part))
    down = by_core(vis_down)
    down = Phase([[down.reshape(chips, 2, -1, features // strips, features)]], [1], "strip", 1)

    made = ffn_backward(
        after(vis_cot, down.sent), vis_slope, vis_x1, down_weight, up_weight, out_weight, norm2_gain, 0
    )
    made, down.got, cotangents, others = beside(made, down.got, cotangents, others)
    cotangents = line_order(cotangents)
    cot_others = other_core(cotangents)
    vis_dz, vis_dx1, vis_du, vis_do, vis_sums = made
    (down,) = down.terms()
    down = Phase([mapped(by_page, down)], [3], "page", 1)
    hidden = up_weight.shape[-1] // features
    vis_b = after(vis_b, down.sent)
    up_a = [by_core(weight_grad(vis_b, vis_dz[i])) for i in range(hidden - 1)]
    up_a = Phase([[jnp.stack(up_a)]], [2], "strip", 1)
    up_b = [by_core(weight_grad(after(vis_b, up_a.sent), vis_dz[hidden - 1]))]
    up_b = Phase([[jnp.stack(up_b + [by_core(weight_grad(vis_attn, vis_du))])]], [2], "strip", 1)
    made = leave(after(vis_result, up_b.sent), columns)
    (vis_keep, vis_send), up_a.got, up_b.got = beside(made, up_a.got, up_b.got)
    vis_first = moved(vis_send, "strip", 1)
    up_a = line_first(up_a.terms(), [1])

    every = core_order(part, others)
    every, up_sent = beside(every, up_a.sent)
    made = ffn_forward(query, every, *weights, 1)
    made, down.got, cot_others = beside(made, down.got, cot_others)
    query_cot = core_order(cotangents, cot_others)
    query_x1, query_b, query_hid, query_slope, query_result = made
    (down,) = down.terms()
    down = Phase([down], [2], "page", 2)
    up_b = Phase([mapped(by_page, terms) for terms in up_b.terms()], [3], "page", 1)
    made = ffn_backward(
        query_cot,
        after(query_slope, up_b.sent, down.sent),
        query_x1,
        down_weight,
        up_weight,
        out_weight,
        norm2_gain,
        1,
    )
    made, up_a.got, up_b.got = beside(made, up_a.got, up_b.got)
    query_dz, query_dx1, query_du, query_do, query_sums = made
    (up_a,) = up_a.terms()
    (up_b,) = up_b.terms()
    up_a = Phase([mapped(by_page, up_a)], [3], "page", 1)
    up_b = Phase([up_b], [2], "page", 2)

    def query_grads(left, right):
        return weight_grad(own_columns(left), right)

    up_rows = features // strips
    query_dz = after(query_dz, up_a.sent, up_b.sent)
    one = jnp.concatenate(
        [
            jnp.stack([query_grads(query_b, query_dz[i]) for i in range(hidden)]),
            query_grads(every[:, :features].astype(bf16), query_du)[None],
            query_grads(query_hid, query_cot).reshape(-1, up_rows, features),
        ],
        0,
    )
    one, down.got = beside(one, down.got)
    one = Phase([[by_page(one)]], [2], "page", 1)
    down = line_first(down.terms(), [0])

    pairs = HEADS // 2
    half = pairs // 2

    def backward(values, first, begun=()):
        return attention_backward(
            values,
            query_qkv,
            own_qkv,
            vis_do,
            query_do,
            region_row,
            region_col,
            closed,
            self_bias,
            vis_lse,
            every,
            first,
            half,
            begun,
        )

    def head_grads(normed, grads, first):
        span = half * PAIR
        return jnp.stack(
            [
                by_core(weight_grad(normed, each[:, first * PAIR : first * PAIR + span]))
                for each in grads
            ],
            2,
        )

    back_one = backward(after(vis_qkv, one.sent, down.sent), 0)
    back_one, up_a.got, up_b.got, down.got, vis_first = beside(
        back_one, up_a.got, up_b.got, down.got, vis_first
    )
    first = Phase([[head_grads(vis_norm, back_one[:3], 0)]], [1], "strip", 1)
    first.sent, one.got = beside(first.sent, one.got)
    (up_a,) = up_a.terms()
    (one,) = one.terms()
    mixed_y = Phase([after(up_a, first.sent), one], [2, 1], "page", 2)
    up_b = line_first(up_b.terms(), [1])
    down = line_last(down.terms(), [0])
    down.sent, up_b.sent, mixed_y.sent, first.got = beside(
        down.sent, up_b.sent, mixed_y.sent, first.got
    )
    (first,) = first.terms()
    first = Phase([mapped(by_page, first)], [3], "page", 1)

    back_two = backward(
        after(vis_qkv, first.sent, mixed_y.sent, up_b.sent, down.sent), half, back_one[:3]
    )
    back_two, first.got, mixed_y.got, up_b.got, down.got = beside(
        back_two, first.got, mixed_y.got, up_b.got, down.got
    )
    part = jnp.stack(
        [by_core(each) for pair in zip(back_one[3:6], back_two[3:6]) for each in pair], 2
    )
    part = Phase([[part]], [1], "strip", 1)
    grads = head_grads(after(vis_norm, part.sent), back_two[:3], half)
    second = Phase([[grads]], [1], "strip", 1)
    second.sent, part.got = beside(second.sent, part.got)
    part = line_first(part.terms(), [0])
    up_a, one = mixed_y.terms()
    (up_b,) = up_b.terms()
    line = line_last([after(up_a, part.sent), up_b], [1, 1])
    line.sent, second.got = beside(line.sent, second.got)
    (second,) = second.terms()
    second = Phase([mapped(by_page, second)], [3], "page", 1)
    (down,) = down.sums()
    one = after(added(one), second.sent)
    early = Gather([one[:5], down[0]], [1, 1], "page", 1)
    early_y = Gather([one[5:]], [1], "page", 2)

    made = input_grad(
        after(back_two[0], part.sent, line.sent, second.sent, early.sent, early_y.sent),
        back_two[1],
        back_two[2],
        qkv_weight,
        vis,
        vis_dx1,
        norm1_gain,
        0,
    )
    made, part.got = beside(made, part.got)
    vis_input, vis_head = made
    part = line_last(part.terms(), [0])
    made = leave(after(vis_input, part.sent), columns)
    made, part.got, second.got, line.got = beside(made, part.got, second.got, line.got)
    grad_keep, grad_send = made
    (part,) = part.terms()
    own_self = [jnp.zeros_like(back_one[6])] * 2 + [back_one[6], back_two[6], back_one[7], back_two[7]]
    own_dqkv = added(mapped(lambda term: term[0], part) + [jnp.stack(own_self)])
    masks = line_masks()
    lined = own_dqkv[None]
    for mask in reversed(masks[1:-1]):
        lined = Gather([lined], [1], "strip", mask).pairs()[0]
        lined = lined.reshape((-1,) + own_dqkv.shape)
    lined = Gather([lined], [0], "strip", masks[-1])
    qkv = Phase(
        [after(terms, lined.sent) for terms in first.terms() + second.terms()], [2, 2], "page", 2
    )
    made = input_grad(
        untiled(after(own_dqkv, lined.sent, qkv.sent)[0:2]),
        untiled(own_dqkv[2:4]),
        untiled(own_dqkv[4:6]),
        qkv_weight,
        query_tokens[0],
        own_rows(query_dx1),
        norm1_gain,
        1,
    )
    made, lined.got, early.got, early_y.got = beside(made, lined.got, early.got, early_y.got)
    own_input, own_head = made
    lined = lined.pairs()[0].reshape((-1,) + own_dqkv.shape)
    lined = Gather([lined], [1], "strip", masks[0])
    one, down = after(early.pairs(), lined.sent)
    (one_b,) = after(early_y.pairs(), lined.sent)
    down = Gather([down], [1], "page", 2)

    small = jnp.concatenate([vis_sums, vis_head + own_head], 0)
    small_others = other_core(small)
    lined.got, small_others, qkv.got = beside(lined.got, small_others, qkv.got)
    small = small + small_others
    lined = lined.pairs()[0].reshape((-1,) + own_dqkv.shape)
    lined_others = other_core(lined)
    for mask in masks[:-2]:
        small = small + swapped(small, "strip", mask)
    small_others = swapped(small, "strip", masks[-2])
    qkv = line_first(after(qkv.terms(), lined), [0, 0])
    up_part, low_part = line.sums()
    up_gather = Gather([after(up_part, lined)[:, 0], low_part[:, 0]], [1, 1], "page", 1)
    grad_near = moved(after(grad_send[: SHIFT // 2], lined), "strip", 1)
    lined_others, small_others, down.got = beside(lined_others, small_others, down.got)
    one_first = Gather([after(one, down.got)], [1], "page", 2)
    small = small + small_others
    query_dqkv = jnp.stack(
        [jnp.where(core == 0, lined, lined_others), jnp.where(core == 0, lined_others, lined)], 1
    )
    query_dqkv = [query_dqkv[:, :, i].reshape(query_count, -1) for i in range(6)]
    three = query_grads(query_norm, jnp.concatenate(query_dqkv, 1))
    three = Phase([[by_page(tiled(three, half * PAIR))]], [2], "page", 1)
    small_others = swapped(small, "strip", masks[-1])
    three.got, qkv.got, small_others, up_gather.got, one_first.got, grad_near = beside(
        three.got, qkv.got, small_others, up_gather.got, one_first.got, grad_near
    )
    three = Phase(three.terms(), [1], "page", 2)
    qkv = line_last(after(qkv.terms(), three.sent), [0, 0])
    small = jnp.concatenate([small + small_others, query_sums], 0)
    last = Gather(after(up_gather.pairs(), three.sent), [1, 1], "page", 2)
    one_last = Gather([after(one_b, three.sent)], [2], "page", 1)
    three.got, qkv.got, small = beside(three.got, qkv.got, small)
    grad_far = moved(after(grad_send[SHIFT // 2 :], three.got), "strip", 1)
    small = tiled(small.astype(bf16), half * PAIR)
    late = PageGather([each[0] for each in qkv.sums()] + three.sums() + [small])

    up_a, up_b = [from_page(each) for each in last.pairs()]
    (one_last,) = [from_page(each) for each in one_last.pairs()]
    (down,) = [from_page(each) for each in down.pairs()]
    one = jnp.concatenate([from_page(each) for each in one_first.pairs()] + [one_last], 0)
    up = jnp.concatenate([up_a, up_b], 0)
    up_grad = jnp.stack([untiled(up[:hidden]), untiled(one[:hidden])]).astype(f32)
    out_grad = jnp.stack([up[hidden], one[hidden]]).astype(f32)
    down_grad = jnp.stack([down, one[hidden + 1 :]]).astype(f32).reshape(2, -1, features)
    vis_final = jnp.concatenate([vis_first, vis_keep], 0)[None]
    grad_final = jnp.concatenate([grad_near, grad_far, grad_keep], 0)[None]
    late.got, up_grad, out_grad, down_grad, vis_final, grad_final = beside(
        late.got, up_grad, out_grad, down_grad, vis_final, grad_final
    )
    first, second, three, small = late.whole()
    tiles, rows, span = small.shape
    pages = lax.axis_size("page")
    small = untiled(small.reshape(tiles, pages, rows // pages, span).astype(f32).sum(1))
    vis_qkv_grad = jnp.concatenate(
        [each[i] for i in range(3) for each in (first, second)], 1
    )
    qkv_grad = jnp.stack([vis_qkv_grad, untiled(three)]).astype(f32)

    count = vis_sums.shape[0]
    gain_two, bias_two, obias, dbias = [
        own_columns(jnp.stack([small[i], small[count + 8 + i]])) for i in range(4)
    ]
    gain_one, bias_one = [
        own_columns(jnp.stack([small[count + i], small[count + 4 + i]])) for i in range(2)
    ]
    ubias = jnp.stack([small[4:count].reshape(-1), small[count + 12 :].reshape(-1)])
    ubias = own_columns(ubias)

    return (
        vis_final,
        own_rows(query_result)[None],
        grad_final,
        own_input[None],
        gain_one,
        bias_one,
        qkv_grad,
        out_grad,
        obias,
        gain_two,
        bias_two,
        up_grad,
        ubias,
        down_grad,
        dbias,
    )


def solution(mesh):
    return jax.shard_map(
        body,
        mesh=mesh,
        in_specs=(
            P("page", "strip", None, None),
            P("page", "strip", None),
            P("page", None, None),
            P("page", None),
            P("page"),
            P(),
            P(),
            P(),
            P(),
            P(),
            P(),
            P(),
            P(),
            P(),
            P(),
            P(),
            P("page", "strip", None, None),
            P("page", "strip", None),
        ),
        out_specs=(
            P("page", "strip", None, None),
            P("page", "strip", None),
            P("page", "strip", None, None),
            P("page", "strip", None),
            P(None, "strip"),
            P(None, "strip"),
            P(None, "strip", None),
            P(None, "strip", None),
            P(None, "strip"),
            P(None, "strip"),
            P(None, "strip"),
            P(None, "strip", None),
            P(None, "strip"),
            P(None, "strip", None),
            P(None, "strip"),
        ),
        check_vma=False,
    )
```
